32 devices in a mesh: ctx: 8 (over y, x, core), fsdp: 4 (over z).
Axes of the slice: x: 2, y: 2, z: 4, core: 2. Of those that a mesh axis runs over, the one named last changes fastest.
Arguments:
- hidden_in: bfloat16 [4, 2048, 2048], P('fsdp', 'ctx'), may hold values from -6 to 6
- segment_ids: int32 [4, 2048], P('fsdp', 'ctx'), may hold values from 0 to 8, as said below
- positions: int32 [4, 2048], P('fsdp', 'ctx'), may hold values from 0 to 1151, as said below
- attn_gain: float32 [2048], replicated, may hold values from 0.5 to 1.5
- qkv_weight: bfloat16 [2048, 4096], P(('ctx', 'fsdp')), may hold values from -0.125 to 0.125
- query_norm_gain: float32 [128], replicated, may hold values from 1.2 to 1.8
- k_gain: float32 [128], replicated, may hold values from 1.2 to 1.8
- out_weight: bfloat16 [2048, 2048], P(('ctx', 'fsdp')), may hold values from -1 to 1
- mlp_gain: float32 [2048], replicated, may hold values from 0.5 to 1.5
- gate_up: bfloat16 [2048, 12288], P(('ctx', 'fsdp')), may hold values from -0.125 to 0.125
- down_weight: bfloat16 [6144, 2048], P(('ctx', 'fsdp')), may hold values from -0.078125 to 0.078125
- cotangent: bfloat16 [4, 2048, 2048], P('fsdp', 'ctx'), may hold values from -6 to 6
Outputs:
- hidden_out: bfloat16 [4, 2048, 2048], P('fsdp', 'ctx')
- d_hidden_in: float32 [4, 2048, 2048], P('fsdp', 'ctx')
- d_attn_gain: float32 [2048], replicated
- d_qkv_weight: float32 [2048, 4096], P(('ctx', 'fsdp'))
- d_q_gain: float32 [128], replicated
- d_k_gain: float32 [128], replicated
- d_out_weight: float32 [2048, 2048], P(('ctx', 'fsdp'))
- d_mlp_gain: float32 [2048], replicated
- d_gate_up: float32 [2048, 12288], P(('ctx', 'fsdp'))
- d_down_weight: float32 [6144, 2048], P(('ctx', 'fsdp'))
The draws below stay inside these ranges and needn't reach their ends.
Inputs may be any that keep to these rules, and one draw needn't show every extreme that they name: `segment_ids`: in each group, segment 0 is a prompt of 1024 tokens and segments 1 to 8 are continuations of 128 tokens each; a segment's tokens lie in runs of 32 consecutive positions, the runs in an order where a group's first and last run belong to the prompt. `positions`: A prompt token's position is its place in the prompt; a continuation token's is 1024 plus its place in the continuation.
All inputs are finite; a program needn't handle non-finite values.
Results may differ from the reference program's by a relative error of at most 0.019.
Values may be sent and summed in bfloat16 or wider, within the bound.
A program may use at most 640 MiB of HBM per device.

```python
import jax
import jax.numpy as jnp
from jax import lax

D = 2048
QUERY_HEADS = 16
KEY_VALUE_HEADS = 8
HEAD_SIZE = 128
FF = 6144
CONT = 128
RUN = 32
PROMPT = 1024
GROUP = 2048
GROUPS = 4
QKV = 4096


def run_layout(key):
    group_keys = jax.random.split(key, GROUPS)

    def one_group(group_key):
        first_key, second_key = jax.random.split(group_key)
        run_count = GROUP // RUN
        prompt_runs = PROMPT // RUN
        prompt_order = jax.random.permutation(first_key, prompt_runs).astype(jnp.int32)
        middle = jnp.concatenate([prompt_order[2:], jnp.arange(prompt_runs, run_count, dtype=jnp.int32)])
        middle = jax.random.permutation(second_key, middle).astype(jnp.int32)
        run_order = jnp.concatenate([prompt_order[:1], middle, prompt_order[1:2]])
        labels = (run_order[:, None] * RUN + jnp.arange(RUN, dtype=jnp.int32)[None, :]).reshape(GROUP)
        in_prompt = labels < PROMPT
        segments = jnp.where(in_prompt, 0, (labels - PROMPT) // CONT + 1)
        places = jnp.where(in_prompt, labels, PROMPT + (labels - PROMPT) % CONT)
        return (segments.astype(jnp.int32), places.astype(jnp.int32))
    return jax.vmap(one_group)(group_keys)


def draw_segment_ids(key, part):
    return run_layout(key)[0]


def draw_positions(key, part):
    return run_layout(key)[1]


def levels(stream_key, shape, shards, low, high):
    level, own = 1.0, jax.random.fold_in(stream_key, 6)
    for position, parts in shards:
        heights = jnp.exp(jax.random.uniform(jax.random.fold_in(own, position), (parts,), jnp.float32, low / len(shards), high / len(shards)))
        level = level * jnp.repeat(heights, shape[position] // parts).reshape([-1 if axis == position else 1 for axis in range(len(shape))])
    return level


def noise(key, dims, deviation, bound, shards=(), kind=jnp.bfloat16):
    level = levels(key, dims, shards, -0.22, 0.18) if shards else 1.0
    entries = jax.random.normal(key, dims, jnp.float32) * deviation * level
    return jnp.minimum(jnp.maximum(entries, -bound), bound).astype(kind)


def setup_inputs(seed: int = 0) -> dict:
    splits = jax.random.split(jax.random.key(seed), 13)
    hidden_in = noise(splits[0], (GROUPS, GROUP, D), 1.0, 6.0, ((0, 4), (1, 8)))
    segment_ids = draw_segment_ids(jax.random.fold_in(splits[12], 71), 0)
    positions = draw_positions(jax.random.fold_in(splits[12], 71), 0)
    attn_gain = jnp.clip(1.0 + 0.1 * jax.random.normal(splits[3], (D,), jnp.float32), 0.5, 1.5)
    qkv_weight = noise(splits[4], (D, QKV), D ** -0.5, 0.125, ((0, 32),))
    query_norm_gain = jnp.clip(jax.random.uniform(splits[5], (HEAD_SIZE,), jnp.float32, 1.2, 1.8), 1.2, 1.8)
    k_gain = jnp.clip(jax.random.uniform(splits[6], (HEAD_SIZE,), jnp.float32, 1.2, 1.8), 1.2, 1.8)
    out_weight = noise(splits[7], (QUERY_HEADS * HEAD_SIZE, D), (QUERY_HEADS * HEAD_SIZE // 64) ** -0.5, 1.0, ((0, 32),))
    mlp_gain = jnp.clip(1.0 + 0.1 * jax.random.normal(splits[8], (D,), jnp.float32), 0.5, 1.5)
    gate_up = noise(splits[9], (D, 2 * FF), D ** -0.5, 0.125, ((0, 32),))
    down_weight = noise(splits[10], (FF, D), FF ** -0.5, 0.078125, ((0, 32),))
    cotangent = noise(splits[11], (GROUPS, GROUP, D), 1.0, 6.0, ((0, 4), (1, 8)))
    return {"hidden_in": hidden_in, "segment_ids": segment_ids, "positions": positions, "attn_gain": attn_gain, "qkv_weight": qkv_weight, "query_norm_gain": query_norm_gain, "k_gain": k_gain, "out_weight": out_weight, "mlp_gain": mlp_gain, "gate_up": gate_up, "down_weight": down_weight, "cotangent": cotangent}


EPS = 1e-06
ROPE_BASE = 1000000.0
MASK_FILL = -1e+30
HIGHEST = lax.Precision.HIGHEST

@jax.custom_vjp
def low(v):
    return lax.optimization_barrier(v.astype(jnp.bfloat16)).astype(jnp.float32)

@jax.custom_vjp
def low_back(v):
    return v

def low_keep(v):
    return (low(v), None)

def low_pass(kept, grad):
    return (grad,)

def back_keep(v):
    return (v, None)

def back_low(kept, grad):
    return (low(grad),)
low.defvjp(low_keep, low_pass)
low_back.defvjp(back_keep, back_low)

def norm_rows(values, gain):
    return values * lax.rsqrt(lax.optimization_barrier(jnp.mean(values * values, axis=-1, keepdims=True)) + EPS) * gain

def rotate_half(values, cosine, sine_table):
    middle = values.shape[-1] // 2
    first_half = values[..., :middle]
    second_half = values[..., middle:]
    return jnp.concatenate([first_half * cosine - second_half * sine_table, second_half * cosine + first_half * sine_table], axis=-1)

def rotary_tables(places):
    exponent = jnp.arange(HEAD_SIZE // 2, dtype=jnp.float32) * (2.0 / HEAD_SIZE)
    inverse = jnp.power(ROPE_BASE, -exponent)
    angles = places.astype(jnp.float32)[:, None] * inverse[None, :]
    return (jnp.cos(angles)[:, None, :], jnp.sin(angles)[:, None, :])

def attention(query_tensor, heads_of_keys, heads_of_values, segments, places):
    count_of_tokens = query_tensor.shape[0]
    rows_per_block = min(512, count_of_tokens)
    block_count = count_of_tokens // rows_per_block
    grouped_heads = query_tensor.reshape(block_count, rows_per_block, KEY_VALUE_HEADS, QUERY_HEADS // KEY_VALUE_HEADS, HEAD_SIZE)

    def one_block(block_items):
        query_rows, query_segs, query_places = block_items
        scores = jnp.einsum('qgrd,kgd->grqk', query_rows, heads_of_keys, precision=HIGHEST) * HEAD_SIZE ** (-0.5)
        scores = low_back(scores)
        visible = ((segments[None, :] == query_segs[:, None]) | (segments[None, :] == 0)) & (places[None, :] <= query_places[:, None])
        scores = jnp.where(visible, scores, MASK_FILL)
        row_top = lax.optimization_barrier(jnp.max(scores, axis=-1, keepdims=True))
        log_total = row_top + jnp.log(lax.optimization_barrier(jnp.sum(jnp.exp(scores - row_top), axis=-1, keepdims=True)))
        weights = low(jnp.exp(scores - log_total))
        return jnp.einsum('grqk,kgd->qgrd', weights, heads_of_values, precision=HIGHEST)
    result = lax.map(jax.checkpoint(one_block), (grouped_heads, segments.reshape(block_count, rows_per_block), places.reshape(block_count, rows_per_block)))
    return result.reshape(count_of_tokens, QUERY_HEADS * HEAD_SIZE)

def residual_block(hidden, attn_gain, w_qkv, query_norm_gain, k_gain, w_out, mlp_gain, w_gu, w_down, segments, places):
    count_of_tokens = hidden.shape[0]
    query_total_width = QUERY_HEADS * HEAD_SIZE
    key_total_width = KEY_VALUE_HEADS * HEAD_SIZE
    normed = low(norm_rows(hidden, attn_gain))
    merged_rows = low_back(jnp.dot(normed, w_qkv, precision=HIGHEST))
    cosine, sine_table = rotary_tables(places)
    query_tensor = merged_rows[:, :query_total_width].reshape(count_of_tokens, QUERY_HEADS, HEAD_SIZE)
    heads_of_keys = merged_rows[:, query_total_width:query_total_width + key_total_width].reshape(count_of_tokens, KEY_VALUE_HEADS, HEAD_SIZE)
    heads_of_values = merged_rows[:, query_total_width + key_total_width:].reshape(count_of_tokens, KEY_VALUE_HEADS, HEAD_SIZE)
    query_tensor = low(low_back(rotate_half(norm_rows(query_tensor, query_norm_gain), cosine, sine_table)))
    heads_of_keys = low(low_back(rotate_half(norm_rows(heads_of_keys, k_gain), cosine, sine_table)))
    heads_of_values = low(low_back(heads_of_values))
    mixed_low = low(low_back(attention(query_tensor, heads_of_keys, heads_of_values, segments, places)))
    middle = hidden + low_back(jnp.dot(mixed_low, w_out, precision=HIGHEST))
    second = low(norm_rows(middle, mlp_gain))
    gate_rows = low_back(jnp.dot(second, w_gu, precision=HIGHEST))
    gate_part = gate_rows[:, :FF]
    uppers = gate_rows[:, FF:]
    activated = low(low_back(gate_part * jax.nn.sigmoid(gate_part) * uppers))
    return middle + low_back(jnp.dot(activated, w_down, precision=HIGHEST))

def reference(hidden_in, segment_ids, positions, attn_gain, qkv_weight, query_norm_gain, k_gain, out_weight, mlp_gain, gate_up, down_weight, cotangent):
    params = (attn_gain.astype(jnp.float32), qkv_weight.astype(jnp.float32), query_norm_gain.astype(jnp.float32), k_gain.astype(jnp.float32), out_weight.astype(jnp.float32), mlp_gain.astype(jnp.float32), gate_up.astype(jnp.float32), down_weight.astype(jnp.float32))

    def one_group(totals, group_items):
        hidden, segments, places, upstream = group_items

        def forward(hidden_f, *weights):
            return residual_block(hidden_f, *weights, segments, places)
        output, pullback = jax.vjp(forward, hidden.astype(jnp.float32), *params)
        group_grads = pullback(upstream.astype(jnp.float32))
        totals = tuple((total + grad for total, grad in zip(totals, group_grads[1:])))
        return (totals, (output.astype(jnp.bfloat16), group_grads[0]))
    zero_grads = tuple((jnp.zeros_like(param) for param in params))
    totals, (outputs, input_grads) = lax.scan(one_group, zero_grads, (hidden_in, segment_ids, positions, cotangent))
    return (outputs, input_grads, totals[0], totals[1], totals[2], totals[3], totals[4], totals[5], totals[6], totals[7])
```

```python
import functools
import math

import jax
import jax.numpy as jnp
from jax import lax
from jax.experimental import pallas as pl
from jax.experimental.pallas import tpu as pltpu
from jax.sharding import PartitionSpec as P

QUERY_HEADS = 16
KEY_VALUE_HEADS = 8
HEAD = 128
FF = 6144
PROMPT = 1024
CONT = 128
RUN = 32
EPS = 1e-06
ROPE_BASE = 1000000.0
SCALE = HEAD ** (-0.5)
SCALE2 = SCALE * math.log2(math.e)
MESH = pl.DeviceIdType.MESH
ANY = pl.BlockSpec(memory_space=pl.ANY)
VMEM = pl.BlockSpec(memory_space=pltpu.VMEM)
SMEM = pl.BlockSpec(memory_space=pltpu.SMEM)
BF16 = jnp.bfloat16
F32 = jnp.float32
DMA = pltpu.SemaphoreType.DMA
VMEM_LIMIT = 60 * 2**20


def cost(us, flops=0):
    return pl.CostEstimate(flops=flops, bytes_accessed=int(us * 3.2e6), transcendentals=0)


def flip(me, mask):
    result = me
    bit = 1
    while bit <= mask:
        if mask & bit:
            result = result + bit - 2 * bit * lax.rem(lax.div(me, bit), 2)
        bit *= 2
    return result


def bits_of(count):
    bits = []
    bit = 1
    while bit < count:
        bits.append(bit)
        bit *= 2
    return bits


def greet(peers):
    barrier = pltpu.get_barrier_semaphore()
    for peer in peers:
        pl.semaphore_signal(barrier, inc=1, device_id=peer, device_id_type=MESH)
    pl.semaphore_wait(barrier, len(peers))


def gather_orders(count):
    chip_bits = bits_of(count)[1:]
    return [chip_bits + [1], chip_bits[::-1] + [1]]


def last_bit(order, slot):
    return [bit for bit in order if slot & bit][-1]


def gather_rows(count, me, group, source, target, send, recv):
    rows = source.shape[0]
    half = rows // 2
    orders = gather_orders(count)

    def copy(part, slot, bit):
        start = pl.multiple_of(flip(me, slot) * rows + part * half, half)
        place = target.at[pl.ds(start, half)]
        origin = source.at[pl.ds(part * half, half)] if slot == 0 else place
        number = part * count + (slot ^ bit)
        return pltpu.make_async_remote_copy(
            origin,
            place,
            send.at[number],
            recv.at[number],
            device_id=(flip(me, bit), group),
            device_id_type=MESH,
        )

    own = pltpu.make_async_copy(
        source, target.at[pl.ds(pl.multiple_of(me * rows, rows), rows)], send.at[0]
    )
    own.start()
    copies = []
    for step in range(len(orders[0])):
        for part in (0, 1):
            item = copy(part, 0, orders[part][step])
            item.start()
            copies.append(item)

    def arrived(part, slot):
        start = pl.multiple_of(flip(me, slot) * rows + part * half, half)
        place = target.at[pl.ds(start, half)]
        number = part * count + slot
        pltpu.make_async_remote_copy(
            place,
            place,
            send.at[number],
            recv.at[number],
            device_id=(flip(me, last_bit(orders[part], slot)), group),
            device_id_type=MESH,
        ).wait_recv()

    def finish():
        waits = []
        for part in (0, 1):
            order = orders[part]
            for slot in range(1, count):
                last = order.index(last_bit(order, slot))
                waits.append((last, bin(slot).count("1"), part, slot))
        for last, _, part, slot in sorted(waits):
            arrived(part, slot)
            for bit in orders[part][last + 1 :]:
                item = copy(part, slot, bit)
                item.start()
                copies.append(item)
        own.wait()
        for item in copies:
            item.wait_send()

    return finish


def gather_kernel(count, source, target, send, recv):
    me = lax.axis_index("ctx")
    group = lax.axis_index("fsdp")
    greet([(flip(me, bit), group) for bit in bits_of(count)])
    gather_rows(count, me, group, source, target, send, recv)()


def gather_ctx(count, collective, values):
    rows, width = values.shape
    return pl.pallas_call(
        functools.partial(gather_kernel, count),
        out_shape=jax.ShapeDtypeStruct((count * rows, width), values.dtype),
        in_specs=[ANY],
        out_specs=ANY,
        scratch_shapes=[DMA((2 * count,)), DMA((2 * count,))],
        compiler_params=pltpu.CompilerParams(collective_id=collective, has_side_effects=True),
        cost_estimate=cost(42),
    )(values)


def trade(count, me, group, pieces, source, target, send, recv):
    copies = []
    local = []
    for slot in list(range(1, count)) + [0]:
        peer = flip(me, slot)
        for number, (origin, place) in enumerate(pieces(peer, me)):
            total = len(pieces(peer, me))
            index = slot * total + number
            if slot == 0:
                item = pltpu.make_async_copy(source.at[origin], target.at[place], send.at[index])
                local.append(item)
            else:
                item = pltpu.make_async_remote_copy(
                    source.at[origin],
                    target.at[place],
                    send.at[index],
                    recv.at[index],
                    device_id=(peer, group),
                    device_id_type=MESH,
                )
                copies.append(item)
            item.start()

    def finish():
        for item in local:
            item.wait()
        for slot in range(1, count):
            peer = flip(me, slot)
            listed = pieces(me, peer)
            for number, (origin, place) in enumerate(listed):
                index = slot * len(listed) + number
                pltpu.make_async_remote_copy(
                    source.at[origin],
                    target.at[place],
                    send.at[index],
                    recv.at[index],
                    device_id=(peer, group),
                    device_id_type=MESH,
                ).wait_recv()
        for item in copies:
            item.wait_send()

    return finish


def span(start, width):
    return pl.ds(pl.multiple_of(start, HEAD), width)


def sharing(count):
    if count not in (KEY_VALUE_HEADS, QUERY_HEADS):
        raise ValueError(count)
    return count // KEY_VALUE_HEADS


def qkv_spans(count, device, gradients=False):
    own = QUERY_HEADS // count * HEAD
    repeat = sharing(count)
    queries = QUERY_HEADS * HEAD
    shared = lax.div(device, repeat) * HEAD
    if repeat == 2 and gradients:
        which = lax.rem(device, 2)
        return [
            (device * own, 0, own),
            (queries + which * (KEY_VALUE_HEADS * HEAD) + shared, own + which * HEAD, HEAD),
        ]
    return [
        (device * own, 0, own),
        (queries + shared, own, HEAD),
        (queries + KEY_VALUE_HEADS * HEAD + shared, own + HEAD, HEAD),
    ]


def mlp_spans(count, device, gradients=False):
    own = FF // count
    return [(device * own, 0, own), (FF + device * own, own, own)]


def outgoing(spans, count):
    def pieces(device, owner):
        return [
            ((slice(None), span(whole, width)), (owner, slice(None), pl.ds(part, width)))
            for whole, part, width in spans(count, device)
        ]

    return pieces


def incoming(spans, count):
    def pieces(device, owner):
        return [
            ((device, slice(None), span(part, width)), (slice(None), span(whole, width)))
            for whole, part, width in spans(count, owner, True)
        ]

    return pieces


def everyone(count, me, group):
    return [(flip(me, slot), group) for slot in range(1, count)]


def spread_kernel(count, source, target, send, recv):
    me = lax.axis_index("ctx")
    group = lax.axis_index("fsdp")
    greet(everyone(count, me, group))
    trade(count, me, group, outgoing(qkv_spans, count), source, target, send, recv)()


def spread_qkv(count, collective, weight):
    rows = weight.shape[0]
    width = QUERY_HEADS // count * HEAD + 2 * HEAD
    return pl.pallas_call(
        functools.partial(spread_kernel, count),
        out_shape=jax.ShapeDtypeStruct((count, rows, width), weight.dtype),
        in_specs=[ANY],
        out_specs=ANY,
        scratch_shapes=[DMA((3 * count,)), DMA((3 * count,))],
        compiler_params=pltpu.CompilerParams(collective_id=collective, has_side_effects=True),
        cost_estimate=cost(12),
    )(weight)


def opening_kernel(
    count, normed, runs, weight, rows, all_runs, parts, send, recv, run_send, run_recv, part_send, part_recv
):
    me = lax.axis_index("ctx")
    group = lax.axis_index("fsdp")
    greet(everyone(count, me, group))
    finish_runs = trade(
        count, me, group, lambda device, owner: [((0,), (owner,))], runs, all_runs, run_send, run_recv
    )
    finish_rows = gather_rows(count, me, group, normed, rows, send, recv)
    finish_parts = trade(
        count, me, group, outgoing(mlp_spans, count), weight, parts, part_send, part_recv
    )
    finish_rows()
    finish_parts()
    finish_runs()


def opening(count, collective, normed, runs, weight):
    tokens, width = normed.shape
    return pl.pallas_call(
        functools.partial(opening_kernel, count),
        out_shape=[
            jax.ShapeDtypeStruct((count * tokens, width), BF16),
            jax.ShapeDtypeStruct((count, 8, 128), jnp.int32),
            jax.ShapeDtypeStruct((count, weight.shape[0], 2 * FF // count), BF16),
        ],
        in_specs=[ANY, ANY, ANY],
        out_specs=[ANY, ANY, ANY],
        scratch_shapes=[
            DMA((2 * count,)),
            DMA((2 * count,)),
            DMA((count,)),
            DMA((count,)),
            DMA((2 * count,)),
            DMA((2 * count,)),
        ],
        compiler_params=pltpu.CompilerParams(collective_id=collective, has_side_effects=True),
        cost_estimate=cost(60),
    )(normed, runs, weight)


def return_kernel(count, spans, source, target, send, recv):
    me = lax.axis_index("ctx")
    group = lax.axis_index("fsdp")
    greet(everyone(count, me, group))
    trade(count, me, group, incoming(spans, count), source, target, send, recv)()


def return_columns(count, collective, spans, width, parts):
    rows = parts.shape[1]
    pieces = len(spans(count, 0, True))
    return pl.pallas_call(
        functools.partial(return_kernel, count, spans),
        out_shape=jax.ShapeDtypeStruct((rows, width), parts.dtype),
        in_specs=[ANY],
        out_specs=ANY,
        scratch_shapes=[DMA((pieces * count,)), DMA((pieces * count,))],
        compiler_params=pltpu.CompilerParams(collective_id=collective, has_side_effects=True),
        cost_estimate=cost(12),
    )(parts)


def total_kernel(count, groups, values, result, near, far, send, recv, far_send, far_recv):
    me = lax.axis_index("ctx")
    group = lax.axis_index("fsdp")
    others = [lax.rem(group + step, groups) for step in range(1, groups)]
    greet(everyone(count, me, group) + [(me, other) for other in others])
    copies = []
    for slot in range(1, count):
        item = pltpu.make_async_remote_copy(
            values,
            near.at[me],
            send.at[slot],
            recv.at[slot],
            device_id=(flip(me, slot), group),
            device_id_type=MESH,
        )
        item.start()
        copies.append(item)
    near[me] = values[...]
    for item in copies:
        item.wait()
    summed = near[0]
    for index in range(1, count):
        summed = summed + near[index]
    far[group] = summed
    copies = []
    for step, other in enumerate(others):
        item = pltpu.make_async_remote_copy(
            far.at[group],
            far.at[group],
            far_send.at[step],
            far_recv.at[step],
            device_id=(me, other),
            device_id_type=MESH,
        )
        item.start()
        copies.append(item)
    for item in copies:
        item.wait()
    summed = far[0]
    for index in range(1, groups):
        summed = summed + far[index]
    result[...] = summed


def total(count, groups, collective, values):
    shape = values.shape
    return pl.pallas_call(
        functools.partial(total_kernel, count, groups),
        out_shape=jax.ShapeDtypeStruct(shape, F32),
        in_specs=[VMEM],
        out_specs=VMEM,
        scratch_shapes=[
            pltpu.VMEM((count,) + shape, F32),
            pltpu.VMEM((groups,) + shape, F32),
            DMA((count,)),
            DMA((count,)),
            DMA((groups,)),
            DMA((groups,)),
        ],
        compiler_params=pltpu.CompilerParams(collective_id=collective, has_side_effects=True),
        cost_estimate=cost(12),
    )(values)


def product_scatter_kernel(
    count, flipped, left, right, result, kept, near_out, near_in, far_out, far_in, ns, nr, fs, fr
):
    me = lax.axis_index("ctx")
    group = lax.axis_index("fsdp")
    rows, width = result.shape
    half = rows // 2
    bits = bits_of(count)
    orders = [bits[1:][::-1], bits[1:]]
    greet([(flip(me, bit), group) for bit in bits])
    tile = min(512, width)

    def product(slot, store):
        start = pl.multiple_of(flip(me, slot) * rows, rows)
        block = left[pl.ds(start, rows), :]

        def step(index, carry):
            columns = pl.ds(pl.multiple_of(index * tile, tile), tile)
            if flipped:
                value = lax.dot_general(
                    block, right[columns, :], (((1,), (1,)), ((), ())), preferred_element_type=F32
                )
            else:
                value = jnp.dot(block, right[:, columns], preferred_element_type=F32)
            store(columns, value)
            return carry

        lax.fori_loop(0, width // tile, step, 0)

    def first(part, slot):
        return [bit for bit in orders[part] if slot & bit][0]

    def near(pair):
        return pltpu.make_async_remote_copy(
            near_out.at[pair],
            near_in.at[pair],
            ns.at[pair],
            nr.at[pair],
            device_id=(flip(me, 1), group),
            device_id_type=MESH,
        )

    def far(part, pair):
        number = part * (count // 2) + pair
        return pltpu.make_async_remote_copy(
            far_out.at[number],
            far_in.at[number],
            fs.at[number],
            fr.at[number],
            device_id=(flip(me, first(part, 2 * pair)), group),
            device_id_type=MESH,
        )

    def needs(part, pair):
        found = []
        for bit in orders[part]:
            if 2 * pair & bit:
                break
            found.append((2 * pair ^ bit) // 2)
        return found

    def settle(part, pair):
        span_rows = pl.ds(part * half, half)
        value = kept[pair, span_rows, :]
        for other in needs(part, pair):
            far(part, other).wait_recv()
            value = value + far_in[part * (count // 2) + other].astype(F32)
        if pair == 0:
            result[span_rows, :] = value
        else:
            far_out[part * (count // 2) + pair] = value.astype(BF16)
            far(part, pair).start()

    pairs = list(range(count // 2))[::-1]
    for pair in pairs:

        def store_near(columns, value):
            near_out[pair, :, columns] = value.astype(BF16)

        def store_kept(columns, value):
            kept[pair, :, columns] = value

        product(2 * pair + 1, store_near)
        near(pair).start()
        product(2 * pair, store_kept)
        near(pair).wait_recv()
        kept[pair] = kept[pair] + near_in[pair].astype(F32)
        for part in (0, 1):
            if pair and not needs(part, pair):
                settle(part, pair)
    for pair in pairs:
        for part in (0, 1):
            if not pair or needs(part, pair):
                settle(part, pair)
    for pair in pairs:
        near(pair).wait_send()
        for part in (0, 1):
            if pair:
                far(part, pair).wait_send()


def product_scatter(count, collective, left, right, flipped):
    tokens, depth = left.shape
    width = right.shape[0] if flipped else right.shape[1]
    rows = tokens // count
    pairs = count // 2
    return pl.pallas_call(
        functools.partial(product_scatter_kernel, count, flipped),
        out_shape=jax.ShapeDtypeStruct((rows, width), F32),
        in_specs=[VMEM, VMEM],
        out_specs=VMEM,
        scratch_shapes=[
            pltpu.VMEM((pairs, rows, width), F32),
            pltpu.VMEM((pairs, rows, width), BF16),
            pltpu.VMEM((pairs, rows, width), BF16),
            pltpu.VMEM((2 * pairs, rows // 2, width), BF16),
            pltpu.VMEM((2 * pairs, rows // 2, width), BF16),
            DMA((pairs,)),
            DMA((pairs,)),
            DMA((2 * pairs,)),
            DMA((2 * pairs,)),
        ],
        compiler_params=pltpu.CompilerParams(
            collective_id=collective, has_side_effects=True, vmem_limit_bytes=VMEM_LIMIT
        ),
        cost_estimate=cost(45, 2 * tokens * depth * width),
    )(left, right)


def swap_halves(value):
    return jnp.concatenate([value[:, HEAD // 2 :], value[:, : HEAD // 2]], axis=1)


def nt(left, right):
    return lax.dot_general(left, right, (((1,), (1,)), ((), ())), preferred_element_type=F32)


def causal(keys, queries):
    key = lax.broadcasted_iota(jnp.int32, (keys, queries), 0)
    query = lax.rem(lax.broadcasted_iota(jnp.int32, (keys, queries), 1), CONT)
    return key <= query


def attention_kernel(
    heads, runs, joined, cosine, sine, q_gain, k_gain, attended, raw, queries, keys, values, mixed, lse, turned, placed
):
    tokens = joined.shape[0]
    blocks = tokens // CONT
    wide = heads * CONT

    def sort(run, carry):
        origin = pl.multiple_of(run * RUN, RUN)
        place = pl.multiple_of(runs[run] * RUN, RUN)
        raw[pl.ds(place, RUN), :] = joined[pl.ds(origin, RUN), :]
        return carry

    lax.fori_loop(0, tokens // RUN, sort, 0)

    def prepare(block, carry):
        span_rows = pl.ds(pl.multiple_of(block * CONT, CONT), CONT)
        cos_rows = cosine[span_rows, :]
        sin_rows = sine[span_rows, :]

        def turn(value, gain):
            value = value * lax.rsqrt(jnp.mean(value * value, axis=-1, keepdims=True) + EPS) * gain
            return (value * cos_rows + swap_halves(value) * sin_rows).astype(BF16)

        for head in range(heads):
            piece = raw[span_rows, head * HEAD : (head + 1) * HEAD]
            queries[block, head * CONT : (head + 1) * CONT, :] = turn(piece, q_gain[...])
        keys[span_rows, :] = turn(raw[span_rows, wide : wide + HEAD], k_gain[...])
        piece = raw[span_rows, wide + HEAD : wide + 2 * HEAD]
        values[span_rows, :] = piece.astype(BF16)
        turned[:, span_rows] = piece.T.astype(BF16)
        return carry

    lax.fori_loop(0, blocks, prepare, 0)

    def attend(block, own, before):
        query = queries[block]
        own_rows = pl.ds(own, CONT)
        weight = jnp.exp2(nt(keys[own_rows, :], query) * SCALE2)
        weight = jnp.where(causal(CONT, wide), weight, 0.0)
        sums = jnp.sum(weight, axis=0, keepdims=True)
        out = jnp.dot(turned[:, own_rows], weight.astype(BF16), preferred_element_type=F32)
        if before:
            weight = jnp.exp2(nt(keys[:before, :], query) * SCALE2)
            sums = sums + jnp.sum(weight, axis=0, keepdims=True)
            out = out + jnp.dot(turned[:, :before], weight.astype(BF16), preferred_element_type=F32)
        out = out / sums
        mixed[block] = out
        lse[block] = jnp.broadcast_to(jnp.log2(sums), (8, wide))
        for head in range(heads):
            placed[own_rows, head * HEAD : (head + 1) * HEAD] = out[
                :, head * CONT : (head + 1) * CONT
            ].T.astype(BF16)

    for block in range(PROMPT // CONT):
        attend(block, block * CONT, block * CONT)

    def continuation(block, carry):
        attend(block, pl.multiple_of(block * CONT, CONT), PROMPT)
        return carry

    lax.fori_loop(PROMPT // CONT, blocks, continuation, 0)

    def unsort(run, carry):
        origin = pl.multiple_of(run * RUN, RUN)
        place = pl.multiple_of(runs[run] * RUN, RUN)
        attended[pl.ds(origin, RUN), :] = placed[pl.ds(place, RUN), :]
        return carry

    lax.fori_loop(0, tokens // RUN, unsort, 0)


def attention(heads, runs, joined, cosine, sine, q_gain, k_gain):
    tokens = joined.shape[0]
    blocks = tokens // CONT
    wide = heads * CONT
    shape = jax.ShapeDtypeStruct
    return pl.pallas_call(
        functools.partial(attention_kernel, heads),
        out_shape=[
            shape((tokens, wide), BF16),
            shape(joined.shape, F32),
            shape((blocks, wide, HEAD), BF16),
            shape((tokens, HEAD), BF16),
            shape((tokens, HEAD), BF16),
            shape((blocks, HEAD, wide), F32),
            shape((blocks, 8, wide), F32),
        ],
        in_specs=[SMEM, VMEM, VMEM, VMEM, VMEM, VMEM],
        out_specs=[VMEM] * 7,
        scratch_shapes=[pltpu.VMEM((HEAD, tokens), BF16), pltpu.VMEM((tokens, wide), BF16)],
        compiler_params=pltpu.CompilerParams(vmem_limit_bytes=VMEM_LIMIT),
        cost_estimate=cost(15),
    )(runs, joined, cosine, sine, q_gain, k_gain)


def attention_back_kernel(
    heads, runs, d_attended, queries, keys, values, mixed, lse, d_queries, d_keys, d_values, arrived, keys_turned
):
    tokens = keys.shape[0]
    blocks = tokens // CONT
    wide = heads * CONT

    def sort(run, carry):
        origin = pl.multiple_of(run * RUN, RUN)
        place = pl.multiple_of(runs[run] * RUN, RUN)
        arrived[pl.ds(place, RUN), :] = d_attended[pl.ds(origin, RUN), :]
        return carry

    lax.fori_loop(0, tokens // RUN, sort, 0)
    d_keys[...] = jnp.zeros_like(d_keys)
    d_values[...] = jnp.zeros_like(d_values)

    def turn(block, carry):
        span_rows = pl.ds(pl.multiple_of(block * CONT, CONT), CONT)
        keys_turned[:, span_rows] = keys[span_rows, :].astype(F32).T.astype(BF16)
        return carry

    lax.fori_loop(0, blocks, turn, 0)

    def back(block, own, before):
        query = queries[block]
        own_rows = pl.ds(own, CONT)
        grad = jnp.concatenate(
            [arrived[own_rows, head * HEAD : (head + 1) * HEAD] for head in range(heads)], axis=0
        )
        grad_turned = grad.astype(F32).T
        delta = jnp.sum(grad_turned * mixed[block], axis=0, keepdims=True)
        total_row = lse[block][:1, :]

        def part(rows, count, masked):
            prob = jnp.exp2(nt(keys[rows, :], query) * SCALE2 - total_row)
            if masked:
                prob = jnp.where(causal(count, wide), prob, 0.0)
            score = (prob * (nt(values[rows, :], grad) - delta)).astype(BF16)
            d_values[rows, :] += jnp.dot(prob.astype(BF16), grad, preferred_element_type=F32)
            d_keys[rows, :] += jnp.dot(score, query, preferred_element_type=F32)
            return jnp.dot(keys_turned[:, rows], score, preferred_element_type=F32)

        result = part(own_rows, CONT, True)
        if before:
            result = result + part(slice(0, before), before, False)
        result = result * SCALE
        for head in range(heads):
            d_queries[own_rows, head * HEAD : (head + 1) * HEAD] = result[
                :, head * CONT : (head + 1) * CONT
            ].T.astype(BF16)

    for block in range(PROMPT // CONT):
        back(block, block * CONT, block * CONT)

    def continuation(block, carry):
        back(block, pl.multiple_of(block * CONT, CONT), PROMPT)
        return carry

    lax.fori_loop(PROMPT // CONT, blocks, continuation, 0)


def attention_back(heads, runs, d_attended, queries, keys, values, mixed, lse):
    tokens = keys.shape[0]
    wide = heads * CONT
    shape = jax.ShapeDtypeStruct
    return pl.pallas_call(
        functools.partial(attention_back_kernel, heads),
        out_shape=[shape((tokens, wide), BF16), shape((tokens, HEAD), F32), shape((tokens, HEAD), F32)],
        in_specs=[SMEM] + [VMEM] * 6,
        out_specs=[VMEM] * 3,
        scratch_shapes=[pltpu.VMEM((tokens, wide), BF16), pltpu.VMEM((HEAD, tokens), BF16)],
        compiler_params=pltpu.CompilerParams(vmem_limit_bytes=VMEM_LIMIT),
        cost_estimate=cost(25),
    )(runs, d_attended, queries, keys, values, mixed, lse)


def joined_back_kernel(
    heads, runs, raw, d_queries, d_keys, d_values, cosine, sine, q_gain, k_gain, share, d_joined, d_q_gain, d_k_gain, placed
):
    tokens = raw.shape[0]
    blocks = tokens // CONT
    wide = heads * CONT
    d_q_gain[...] = jnp.zeros_like(d_q_gain)
    d_k_gain[...] = jnp.zeros_like(d_k_gain)

    def step(block, carry):
        span_rows = pl.ds(pl.multiple_of(block * CONT, CONT), CONT)
        cos_rows = cosine[span_rows, :]
        sin_rows = sine[span_rows, :]

        def pull(value, grad, gain):
            grad = grad * cos_rows - swap_halves(grad) * sin_rows
            scale = lax.rsqrt(jnp.mean(value * value, axis=-1, keepdims=True) + EPS)
            scaled = value * scale
            gain_grad = jnp.sum(grad * scaled, axis=0, keepdims=True)
            grad = grad * gain
            return scale * (grad - scaled * jnp.mean(grad * scaled, axis=-1, keepdims=True)), gain_grad

        for head in range(heads):
            columns = slice(head * HEAD, (head + 1) * HEAD)
            grad, gain_grad = pull(
                raw[span_rows, columns], d_queries[span_rows, columns].astype(F32), q_gain[...]
            )
            placed[span_rows, columns] = grad.astype(BF16)
            d_q_gain[...] += gain_grad
        key_part, value_part = share[:1, :], share[1:, :]
        grad, gain_grad = pull(
            raw[span_rows, wide : wide + HEAD],
            (d_keys[span_rows, :] * SCALE).astype(BF16).astype(F32),
            k_gain[...],
        )
        placed[span_rows, wide : wide + HEAD] = (grad * key_part).astype(BF16)
        d_k_gain[...] += gain_grad * key_part
        placed[span_rows, wide + HEAD : wide + 2 * HEAD] = (d_values[span_rows, :] * value_part).astype(BF16)
        return carry

    lax.fori_loop(0, blocks, step, 0)

    def unsort(run, carry):
        origin = pl.multiple_of(run * RUN, RUN)
        place = pl.multiple_of(runs[run] * RUN, RUN)
        d_joined[pl.ds(origin, RUN), :] = placed[pl.ds(place, RUN), :]
        return carry

    lax.fori_loop(0, tokens // RUN, unsort, 0)


def joined_back(heads, runs, raw, d_queries, d_keys, d_values, cosine, sine, q_gain, k_gain, share):
    shape = jax.ShapeDtypeStruct
    return pl.pallas_call(
        functools.partial(joined_back_kernel, heads),
        out_shape=[shape(raw.shape, BF16), shape((1, HEAD), F32), shape((1, HEAD), F32)],
        in_specs=[SMEM] + [VMEM] * 9,
        out_specs=[VMEM] * 3,
        scratch_shapes=[pltpu.VMEM(raw.shape, BF16)],
        compiler_params=pltpu.CompilerParams(vmem_limit_bytes=VMEM_LIMIT),
        cost_estimate=cost(8),
    )(runs, raw, d_queries, d_keys, d_values, cosine, sine, q_gain, k_gain, share)


def norm_back(values, gain, grad):
    scale = lax.rsqrt(jnp.mean(values * values, axis=-1, keepdims=True) + EPS)
    scaled = values * scale
    pushed = grad * gain
    back = scale * (pushed - scaled * jnp.mean(pushed * scaled, axis=-1, keepdims=True))
    return back, jnp.sum(grad * scaled, axis=0)


def norm_rows(values, gain):
    return values * lax.rsqrt(jnp.mean(values * values, axis=-1, keepdims=True) + EPS) * gain


def rotary(tokens):
    index = jnp.arange(tokens, dtype=jnp.int32)
    place = jnp.where(index < PROMPT, index, PROMPT + (index - PROMPT) % CONT).astype(F32)
    exponent = jnp.arange(HEAD // 2, dtype=F32) * (2.0 / HEAD)
    angles = place[:, None] * jnp.power(ROPE_BASE, -exponent)[None, :]
    cosine, sine = jnp.cos(angles), jnp.sin(angles)
    return jnp.concatenate([cosine, cosine], axis=1), jnp.concatenate([-sine, sine], axis=1)


def body(
    count,
    groups,
    hidden_in,
    segment_ids,
    positions,
    attn_gain,
    qkv_weight,
    query_norm_gain,
    k_gain,
    out_weight,
    mlp_gain,
    gate_up,
    down_weight,
    cotangent,
):
    hidden = hidden_in[0].astype(F32)
    rows, width = hidden.shape
    tokens = rows * count
    heads = QUERY_HEADS // count
    repeat = sharing(count)
    me = lax.axis_index("ctx")

    first = segment_ids[0, ::RUN]
    place = positions[0, ::RUN]
    order = jnp.where(first == 0, place, place + (first - 1) * CONT) // RUN
    runs = jnp.zeros((1, 8, 128), jnp.int32).at[0, 0, : rows // RUN].set(order)

    def gather_groups(values, axis):
        return lax.all_gather(values, "fsdp", axis=axis, tiled=True)

    def scatter_groups(values):
        return lax.psum_scatter(values, "fsdp", scatter_dimension=0, tiled=True)

    w_out = gather_groups(out_weight, 0)
    w_down = gather_groups(down_weight, 0)
    qkv_parts = spread_qkv(count, 1, qkv_weight)
    normed_local = norm_rows(hidden, attn_gain).astype(BF16)
    normed, all_runs, mlp_parts = opening(count, 2, normed_local, runs, gate_up)
    w_qkv = gather_groups(qkv_parts, 1).reshape(width, -1)
    w_gu = gather_groups(mlp_parts, 1).reshape(width, -1)
    run_order = all_runs[:, 0, : rows // RUN].reshape(-1)
    cosine, sine = rotary(tokens)
    q_gain_row = query_norm_gain[None, :]
    k_gain_row = k_gain[None, :]

    joined = jnp.dot(normed, w_qkv, preferred_element_type=F32)
    attended, raw, queries, keys, values, mixed, lse = attention(
        heads, run_order, joined, cosine, sine, q_gain_row, k_gain_row
    )
    middle = hidden + product_scatter(count, 3, attended, w_out, False)
    second = gather_ctx(count, 4, norm_rows(middle, mlp_gain).astype(BF16))
    both = jnp.dot(second, w_gu, preferred_element_type=F32)
    own = both.shape[1] // 2
    gate, up = both[:, :own], both[:, own:]
    sigmoid = jax.nn.sigmoid(gate)
    activated = (gate * sigmoid * up).astype(BF16)

    upstream = gather_ctx(count, 5, cotangent[0])
    d_down = jnp.dot(activated.T, upstream, preferred_element_type=F32).astype(BF16)
    d_down = scatter_groups(d_down)
    d_activated = lax.dot_general(
        upstream, w_down, (((1,), (1,)), ((), ())), preferred_element_type=F32
    ).astype(BF16).astype(F32)
    d_gate = d_activated * up * sigmoid * (1.0 + gate * (1.0 - sigmoid))
    d_up = d_activated * gate * sigmoid
    d_both = jnp.concatenate([d_gate, d_up], axis=1).astype(BF16)

    def weight_grad(left, right):
        grad = lax.dot_general(left, right, (((0,), (0,)), ((), ())), preferred_element_type=F32)
        grad = grad.astype(BF16).reshape(count, groups, -1, right.shape[1])
        return scatter_groups(grad.transpose(1, 0, 2, 3).reshape(groups * count, -1, right.shape[1]))

    gu_parts = weight_grad(second, d_both)
    d_second = product_scatter(count, 6, d_both, w_gu, True)
    middle_back, mlp_gain_grad = norm_back(middle, mlp_gain, d_second)
    d_middle = cotangent[0].astype(F32) + middle_back
    middle_low = gather_ctx(count, 7, d_middle.astype(BF16))
    d_out = lax.dot_general(
        attended, middle_low, (((0,), (0,)), ((), ())), preferred_element_type=F32
    ).astype(BF16)
    d_out = scatter_groups(d_out)
    d_attended = lax.dot_general(
        middle_low, w_out, (((1,), (1,)), ((), ())), preferred_element_type=F32
    ).astype(BF16)
    d_queries, d_keys, d_values = attention_back(
        heads, run_order, d_attended, queries, keys, values, mixed, lse
    )
    share = jnp.ones((2, HEAD), F32)
    if repeat > 1:
        swap = [(index, index ^ 1) for index in range(count)]
        d_keys = d_keys + lax.ppermute(d_keys, "ctx", swap)
        d_values = d_values + lax.ppermute(d_values, "ctx", swap)
        mine = lax.rem(me, 2) == jnp.arange(2)
        share = share * mine[:, None].astype(F32)
    d_joined, q_gain_grad, k_gain_grad = joined_back(
        heads, run_order, raw, d_queries, d_keys, d_values, cosine, sine, q_gain_row, k_gain_row, share
    )
    qkv_grad_parts = weight_grad(normed, d_joined)
    d_normed = product_scatter(count, 8, d_joined, w_qkv, True)
    output = middle + product_scatter(count, 9, activated, w_down, False)
    hidden_back, attn_gain_grad = norm_back(hidden, attn_gain, d_normed)
    d_hidden = d_middle + hidden_back

    d_gate_up = return_columns(count, 10, mlp_spans, 2 * FF, gu_parts)
    qkv_width = qkv_weight.shape[1]
    d_qkv = return_columns(count, 11, qkv_spans, qkv_width, qkv_grad_parts)
    small = jnp.concatenate([attn_gain_grad, mlp_gain_grad, q_gain_grad[0], k_gain_grad[0]])
    padded = -(-small.shape[0] // 1024) * 1024
    small = jnp.pad(small, (0, padded - small.shape[0])).reshape(-1, 128)
    summed = total(count, groups, 12, small).reshape(-1)
    return (
        output.astype(BF16)[None],
        d_hidden[None],
        summed[:width],
        d_qkv.astype(F32),
        summed[2 * width : 2 * width + HEAD],
        summed[2 * width + HEAD : 2 * width + 2 * HEAD],
        d_out.astype(F32),
        summed[width : 2 * width],
        d_gate_up.astype(F32),
        d_down.astype(F32),
    )


def solution(mesh):
    return jax.shard_map(
        functools.partial(body, mesh.shape["ctx"], mesh.shape["fsdp"]),
        mesh=mesh,
        in_specs=(
            P("fsdp", "ctx", None),
            P("fsdp", "ctx"),
            P("fsdp", "ctx"),
            P(),
            P(("ctx", "fsdp"), None),
            P(),
            P(),
            P(("ctx", "fsdp"), None),
            P(),
            P(("ctx", "fsdp"), None),
            P(("ctx", "fsdp"), None),
            P("fsdp", "ctx", None),
        ),
        out_specs=(
            P("fsdp", "ctx", None),
            P("fsdp", "ctx", None),
            P(),
            P(("ctx", "fsdp"), None),
            P(),
            P(),
            P(("ctx", "fsdp"), None),
            P(),
            P(("ctx", "fsdp"), None),
            P(("ctx", "fsdp"), None),
        ),
        check_vma=False,
    )
```

```python
import functools
import math

import jax
import jax.numpy as jnp
import numpy as np
from jax import lax
from jax.experimental import pallas as pl
from jax.experimental.pallas import tpu as pltpu
from jax.sharding import PartitionSpec as P

QUERY_HEADS = 16
KEY_VALUE_HEADS = 8
HEAD = 128
FF = 6144
PROMPT = 1024
CONT = 128
RUN = 32
EPS = 1e-06
ROPE_BASE = 1000000.0
SCALE = HEAD ** (-0.5)
SCALE2 = SCALE * math.log2(math.e)
MESH = pl.DeviceIdType.MESH
ANY = pl.BlockSpec(memory_space=pl.ANY)
VMEM = pl.BlockSpec(memory_space=pltpu.VMEM)
SMEM = pl.BlockSpec(memory_space=pltpu.SMEM)
BF16 = jnp.bfloat16
F32 = jnp.float32
DMA = pltpu.SemaphoreType.DMA
VMEM_LIMIT = 60 * 2**20


def cost(us, flops=0):
    return pl.CostEstimate(flops=flops, bytes_accessed=int(us * 3.2e6), transcendentals=0)


def flip(me, mask):
    result = me
    bit = 1
    while bit <= mask:
        if mask & bit:
            result = result + bit - 2 * bit * lax.rem(lax.div(me, bit), 2)
        bit *= 2
    return result


def bits_of(count):
    bits = []
    bit = 1
    while bit < count:
        bits.append(bit)
        bit *= 2
    return bits


def greet(peers):
    barrier = pltpu.get_barrier_semaphore()
    for peer in peers:
        pl.semaphore_signal(barrier, inc=1, device_id=peer, device_id_type=MESH)
    pl.semaphore_wait(barrier, len(peers))


def gather_orders(count):
    chip_bits = bits_of(count)[1:]
    return [chip_bits + [1], chip_bits[::-1] + [1]]


def last_bit(order, slot):
    return [bit for bit in order if slot & bit][-1]


def gather_rows(count, me, group, source, target, send, recv, own):
    rows = source.shape[0]
    half = rows // 2
    orders = gather_orders(count)
    copies = []

    def place(part, slot):
        return pl.multiple_of(flip(me, slot) * rows + part * half, half)

    def copy(part, slot, bit):
        there = target.at[pl.ds(place(part, slot), half)]
        origin = source.at[pl.ds(part * half, half)] if slot == 0 else there
        number = part * count + (slot ^ bit)
        return pltpu.make_async_remote_copy(
            origin,
            there,
            send.at[number],
            recv.at[number],
            device_id=(flip(me, bit), group),
            device_id_type=MESH,
        )

    def keep(part):
        there = target.at[pl.ds(place(part, 0), half)]
        return pltpu.make_async_copy(source.at[pl.ds(part * half, half)], there, own.at[part])

    def start(part):
        for bit in orders[part]:
            item = copy(part, 0, bit)
            item.start()
            copies.append(item)
        keep(part).start()

    def wait(part, slot):
        there = target.at[pl.ds(place(part, slot), half)]
        number = part * count + slot
        pltpu.make_async_remote_copy(
            there,
            there,
            send.at[number],
            recv.at[number],
            device_id=(flip(me, last_bit(orders[part], slot)), group),
            device_id_type=MESH,
        ).wait_recv()

    def finish(arrived=None):
        waits = []
        for part in (0, 1):
            order = orders[part]
            for slot in range(1, count):
                last = order.index(last_bit(order, slot))
                waits.append((last, bin(slot).count("1"), part, slot))
            if arrived:
                arrived(place(part, 0), source, part * half)
        for last, _, part, slot in sorted(waits):
            wait(part, slot)
            for bit in orders[part][last + 1 :]:
                item = copy(part, slot, bit)
                item.start()
                copies.append(item)
            if arrived:
                arrived(place(part, slot), target, place(part, slot))
        for part in (0, 1):
            keep(part).wait()
        for item in copies:
            item.wait_send()

    return start, finish


def trade(count, me, group, pieces, source, target, send, recv):
    copies = []
    local = []
    for slot in list(range(1, count)) + [0]:
        peer = flip(me, slot)
        for number, (origin, place) in enumerate(pieces(peer, me)):
            total = len(pieces(peer, me))
            index = slot * total + number
            if slot == 0:
                item = pltpu.make_async_copy(source.at[origin], target.at[place], send.at[index])
                local.append(item)
            else:
                item = pltpu.make_async_remote_copy(
                    source.at[origin],
                    target.at[place],
                    send.at[index],
                    recv.at[index],
                    device_id=(peer, group),
                    device_id_type=MESH,
                )
                copies.append(item)
            item.start()

    def finish():
        for item in local:
            item.wait()
        for slot in range(1, count):
            peer = flip(me, slot)
            listed = pieces(me, peer)
            for number, (origin, place) in enumerate(listed):
                index = slot * len(listed) + number
                pltpu.make_async_remote_copy(
                    source.at[origin],
                    target.at[place],
                    send.at[index],
                    recv.at[index],
                    device_id=(peer, group),
                    device_id_type=MESH,
                ).wait_recv()
        for item in copies:
            item.wait_send()

    return finish


def span(start, width):
    return pl.ds(pl.multiple_of(start, HEAD), width)


def sharing(count):
    if count not in (KEY_VALUE_HEADS, QUERY_HEADS):
        raise ValueError(count)
    return count // KEY_VALUE_HEADS


def qkv_spans(count, device, gradients=False):
    own = QUERY_HEADS // count * HEAD
    repeat = sharing(count)
    queries = QUERY_HEADS * HEAD
    shared = lax.div(device, repeat) * HEAD
    if repeat == 2 and gradients:
        which = lax.rem(device, 2)
        return [
            (device * own, 0, own),
            (queries + which * (KEY_VALUE_HEADS * HEAD) + shared, own + which * HEAD, HEAD),
        ]
    return [
        (device * own, 0, own),
        (queries + shared, own, HEAD),
        (queries + KEY_VALUE_HEADS * HEAD + shared, own + HEAD, HEAD),
    ]


def mlp_spans(count, device, gradients=False):
    own = FF // count
    return [(device * own, 0, own), (FF + device * own, own, own)]


def outgoing(spans, count):
    def pieces(device, owner):
        return [
            ((slice(None), span(whole, width)), (owner, slice(None), pl.ds(part, width)))
            for whole, part, width in spans(count, device)
        ]

    return pieces


def incoming(spans, count):
    def pieces(device, owner):
        return [
            ((device, slice(None), span(part, width)), (slice(None), span(whole, width)))
            for whole, part, width in spans(count, owner, True)
        ]

    return pieces


def everyone(count, me, group):
    return [(flip(me, slot), group) for slot in range(1, count)]


def spread_kernel(count, qkv, mlp, qkv_parts, mlp_parts, send, recv, mlp_send, mlp_recv):
    me = lax.axis_index("ctx")
    group = lax.axis_index("fsdp")
    greet(everyone(count, me, group))
    finish = trade(count, me, group, outgoing(qkv_spans, count), qkv, qkv_parts, send, recv)
    finish_mlp = trade(count, me, group, outgoing(mlp_spans, count), mlp, mlp_parts, mlp_send, mlp_recv)
    finish()
    finish_mlp()


def spread(count, collective, qkv, mlp):
    rows = qkv.shape[0]
    width = QUERY_HEADS // count * HEAD + 2 * HEAD
    return pl.pallas_call(
        functools.partial(spread_kernel, count),
        out_shape=[
            jax.ShapeDtypeStruct((count, rows, width), BF16),
            jax.ShapeDtypeStruct((count, rows, 2 * FF // count), BF16),
        ],
        in_specs=[ANY, ANY],
        out_specs=[ANY, ANY],
        scratch_shapes=[DMA((3 * count,)), DMA((3 * count,)), DMA((2 * count,)), DMA((2 * count,))],
        compiler_params=pltpu.CompilerParams(collective_id=collective, has_side_effects=True),
        cost_estimate=cost(28),
    )(qkv, mlp)


def opening_kernel(count, normed, runs, rows, all_runs, send, recv, own, run_send, run_recv):
    me = lax.axis_index("ctx")
    group = lax.axis_index("fsdp")
    greet(everyone(count, me, group))
    finish_runs = trade(
        count, me, group, lambda device, owner: [((0,), (owner,))], runs, all_runs, run_send, run_recv
    )
    start, finish = gather_rows(count, me, group, normed, rows, send, recv, own)
    start(0)
    start(1)
    finish()
    finish_runs()


def opening(count, collective, normed, runs):
    tokens, width = normed.shape
    return pl.pallas_call(
        functools.partial(opening_kernel, count),
        out_shape=[
            jax.ShapeDtypeStruct((count * tokens, width), BF16),
            jax.ShapeDtypeStruct((count, 8, 128), jnp.int32),
        ],
        in_specs=[ANY, ANY],
        out_specs=[ANY, ANY],
        scratch_shapes=[DMA((2 * count,)), DMA((2 * count,)), DMA((2,)), DMA((count,)), DMA((count,))],
        compiler_params=pltpu.CompilerParams(collective_id=collective, has_side_effects=True),
        cost_estimate=cost(45),
    )(normed, runs)


def across(count, bit, values):
    return lax.ppermute(values, "ctx", [(index, index ^ bit) for index in range(count)])


def join_kernel(count, slots, *refs):
    blocks, (target, send, recv) = refs[:-3], refs[-3:]
    me = lax.axis_index("ctx")
    group = lax.axis_index("fsdp")
    other = flip(me, 1)
    greet([(other, group)])
    half = blocks[0].shape[1]
    items = []
    for block, (part, masks) in zip(blocks, slots):
        items += [(block, index, part, mask) for index, mask in enumerate(masks)]

    def place(number, owner):
        _, _, part, mask = items[number]
        return pl.ds(pl.multiple_of(flip(owner, mask) * 2 * half + part * half, half), half)

    def copy(number, owner):
        block, index = items[number][:2]
        return pltpu.make_async_remote_copy(
            block.at[index],
            target.at[place(number, owner)],
            send.at[number],
            recv.at[number],
            device_id=(other, group),
            device_id_type=MESH,
        )

    for number in range(len(items)):
        copy(number, me).start()
    for number in range(len(items)):
        block, index = items[number][:2]
        target[place(number, me), :] = block[index]
    for number in range(len(items)):
        copy(number, other).wait_recv()
    for number in range(len(items)):
        copy(number, me).wait_send()


def gather_step(count, masks, blocks, step):
    arrived, filled = [], []
    for part, order in enumerate(gather_orders(count)):
        arrived.append(across(count, order[step], blocks[part]))
        filled.append([mask ^ order[step] for mask in masks[part]])
    return arrived, filled


def gather_join(count, collective, masks, blocks, filled, arrived):
    slots = []
    for part in (0, 1):
        slots += [(part, masks[part]), (part, filled[part])]
    held = [block for pair in zip(blocks, arrived) for block in pair]
    half, width = held[0].shape[1:]
    return pl.pallas_call(
        functools.partial(join_kernel, count, slots),
        out_shape=jax.ShapeDtypeStruct((count * 2 * half, width), BF16),
        in_specs=[VMEM] * len(held),
        out_specs=VMEM,
        scratch_shapes=[DMA((count,)), DMA((count,))],
        compiler_params=pltpu.CompilerParams(
            collective_id=collective, has_side_effects=True, vmem_limit_bytes=VMEM_LIMIT
        ),
        cost_estimate=cost(13),
    )(*held)


def last_kernel(
    count, groups, values, parts, result, columns, near, far, send, recv, far_send, far_recv, part_send, part_recv
):
    me = lax.axis_index("ctx")
    group = lax.axis_index("fsdp")
    others = [lax.rem(group + step, groups) for step in range(1, groups)]
    greet(everyone(count, me, group) + [(me, other) for other in others])
    copies = []
    for slot in range(1, count):
        item = pltpu.make_async_remote_copy(
            values,
            near.at[me],
            send.at[slot],
            recv.at[slot],
            device_id=(flip(me, slot), group),
            device_id_type=MESH,
        )
        item.start()
        copies.append(item)
    finish = trade(count, me, group, incoming(qkv_spans, count), parts, columns, part_send, part_recv)
    near[me] = values[...]
    for item in copies:
        item.wait()
    summed = near[0]
    for index in range(1, count):
        summed = summed + near[index]
    far[group] = summed
    copies = []
    for step, other in enumerate(others):
        item = pltpu.make_async_remote_copy(
            far.at[group],
            far.at[group],
            far_send.at[step],
            far_recv.at[step],
            device_id=(me, other),
            device_id_type=MESH,
        )
        item.start()
        copies.append(item)
    for item in copies:
        item.wait()
    summed = far[0]
    for index in range(1, groups):
        summed = summed + far[index]
    result[...] = summed
    finish()


def last(count, groups, collective, values, parts, width):
    shape = values.shape
    pieces = len(qkv_spans(count, 0, True))
    return pl.pallas_call(
        functools.partial(last_kernel, count, groups),
        out_shape=[
            jax.ShapeDtypeStruct(shape, F32),
            jax.ShapeDtypeStruct((parts.shape[1], width), BF16),
        ],
        in_specs=[VMEM, ANY],
        out_specs=[VMEM, ANY],
        scratch_shapes=[
            pltpu.VMEM((count,) + shape, F32),
            pltpu.VMEM((groups,) + shape, F32),
            DMA((count,)),
            DMA((count,)),
            DMA((groups,)),
            DMA((groups,)),
            DMA((pieces * count,)),
            DMA((pieces * count,)),
        ],
        compiler_params=pltpu.CompilerParams(collective_id=collective, has_side_effects=True),
        cost_estimate=cost(14),
    )(values, parts)


def product_scatter(count, me, group, flipped, left, right, done, kept, near_out, near_in, far_out, far_in, ns, nr, fs, fr):
    rows, width = kept.shape
    half = rows // 2
    bits = bits_of(count)
    orders = [bits[1:][::-1], bits[1:]]
    tile = min(512, width)

    def product(slot, store):
        start = pl.multiple_of(flip(me, slot) * rows, rows)
        block = left[pl.ds(start, rows), :]

        def step(index, carry):
            columns = pl.ds(pl.multiple_of(index * tile, tile), tile)
            if flipped:
                value = nt(block, right[columns, :])
            else:
                value = jnp.dot(block, right[:, columns], preferred_element_type=F32)
            store(columns, value)
            return carry

        lax.fori_loop(0, width // tile, step, 0)

    def first(part, slot):
        return [bit for bit in orders[part] if slot & bit][0]

    def near(pair):
        return pltpu.make_async_remote_copy(
            near_out.at[pair],
            near_in.at[pair],
            ns.at[pair],
            nr.at[pair],
            device_id=(flip(me, 1), group),
            device_id_type=MESH,
        )

    def number(part, pair):
        return part * (count // 2 - 1) + pair - 1

    def far(part, pair):
        index = number(part, pair)
        return pltpu.make_async_remote_copy(
            far_out.at[index],
            far_in.at[index],
            fs.at[index],
            fr.at[index],
            device_id=(flip(me, first(part, 2 * pair)), group),
            device_id_type=MESH,
        )

    def needs(part, pair):
        found = []
        for bit in orders[part]:
            if 2 * pair & bit:
                break
            found.append((2 * pair ^ bit) // 2)
        return found

    def settle(part, pair):
        if pair == 0:
            value = kept[pl.ds(part * half, half), :]
        else:
            value = far_out[number(part, pair)].astype(F32)
        for other in needs(part, pair):
            far(part, other).wait_recv()
            value = value + far_in[number(part, other)].astype(F32)
        if pair == 0:
            done(part, value)
        else:
            far_out[number(part, pair)] = value.astype(BF16)
            far(part, pair).start()

    pairs = list(range(count // 2))[::-1]

    def send_near(pair):
        def store(columns, value):
            near_out[pair, :, columns] = value.astype(BF16)

        product(2 * pair + 1, store)
        near(pair).start()

    def sum_near(pair):
        near(pair).wait_recv()

        def store(columns, value):
            value = value + near_in[pair, :, columns].astype(F32)
            if pair == 0:
                kept[:, columns] = value
            else:
                for part in (0, 1):
                    far_out[number(part, pair), :, columns] = value[part * half : (part + 1) * half].astype(BF16)

        product(2 * pair, store)
        for part in (0, 1):
            if pair and not needs(part, pair):
                far(part, pair).start()

    def begin():
        send_near(pairs[0])
        for pair in pairs:
            if pair:
                send_near(pair - 1)
            sum_near(pair)

    def end():
        for pair in pairs:
            for part in (0, 1):
                if needs(part, pair):
                    settle(part, pair)
        for pair in pairs:
            near(pair).wait_send()
            for part in (0, 1):
                if pair:
                    far(part, pair).wait_send()

    return begin, end


def scatter_scratch(count, rows, width):
    pairs = count // 2
    links = 2 * (pairs - 1)
    return [
        pltpu.VMEM((rows, width), F32),
        pltpu.VMEM((pairs, rows, width), BF16),
        pltpu.VMEM((pairs, rows, width), BF16),
        pltpu.VMEM((links, rows // 2, width), BF16),
        pltpu.VMEM((links, rows // 2, width), BF16),
        DMA((pairs,)),
        DMA((pairs,)),
        DMA((links,)),
        DMA((links,)),
    ]


SCATTER = 9


def comm_params(collective):
    return pltpu.CompilerParams(
        collective_id=collective, has_side_effects=True, vmem_limit_bytes=VMEM_LIMIT
    )


def row_blocks(first, count, step):
    def body(index, carry):
        step(pl.multiple_of(first + index * 32, 32), pl.multiple_of(index * 32, 32))
        return carry

    lax.fori_loop(0, count // 32, body, 0)


def norm_back(values, gain, grad):
    scale = lax.rsqrt(jnp.mean(values * values, axis=-1, keepdims=True) + EPS)
    scaled = values * scale
    pushed = grad * gain
    back = scale * (pushed - scaled * jnp.mean(pushed * scaled, axis=-1, keepdims=True))
    return back, jnp.sum(grad * scaled, axis=0, keepdims=True)


def norm_rows(values, gain):
    return values * lax.rsqrt(jnp.mean(values * values, axis=-1, keepdims=True) + EPS) * gain


def middle_kernel(count, left, right, hidden, gain, middle, gathered, own_rows, sums, *scratch):
    me = lax.axis_index("ctx")
    group = lax.axis_index("fsdp")
    rows = middle.shape[0]
    half = rows // 2
    greet([(flip(me, bit), group) for bit in bits_of(count)])
    start, finish = gather_rows(count, me, group, own_rows, gathered, *scratch[SCATTER:])

    def done(part, value):
        sums[...] = value

        def step(row, place):
            total_rows = hidden[pl.ds(row, 32), :].astype(F32) + sums[pl.ds(place, 32), :]
            middle[pl.ds(row, 32), :] = total_rows
            own_rows[pl.ds(row, 32), :] = norm_rows(total_rows, gain[...]).astype(BF16)

        row_blocks(part * half, half, step)
        start(part)

    begin, end = product_scatter(count, me, group, False, left, right, done, *scratch[:SCATTER])
    begin()
    end()
    finish()


def gather_scratch(count):
    return [DMA((2 * count,)), DMA((2 * count,)), DMA((2,))]


def middle_and_second(count, collective, left, right, hidden, gain):
    rows, width = hidden.shape
    return pl.pallas_call(
        functools.partial(middle_kernel, count),
        out_shape=[
            jax.ShapeDtypeStruct((rows, width), F32),
            jax.ShapeDtypeStruct((count * rows, width), BF16),
        ],
        in_specs=[VMEM] * 4,
        out_specs=[VMEM, ANY],
        scratch_shapes=[pltpu.VMEM((rows, width), BF16), pltpu.VMEM((rows // 2, width), F32)]
        + scatter_scratch(count, rows, width)
        + gather_scratch(count),
        compiler_params=comm_params(collective),
        cost_estimate=cost(80, 2 * left.shape[0] * left.shape[1] * width),
    )(left, right, hidden, gain)


def back_kernel(
    count,
    left,
    right,
    middle,
    cotangent,
    gain,
    attended,
    out_weight,
    d_middle,
    d_gain,
    d_attended,
    d_out,
    own_rows,
    sums,
    gathered,
    turned,
    out_sum,
    *scratch,
):
    me = lax.axis_index("ctx")
    group = lax.axis_index("fsdp")
    rows, width = middle.shape
    half = rows // 2
    greet([(flip(me, bit), group) for bit in bits_of(count)])
    start, finish = gather_rows(count, me, group, own_rows, gathered, *scratch[SCATTER:])
    d_gain[...] = jnp.zeros_like(d_gain)

    def done(part, value):
        sums[...] = value

        def step(row, place):
            span_rows = pl.ds(row, 32)
            back, gain_part = norm_back(middle[span_rows, :], gain[...], sums[pl.ds(place, 32), :])
            back = back + cotangent[span_rows, :].astype(F32)
            d_middle[span_rows, :] = back
            own_rows[span_rows, :] = back.astype(BF16)
            d_gain[...] += gain_part

        row_blocks(part * half, half, step)
        start(part)

    begin, end = product_scatter(count, me, group, True, left, right, done, *scratch[:SCATTER])
    begin()
    out_sum[...] = jnp.zeros_like(out_sum)

    def turn(index, carry):
        span_rows = pl.ds(pl.multiple_of(index * 256, 256), 256)
        turned[:, span_rows] = attended[span_rows, :].astype(F32).T.astype(BF16)
        return carry

    lax.fori_loop(0, attended.shape[0] // 256, turn, 0)
    end()

    def arrived(row, ref, place):
        block = ref[pl.ds(place, half), :]
        d_attended[pl.ds(row, half), :] = nt(block, out_weight[...]).astype(BF16)
        if half % 128 == 0:
            out_sum[...] += jnp.dot(turned[:, pl.ds(row, half)], block, preferred_element_type=F32)

    finish(arrived)
    if half % 128:
        out_sum[...] = jnp.dot(turned[...], gathered[...], preferred_element_type=F32)
    d_out[...] = out_sum[...].astype(BF16)


def back_through_middle(count, collective, left, right, middle, cotangent, gain, attended, out_weight):
    rows, width = middle.shape
    tokens, wide = attended.shape
    shape = jax.ShapeDtypeStruct
    return pl.pallas_call(
        functools.partial(back_kernel, count),
        out_shape=[
            shape((rows, width), F32),
            shape((1, width), F32),
            shape((tokens, wide), BF16),
            shape((wide, width), BF16),
        ],
        in_specs=[VMEM] * 7,
        out_specs=[VMEM] * 4,
        scratch_shapes=[
            pltpu.VMEM((rows, width), BF16),
            pltpu.VMEM((rows // 2, width), F32),
            pltpu.VMEM((tokens, width), BF16),
            pltpu.VMEM((wide, tokens), BF16),
            pltpu.VMEM((wide, width), F32),
        ]
        + scatter_scratch(count, rows, width)
        + gather_scratch(count),
        compiler_params=comm_params(collective),
        cost_estimate=cost(85, 2 * left.shape[0] * left.shape[1] * width),
    )(left, right, middle, cotangent, gain, attended, out_weight)


def input_kernel(
    count, left, right, hidden, d_middle, gain, parts, d_hidden, d_gain, columns, sums, send, recv, *scratch
):
    me = lax.axis_index("ctx")
    group = lax.axis_index("fsdp")
    half = hidden.shape[0] // 2
    greet(everyone(count, me, group))
    finish = trade(count, me, group, incoming(mlp_spans, count), parts, columns, send, recv)
    d_gain[...] = jnp.zeros_like(d_gain)

    def done(part, value):
        sums[...] = value

        def step(row, place):
            span_rows = pl.ds(row, 32)
            values = hidden[span_rows, :].astype(F32)
            back, gain_part = norm_back(values, gain[...], sums[pl.ds(place, 32), :])
            d_hidden[span_rows, :] = d_middle[span_rows, :] + back
            d_gain[...] += gain_part

        row_blocks(part * half, half, step)

    begin, end = product_scatter(count, me, group, True, left, right, done, *scratch)
    begin()
    end()
    finish()


def back_to_input(count, collective, left, right, hidden, d_middle, gain, parts):
    rows, width = hidden.shape
    shape = jax.ShapeDtypeStruct
    return pl.pallas_call(
        functools.partial(input_kernel, count),
        out_shape=[
            shape((rows, width), F32),
            shape((1, width), F32),
            shape((parts.shape[1], 2 * FF), BF16),
        ],
        in_specs=[VMEM] * 5 + [ANY],
        out_specs=[VMEM, VMEM, ANY],
        scratch_shapes=[pltpu.VMEM((rows // 2, width), F32), DMA((2 * count,)), DMA((2 * count,))]
        + scatter_scratch(count, rows, width),
        compiler_params=comm_params(collective),
        cost_estimate=cost(60, 2 * left.shape[0] * left.shape[1] * width),
    )(left, right, hidden, d_middle, gain, parts)


def output_kernel(count, left, right, middle, output, *scratch):
    me = lax.axis_index("ctx")
    group = lax.axis_index("fsdp")
    half = middle.shape[0] // 2
    greet([(flip(me, bit), group) for bit in bits_of(count)])

    def done(part, value):
        span_rows = pl.ds(part * half, half)
        output[span_rows, :] = (middle[span_rows, :] + value).astype(BF16)

    begin, end = product_scatter(count, me, group, False, left, right, done, *scratch)
    begin()
    end()


def output_rows(count, collective, left, right, middle):
    rows, width = middle.shape
    return pl.pallas_call(
        functools.partial(output_kernel, count),
        out_shape=jax.ShapeDtypeStruct((rows, width), BF16),
        in_specs=[VMEM] * 3,
        out_specs=VMEM,
        scratch_shapes=scatter_scratch(count, rows, width),
        compiler_params=comm_params(collective),
        cost_estimate=cost(45, 2 * left.shape[0] * left.shape[1] * width),
    )(left, right, middle)


def swap_halves(value):
    return jnp.concatenate([value[:, HEAD // 2 :], value[:, : HEAD // 2]], axis=1)


def nt(left, right):
    return lax.dot_general(left, right, (((1,), (1,)), ((), ())), preferred_element_type=F32)


def causal(keys, queries):
    key = lax.broadcasted_iota(jnp.int32, (keys, queries), 0)
    query = lax.rem(lax.broadcasted_iota(jnp.int32, (keys, queries), 1), CONT)
    return key <= query


def attention_kernel(
    heads, runs, joined, cosine, sine, q_gain, k_gain, attended, raw, queries, keys, values, mixed, lse, turned, placed
):
    tokens = joined.shape[0]
    blocks = tokens // CONT
    wide = heads * CONT

    def sort(run, carry):
        origin = pl.multiple_of(run * RUN, RUN)
        place = pl.multiple_of(runs[run] * RUN, RUN)
        raw[pl.ds(place, RUN), :] = joined[pl.ds(origin, RUN), :]
        return carry

    lax.fori_loop(0, tokens // RUN, sort, 0)

    def prepare(block, carry):
        span_rows = pl.ds(pl.multiple_of(block * CONT, CONT), CONT)
        cos_rows = cosine[span_rows, :]
        sin_rows = sine[span_rows, :]

        def turn(value, gain):
            value = value * lax.rsqrt(jnp.mean(value * value, axis=-1, keepdims=True) + EPS) * gain
            return (value * cos_rows + swap_halves(value) * sin_rows).astype(BF16)

        for head in range(heads):
            piece = raw[span_rows, head * HEAD : (head + 1) * HEAD]
            queries[block, head * CONT : (head + 1) * CONT, :] = turn(piece, q_gain[...])
        keys[span_rows, :] = turn(raw[span_rows, wide : wide + HEAD], k_gain[...])
        piece = raw[span_rows, wide + HEAD : wide + 2 * HEAD]
        values[span_rows, :] = piece.astype(BF16)
        turned[:, span_rows] = piece.T.astype(BF16)
        return carry

    lax.fori_loop(0, blocks, prepare, 0)

    def attend(block, own, before):
        query = queries[block]
        own_rows = pl.ds(own, CONT)
        weight = jnp.exp2(nt(keys[own_rows, :], query) * SCALE2)
        weight = jnp.where(causal(CONT, wide), weight, 0.0)
        sums = jnp.sum(weight, axis=0, keepdims=True)
        out = jnp.dot(turned[:, own_rows], weight.astype(BF16), preferred_element_type=F32)
        if before:
            weight = jnp.exp2(nt(keys[:before, :], query) * SCALE2)
            sums = sums + jnp.sum(weight, axis=0, keepdims=True)
            out = out + jnp.dot(turned[:, :before], weight.astype(BF16), preferred_element_type=F32)
        out = out / sums
        mixed[block] = out
        lse[block] = jnp.broadcast_to(jnp.log2(sums), (8, wide))
        for head in range(heads):
            placed[own_rows, head * HEAD : (head + 1) * HEAD] = out[
                :, head * CONT : (head + 1) * CONT
            ].T.astype(BF16)

    for block in range(PROMPT // CONT):
        attend(block, block * CONT, block * CONT)

    def continuation(block, carry):
        attend(block, pl.multiple_of(block * CONT, CONT), PROMPT)
        return carry

    lax.fori_loop(PROMPT // CONT, blocks, continuation, 0)

    def unsort(run, carry):
        origin = pl.multiple_of(run * RUN, RUN)
        place = pl.multiple_of(runs[run] * RUN, RUN)
        attended[pl.ds(origin, RUN), :] = placed[pl.ds(place, RUN), :]
        return carry

    lax.fori_loop(0, tokens // RUN, unsort, 0)


def attention(heads, runs, joined, cosine, sine, q_gain, k_gain):
    tokens = joined.shape[0]
    blocks = tokens // CONT
    wide = heads * CONT
    shape = jax.ShapeDtypeStruct
    return pl.pallas_call(
        functools.partial(attention_kernel, heads),
        out_shape=[
            shape((tokens, wide), BF16),
            shape(joined.shape, F32),
            shape((blocks, wide, HEAD), BF16),
            shape((tokens, HEAD), BF16),
            shape((tokens, HEAD), BF16),
            shape((blocks, HEAD, wide), F32),
            shape((blocks, 8, wide), F32),
        ],
        in_specs=[SMEM, VMEM, VMEM, VMEM, VMEM, VMEM],
        out_specs=[VMEM] * 7,
        scratch_shapes=[pltpu.VMEM((HEAD, tokens), BF16), pltpu.VMEM((tokens, wide), BF16)],
        compiler_params=pltpu.CompilerParams(vmem_limit_bytes=VMEM_LIMIT),
        cost_estimate=cost(15),
    )(runs, joined, cosine, sine, q_gain, k_gain)


def attention_back_kernel(
    heads, runs, d_attended, queries, keys, values, mixed, lse, d_queries, d_keys, d_values, arrived, keys_turned
):
    tokens = keys.shape[0]
    blocks = tokens // CONT
    wide = heads * CONT

    def sort(run, carry):
        origin = pl.multiple_of(run * RUN, RUN)
        place = pl.multiple_of(runs[run] * RUN, RUN)
        arrived[pl.ds(place, RUN), :] = d_attended[pl.ds(origin, RUN), :]
        return carry

    lax.fori_loop(0, tokens // RUN, sort, 0)
    d_keys[...] = jnp.zeros_like(d_keys)
    d_values[...] = jnp.zeros_like(d_values)

    def turn(block, carry):
        span_rows = pl.ds(pl.multiple_of(block * CONT, CONT), CONT)
        keys_turned[:, span_rows] = keys[span_rows, :].astype(F32).T.astype(BF16)
        return carry

    lax.fori_loop(0, blocks, turn, 0)

    def back(block, own, before):
        query = queries[block]
        own_rows = pl.ds(own, CONT)
        grad = jnp.concatenate(
            [arrived[own_rows, head * HEAD : (head + 1) * HEAD] for head in range(heads)], axis=0
        )
        grad_turned = grad.astype(F32).T
        delta = jnp.sum(grad_turned * mixed[block], axis=0, keepdims=True)
        total_row = lse[block][:1, :]

        def part(rows, count, masked):
            prob = jnp.exp2(nt(keys[rows, :], query) * SCALE2 - total_row)
            if masked:
                prob = jnp.where(causal(count, wide), prob, 0.0)
            score = (prob * (nt(values[rows, :], grad) - delta)).astype(BF16)
            d_values[rows, :] += jnp.dot(prob.astype(BF16), grad, preferred_element_type=F32)
            d_keys[rows, :] += jnp.dot(score, query, preferred_element_type=F32)
            return jnp.dot(keys_turned[:, rows], score, preferred_element_type=F32)

        result = part(own_rows, CONT, True)
        if before:
            result = result + part(slice(0, before), before, False)
        result = result * SCALE
        for head in range(heads):
            d_queries[own_rows, head * HEAD : (head + 1) * HEAD] = result[
                :, head * CONT : (head + 1) * CONT
            ].T.astype(BF16)

    for block in range(PROMPT // CONT):
        back(block, block * CONT, block * CONT)

    def continuation(block, carry):
        back(block, pl.multiple_of(block * CONT, CONT), PROMPT)
        return carry

    lax.fori_loop(PROMPT // CONT, blocks, continuation, 0)


def attention_back(heads, runs, d_attended, queries, keys, values, mixed, lse):
    tokens = keys.shape[0]
    wide = heads * CONT
    shape = jax.ShapeDtypeStruct
    return pl.pallas_call(
        functools.partial(attention_back_kernel, heads),
        out_shape=[shape((tokens, wide), BF16), shape((tokens, HEAD), F32), shape((tokens, HEAD), F32)],
        in_specs=[SMEM] + [VMEM] * 6,
        out_specs=[VMEM] * 3,
        scratch_shapes=[pltpu.VMEM((tokens, wide), BF16), pltpu.VMEM((HEAD, tokens), BF16)],
        compiler_params=pltpu.CompilerParams(vmem_limit_bytes=VMEM_LIMIT),
        cost_estimate=cost(25),
    )(runs, d_attended, queries, keys, values, mixed, lse)


def joined_back_kernel(
    heads, runs, raw, d_queries, d_keys, d_values, cosine, sine, q_gain, k_gain, share, d_joined, d_q_gain, d_k_gain, placed
):
    tokens = raw.shape[0]
    blocks = tokens // CONT
    wide = heads * CONT
    d_q_gain[...] = jnp.zeros_like(d_q_gain)
    d_k_gain[...] = jnp.zeros_like(d_k_gain)

    def step(block, carry):
        span_rows = pl.ds(pl.multiple_of(block * CONT, CONT), CONT)
        cos_rows = cosine[span_rows, :]
        sin_rows = sine[span_rows, :]

        def pull(value, grad, gain):
            grad = grad * cos_rows - swap_halves(grad) * sin_rows
            scale = lax.rsqrt(jnp.mean(value * value, axis=-1, keepdims=True) + EPS)
            scaled = value * scale
            gain_grad = jnp.sum(grad * scaled, axis=0, keepdims=True)
            grad = grad * gain
            return scale * (grad - scaled * jnp.mean(grad * scaled, axis=-1, keepdims=True)), gain_grad

        for head in range(heads):
            columns = slice(head * HEAD, (head + 1) * HEAD)
            grad, gain_grad = pull(
                raw[span_rows, columns], d_queries[span_rows, columns].astype(F32), q_gain[...]
            )
            placed[span_rows, columns] = grad.astype(BF16)
            d_q_gain[...] += gain_grad
        key_part, value_part = share[:1, :], share[1:, :]
        grad, gain_grad = pull(
            raw[span_rows, wide : wide + HEAD],
            (d_keys[span_rows, :] * SCALE).astype(BF16).astype(F32),
            k_gain[...],
        )
        placed[span_rows, wide : wide + HEAD] = (grad * key_part).astype(BF16)
        d_k_gain[...] += gain_grad * key_part
        placed[span_rows, wide + HEAD : wide + 2 * HEAD] = (d_values[span_rows, :] * value_part).astype(BF16)
        return carry

    lax.fori_loop(0, blocks, step, 0)

    def unsort(run, carry):
        origin = pl.multiple_of(run * RUN, RUN)
        place = pl.multiple_of(runs[run] * RUN, RUN)
        d_joined[pl.ds(origin, RUN), :] = placed[pl.ds(place, RUN), :]
        return carry

    lax.fori_loop(0, tokens // RUN, unsort, 0)


def joined_back(heads, runs, raw, d_queries, d_keys, d_values, cosine, sine, q_gain, k_gain, share):
    shape = jax.ShapeDtypeStruct
    return pl.pallas_call(
        functools.partial(joined_back_kernel, heads),
        out_shape=[shape(raw.shape, BF16), shape((1, HEAD), F32), shape((1, HEAD), F32)],
        in_specs=[SMEM] + [VMEM] * 9,
        out_specs=[VMEM] * 3,
        scratch_shapes=[pltpu.VMEM(raw.shape, BF16)],
        compiler_params=pltpu.CompilerParams(vmem_limit_bytes=VMEM_LIMIT),
        cost_estimate=cost(8),
    )(runs, raw, d_queries, d_keys, d_values, cosine, sine, q_gain, k_gain, share)


def rotary(tokens):
    index = np.arange(tokens)
    place = np.where(index < PROMPT, index, PROMPT + (index - PROMPT) % CONT).astype(np.float32)
    exponent = np.arange(HEAD // 2, dtype=np.float32) * np.float32(2.0 / HEAD)
    inverse = np.power(np.float32(ROPE_BASE), -exponent).astype(np.float32)
    angles = place[:, None] * inverse[None, :]
    cosine, sine = np.cos(angles), np.sin(angles)
    tables = np.concatenate([cosine, cosine], axis=1), np.concatenate([-sine, sine], axis=1)
    return tuple(jnp.asarray(table, F32) for table in tables)


def body(
    count,
    groups,
    hidden_in,
    segment_ids,
    positions,
    attn_gain,
    qkv_weight,
    query_norm_gain,
    k_gain,
    out_weight,
    mlp_gain,
    gate_up,
    down_weight,
    cotangent,
):
    hidden = hidden_in[0].astype(F32)
    rows, width = hidden.shape
    tokens = rows * count
    heads = QUERY_HEADS // count
    repeat = sharing(count)
    me = lax.axis_index("ctx")

    first = segment_ids[0, ::RUN]
    place = positions[0, ::RUN]
    order = jnp.where(first == 0, place, place + (first - 1) * CONT) // RUN
    runs = jnp.zeros((1, 8, 128), jnp.int32).at[0, 0, : rows // RUN].set(order)

    def gather_groups(values, axis):
        return lax.all_gather(values, "fsdp", axis=axis, tiled=True)

    def scatter_groups(values):
        return lax.psum_scatter(values, "fsdp", scatter_dimension=0, tiled=True)

    w_out = gather_groups(out_weight, 0)
    qkv_parts, mlp_parts = spread(count, 1, qkv_weight, gate_up)
    qkv_parts, w_out = lax.optimization_barrier((qkv_parts, w_out))
    w_qkv = gather_groups(qkv_parts, 1).reshape(width, -1)
    normed_local = norm_rows(hidden, attn_gain).astype(BF16)
    normed_local, qkv_parts = lax.optimization_barrier((normed_local, qkv_parts))
    normed, all_runs = opening(count, 2, normed_local, runs)
    mlp_parts, w_qkv, normed, upstream = lax.optimization_barrier((mlp_parts, w_qkv, normed, cotangent[0]))
    w_gu = gather_groups(mlp_parts, 1).reshape(width, -1)
    w_down = gather_groups(down_weight, 0)
    run_order = all_runs[:, 0, : rows // RUN].reshape(-1)
    cosine, sine = rotary(tokens)
    q_gain_row = query_norm_gain[None, :]
    k_gain_row = k_gain[None, :]

    blocks, masks = [upstream[None, : rows // 2], upstream[None, rows // 2 :]], [[0], [0]]
    chip_steps = len(bits_of(count)) - 1
    for step in range(chip_steps - 1):
        arrived, filled = gather_step(count, masks, blocks, step)
        if step == 0:
            joined = jnp.dot(normed, w_qkv, preferred_element_type=F32)
            joined, arrived = lax.optimization_barrier((joined, arrived))
        blocks = [jnp.concatenate(pair) for pair in zip(blocks, arrived)]
        masks = [held + more for held, more in zip(masks, filled)]
    arrived, filled = gather_step(count, masks, blocks, chip_steps - 1)
    attended, raw, queries, keys, values, mixed, lse = attention(
        heads, run_order, joined, cosine, sine, q_gain_row, k_gain_row
    )
    attended, arrived = lax.optimization_barrier((attended, arrived))
    middle, second = middle_and_second(count, 3, attended, w_out, hidden_in[0], mlp_gain[None, :])
    both = jnp.dot(second, w_gu, preferred_element_type=F32)
    own = both.shape[1] // 2
    gate, up = both[:, :own], both[:, own:]
    sigmoid = jax.nn.sigmoid(gate)
    activated = (gate * sigmoid * up).astype(BF16)

    activated, arrived = lax.optimization_barrier((activated, arrived))
    upstream = gather_join(count, 5, masks, blocks, filled, arrived)
    d_down = jnp.dot(activated.T, upstream, preferred_element_type=F32).astype(BF16)
    d_down, upstream = lax.optimization_barrier((d_down, upstream))
    d_down = scatter_groups(d_down)
    d_activated = lax.dot_general(
        upstream, w_down, (((1,), (1,)), ((), ())), preferred_element_type=F32
    ).astype(BF16).astype(F32)
    d_gate = d_activated * up * sigmoid * (1.0 + gate * (1.0 - sigmoid))
    d_up = d_activated * gate * sigmoid
    d_both = jnp.concatenate([d_gate, d_up], axis=1).astype(BF16)

    def weight_grad(left, right):
        grad = lax.dot_general(left, right, (((0,), (0,)), ((), ())), preferred_element_type=F32)
        grad = grad.astype(BF16).reshape(count, groups, -1, right.shape[1])
        return grad.transpose(1, 0, 2, 3).reshape(groups * count, -1, right.shape[1])

    gu_parts, d_both = lax.optimization_barrier((weight_grad(second, d_both), d_both))
    gu_parts = scatter_groups(gu_parts)
    d_middle, mlp_gain_grad, d_attended, d_out = back_through_middle(
        count, 6, d_both, w_gu, middle, cotangent[0], mlp_gain[None, :], attended, w_out
    )
    d_attended, d_down = lax.optimization_barrier((d_attended, d_down))
    d_queries, d_keys, d_values = attention_back(
        heads, run_order, d_attended, queries, keys, values, mixed, lse
    )
    share = jnp.ones((2, HEAD), F32)
    if repeat > 1:
        swap = [(index, index ^ 1) for index in range(count)]
        d_keys = d_keys + lax.ppermute(d_keys, "ctx", swap)
        d_values = d_values + lax.ppermute(d_values, "ctx", swap)
        mine = lax.rem(me, 2) == jnp.arange(2)
        share = share * mine[:, None].astype(F32)
    d_joined, q_gain_grad, k_gain_grad = joined_back(
        heads, run_order, raw, d_queries, d_keys, d_values, cosine, sine, q_gain_row, k_gain_row, share
    )
    qkv_grad_parts, d_joined = lax.optimization_barrier((weight_grad(normed, d_joined), d_joined))
    qkv_grad_parts, gu_parts = lax.optimization_barrier((qkv_grad_parts, gu_parts))
    qkv_grad_parts = scatter_groups(qkv_grad_parts)
    d_hidden, attn_gain_grad, d_gate_up = back_to_input(
        count, 8, d_joined, w_qkv, hidden_in[0], d_middle, attn_gain[None, :], gu_parts
    )
    d_out, qkv_grad_parts, d_hidden, activated = lax.optimization_barrier(
        (d_out, qkv_grad_parts, d_hidden, activated)
    )
    d_out = scatter_groups(d_out)
    output = output_rows(count, 9, activated, w_down, middle)

    small = jnp.concatenate([attn_gain_grad[0], mlp_gain_grad[0], q_gain_grad[0], k_gain_grad[0]])
    padded = -(-small.shape[0] // 1024) * 1024
    small = jnp.pad(small, (0, padded - small.shape[0])).reshape(-1, 128)
    summed, d_qkv = last(count, groups, 11, small, qkv_grad_parts, qkv_weight.shape[1])
    summed = summed.reshape(-1)
    return (
        output[None],
        d_hidden[None],
        summed[:width],
        d_qkv.astype(F32),
        summed[2 * width : 2 * width + HEAD],
        summed[2 * width + HEAD : 2 * width + 2 * HEAD],
        d_out.astype(F32),
        summed[width : 2 * width],
        d_gate_up.astype(F32),
        d_down.astype(F32),
    )


def solution(mesh):
    return jax.shard_map(
        functools.partial(body, mesh.shape["ctx"], mesh.shape["fsdp"]),
        mesh=mesh,
        in_specs=(
            P("fsdp", "ctx", None),
            P("fsdp", "ctx"),
            P("fsdp", "ctx"),
            P(),
            P(("ctx", "fsdp"), None),
            P(),
            P(),
            P(("ctx", "fsdp"), None),
            P(),
            P(("ctx", "fsdp"), None),
            P(("ctx", "fsdp"), None),
            P("fsdp", "ctx", None),
        ),
        out_specs=(
            P("fsdp", "ctx", None),
            P("fsdp", "ctx", None),
            P(),
            P(("ctx", "fsdp"), None),
            P(),
            P(),
            P(("ctx", "fsdp"), None),
            P(),
            P(("ctx", "fsdp"), None),
            P(("ctx", "fsdp"), None),
        ),
        check_vma=False,
    )
```

```python
import functools
import math

import jax
import jax.numpy as jnp
import numpy as np
from jax import lax
from jax.experimental import pallas as pl
from jax.experimental.pallas import tpu as pltpu
from jax.sharding import PartitionSpec as P

QUERY_HEADS = 16
KEY_VALUE_HEADS = 8
HEAD = 128
FF = 6144
PROMPT = 1024
CONT = 128
RUN = 32
EPS = 1e-06
ROPE_BASE = 1000000.0
SCALE = HEAD ** (-0.5)
SCALE2 = SCALE * math.log2(math.e)
MESH = pl.DeviceIdType.MESH
ANY = pl.BlockSpec(memory_space=pl.ANY)
VMEM = pl.BlockSpec(memory_space=pltpu.VMEM)
SMEM = pl.BlockSpec(memory_space=pltpu.SMEM)
BF16 = jnp.bfloat16
F32 = jnp.float32
DMA = pltpu.SemaphoreType.DMA
VMEM_LIMIT = 60 * 2**20


def cost(us):
    return pl.CostEstimate(flops=0, bytes_accessed=int(us * 1e6), transcendentals=0)


def flip(me, mask):
    result = me
    bit = 1
    while bit <= mask:
        if mask & bit:
            result = result + bit - 2 * bit * lax.rem(lax.div(me, bit), 2)
        bit *= 2
    return result


def bits_of(count):
    bits = []
    bit = 1
    while bit < count:
        bits.append(bit)
        bit *= 2
    return bits


def greet(peers):
    barrier = pltpu.get_barrier_semaphore()
    for peer in peers:
        pl.semaphore_signal(barrier, inc=1, device_id=peer, device_id_type=MESH)
    pl.semaphore_wait(barrier, len(peers))


def gather_orders(count):
    chip_bits = bits_of(count)[1:]
    return [chip_bits + [1], chip_bits[::-1] + [1]]


def last_bit(order, slot):
    return [bit for bit in order if slot & bit][-1]


def gather_rows(count, me, group, parts, source, target, send, recv, own=None):
    rows = target.shape[0] // count
    piece = rows // parts
    orders = gather_orders(count)
    copies = []

    def place(part, slot):
        return pl.multiple_of(flip(me, slot) * rows + part * piece, piece)

    def copy(part, slot, bit):
        there = target.at[pl.ds(place(part, slot), piece)]
        own_place = slot == 0 and source is not None
        origin = source.at[pl.ds(part * piece, piece)] if own_place else there
        number = part * count + (slot ^ bit)
        return pltpu.make_async_remote_copy(
            origin,
            there,
            send.at[number],
            recv.at[number],
            device_id=(flip(me, bit), group),
            device_id_type=MESH,
        )

    def keep(part):
        there = target.at[pl.ds(place(part, 0), piece)]
        return pltpu.make_async_copy(source.at[pl.ds(part * piece, piece)], there, own.at[part])

    def start(part):
        for bit in orders[part % 2]:
            item = copy(part, 0, bit)
            item.start()
            copies.append(item)
        if source is not None:
            keep(part).start()

    def wait(part, slot):
        there = target.at[pl.ds(place(part, slot), piece)]
        number = part * count + slot
        pltpu.make_async_remote_copy(
            there,
            there,
            send.at[number],
            recv.at[number],
            device_id=(flip(me, last_bit(orders[part % 2], slot)), group),
            device_id_type=MESH,
        ).wait_recv()

    def finish(arrived=None):
        waits = []
        for part in range(parts):
            order = orders[part % 2]
            for slot in range(1, count):
                last = order.index(last_bit(order, slot))
                waits.append((part // 2 + last, last, bin(slot).count("1"), part, slot))
        if arrived:
            for part in range(0, parts, 2):
                arrived(place(part, 0), 2 * piece)
        there = set()
        for _, last, _, part, slot in sorted(waits):
            wait(part, slot)
            for bit in orders[part % 2][last + 1 :]:
                item = copy(part, slot, bit)
                item.start()
                copies.append(item)
            there.add((part, slot))
            if arrived and (part ^ 1, slot) in there:
                arrived(place(part // 2 * 2, slot), 2 * piece)
        for part in range(parts):
            if source is not None:
                keep(part).wait()
        for item in copies:
            item.wait_send()

    return start, finish


def trade(count, me, group, pieces, source, target, send, recv):
    copies = []
    local = []
    for slot in list(range(1, count)) + [0]:
        peer = flip(me, slot)
        for number, (origin, place) in enumerate(pieces(peer, me)):
            total = len(pieces(peer, me))
            index = slot * total + number
            if slot == 0:
                item = pltpu.make_async_copy(source.at[origin], target.at[place], send.at[index])
                local.append(item)
            else:
                item = pltpu.make_async_remote_copy(
                    source.at[origin],
                    target.at[place],
                    send.at[index],
                    recv.at[index],
                    device_id=(peer, group),
                    device_id_type=MESH,
                )
                copies.append(item)
            item.start()

    def finish():
        for item in local:
            item.wait()
        for slot in range(1, count):
            peer = flip(me, slot)
            listed = pieces(me, peer)
            for number, (origin, place) in enumerate(listed):
                index = slot * len(listed) + number
                pltpu.make_async_remote_copy(
                    source.at[origin],
                    target.at[place],
                    send.at[index],
                    recv.at[index],
                    device_id=(peer, group),
                    device_id_type=MESH,
                ).wait_recv()
        for item in copies:
            item.wait_send()

    return finish


def span(start, width):
    return pl.ds(pl.multiple_of(start, HEAD), width)


def sharing(count):
    if count not in (KEY_VALUE_HEADS, QUERY_HEADS):
        raise ValueError(count)
    return count // KEY_VALUE_HEADS


def qkv_spans(count, device, gradients=False):
    own = QUERY_HEADS // count * HEAD
    repeat = sharing(count)
    queries = QUERY_HEADS * HEAD
    shared = lax.div(device, repeat) * HEAD
    if repeat == 2 and gradients:
        which = lax.rem(device, 2)
        return [
            (device * own, 0, own),
            (queries + which * (KEY_VALUE_HEADS * HEAD) + shared, own + which * HEAD, HEAD),
        ]
    return [
        (device * own, 0, own),
        (queries + shared, own, HEAD),
        (queries + KEY_VALUE_HEADS * HEAD + shared, own + HEAD, HEAD),
    ]


def mlp_spans(count, device, gradients=False):
    own = FF // count
    return [(device * own, 0, own), (FF + device * own, own, own)]


def outgoing(spans, count):
    def pieces(device, owner):
        return [
            ((slice(None), span(whole, width)), (owner, slice(None), pl.ds(part, width)))
            for whole, part, width in spans(count, device)
        ]

    return pieces


def incoming(spans, count):
    def pieces(device, owner):
        return [
            ((device, slice(None), span(part, width)), (slice(None), span(whole, width)))
            for whole, part, width in spans(count, owner, True)
        ]

    return pieces


def everyone(count, me, group):
    return [(flip(me, slot), group) for slot in range(1, count)]


def spread_kernel(count, qkv, mlp, qkv_parts, mlp_parts, send, recv, mlp_send, mlp_recv):
    me = lax.axis_index("ctx")
    group = lax.axis_index("fsdp")
    greet(everyone(count, me, group))
    finish = trade(count, me, group, outgoing(qkv_spans, count), qkv, qkv_parts, send, recv)
    finish_mlp = trade(count, me, group, outgoing(mlp_spans, count), mlp, mlp_parts, mlp_send, mlp_recv)
    finish()
    finish_mlp()


def spread(count, collective, qkv, mlp):
    rows = qkv.shape[0]
    width = QUERY_HEADS // count * HEAD + 2 * HEAD
    return pl.pallas_call(
        functools.partial(spread_kernel, count),
        out_shape=[
            jax.ShapeDtypeStruct((count, rows, width), BF16),
            jax.ShapeDtypeStruct((count, rows, 2 * FF // count), BF16),
        ],
        in_specs=[ANY, ANY],
        out_specs=[ANY, ANY],
        scratch_shapes=[DMA((3 * count,)), DMA((3 * count,)), DMA((2 * count,)), DMA((2 * count,))],
        compiler_params=pltpu.CompilerParams(collective_id=collective, has_side_effects=True),
        cost_estimate=cost(28),
    )(qkv, mlp)


def opening_kernel(count, normed, runs, rows, all_runs, send, recv, own, run_send, run_recv):
    me = lax.axis_index("ctx")
    group = lax.axis_index("fsdp")
    greet(everyone(count, me, group))
    finish_runs = trade(
        count, me, group, lambda device, owner: [((0,), (owner,))], runs, all_runs, run_send, run_recv
    )
    start, finish = gather_rows(count, me, group, 2, normed, rows, send, recv, own)
    start(0)
    start(1)
    finish()
    finish_runs()


def opening(count, collective, normed, runs):
    tokens, width = normed.shape
    return pl.pallas_call(
        functools.partial(opening_kernel, count),
        out_shape=[
            jax.ShapeDtypeStruct((count * tokens, width), BF16),
            jax.ShapeDtypeStruct((count, 8, 128), jnp.int32),
        ],
        in_specs=[VMEM, ANY],
        out_specs=[ANY, ANY],
        scratch_shapes=[DMA((2 * count,)), DMA((2 * count,)), DMA((2,)), DMA((count,)), DMA((count,))],
        compiler_params=pltpu.CompilerParams(collective_id=collective, has_side_effects=True),
        cost_estimate=cost(45),
    )(normed, runs)


def across(count, bit, values):
    return lax.ppermute(values, "ctx", [(index, index ^ bit) for index in range(count)])


def join_kernel(count, slots, *refs):
    blocks, (target, send, recv) = refs[:-3], refs[-3:]
    me = lax.axis_index("ctx")
    group = lax.axis_index("fsdp")
    other = flip(me, 1)
    greet([(other, group)])
    half = blocks[0].shape[1]
    items = []
    for block, (part, masks) in zip(blocks, slots):
        items += [(block, index, part, mask) for index, mask in enumerate(masks)]

    def place(number, owner):
        _, _, part, mask = items[number]
        return pl.ds(pl.multiple_of(flip(owner, mask) * 2 * half + part * half, half), half)

    def copy(number, owner):
        block, index = items[number][:2]
        return pltpu.make_async_remote_copy(
            block.at[index],
            target.at[place(number, owner)],
            send.at[number],
            recv.at[number],
            device_id=(other, group),
            device_id_type=MESH,
        )

    for number in range(len(items)):
        copy(number, me).start()
    for number in range(len(items)):
        block, index = items[number][:2]
        target[place(number, me), :] = block[index]
    for number in range(len(items)):
        copy(number, other).wait_recv()
    for number in range(len(items)):
        copy(number, me).wait_send()


def gather_step(count, masks, blocks, step):
    arrived, filled = [], []
    for part, order in enumerate(gather_orders(count)):
        arrived.append(across(count, order[step], blocks[part]))
        filled.append([mask ^ order[step] for mask in masks[part]])
    return arrived, filled


def gather_join(count, collective, masks, blocks, filled, arrived):
    slots = []
    for part in (0, 1):
        slots += [(part, masks[part]), (part, filled[part])]
    held = [block for pair in zip(blocks, arrived) for block in pair]
    half, width = held[0].shape[1:]
    return pl.pallas_call(
        functools.partial(join_kernel, count, slots),
        out_shape=jax.ShapeDtypeStruct((count * 2 * half, width), BF16),
        in_specs=[VMEM] * len(held),
        out_specs=VMEM,
        scratch_shapes=[DMA((count,)), DMA((count,))],
        compiler_params=pltpu.CompilerParams(
            collective_id=collective, has_side_effects=True, vmem_limit_bytes=VMEM_LIMIT
        ),
        cost_estimate=cost(13),
    )(*held)


def last_kernel(
    count,
    groups,
    values,
    parts,
    attn_gain,
    mlp_gain,
    q_gain,
    k_gain,
    d_qkv,
    columns,
    near,
    far,
    send,
    recv,
    far_send,
    far_recv,
    part_send,
    part_recv,
):
    me = lax.axis_index("ctx")
    group = lax.axis_index("fsdp")
    others = [lax.rem(group + step, groups) for step in range(1, groups)]
    greet(everyone(count, me, group) + [(me, other) for other in others])
    copies = []
    for slot in range(1, count):
        item = pltpu.make_async_remote_copy(
            values,
            near.at[me],
            send.at[slot],
            recv.at[slot],
            device_id=(flip(me, slot), group),
            device_id_type=MESH,
        )
        item.start()
        copies.append(item)
    finish = trade(count, me, group, incoming(qkv_spans, count), parts, columns, part_send, part_recv)
    near[me] = values[...]
    for item in copies:
        item.wait()
    summed = near[0]
    for index in range(1, count):
        summed = summed + near[index]
    far[group] = summed
    copies = []
    for step, other in enumerate(others):
        item = pltpu.make_async_remote_copy(
            far.at[group],
            far.at[group],
            far_send.at[step],
            far_recv.at[step],
            device_id=(me, other),
            device_id_type=MESH,
        )
        item.start()
        copies.append(item)
    for item in copies:
        item.wait()
    summed = far[0]
    for index in range(1, groups):
        summed = summed + far[index]
    rows = attn_gain.shape[0]
    attn_gain[...] = summed[:rows]
    mlp_gain[...] = summed[rows : 2 * rows]
    q_gain[...] = summed[2 * rows : 2 * rows + 1]
    k_gain[...] = summed[2 * rows + 1 : 2 * rows + 2]
    finish()
    d_qkv[...] = columns[...].astype(F32)


def last(count, groups, collective, values, parts, width, columns):
    shape = values.shape
    long, short = (width // 128, 128), (1, 128)
    pieces = len(qkv_spans(count, 0, True))
    return pl.pallas_call(
        functools.partial(last_kernel, count, groups),
        out_shape=[
            jax.ShapeDtypeStruct(size, F32)
            for size in (long, long, short, short, (parts.shape[1], columns))
        ],
        in_specs=[VMEM, ANY],
        out_specs=[VMEM] * 5,
        scratch_shapes=[
            pltpu.VMEM((parts.shape[1], columns), BF16),
            pltpu.VMEM((count,) + shape, F32),
            pltpu.VMEM((groups,) + shape, F32),
            DMA((count,)),
            DMA((count,)),
            DMA((groups,)),
            DMA((groups,)),
            DMA((pieces * count,)),
            DMA((pieces * count,)),
        ],
        compiler_params=pltpu.CompilerParams(collective_id=collective, has_side_effects=True),
        cost_estimate=cost(14),
    )(values, parts)


def product_scatter(
    count, me, group, parts, flipped, left, right, done, kept, near_out, near_in, far_out, far_in, ns, nr, fs, fr
):
    rows, width = kept.shape
    piece = rows // parts
    bits = bits_of(count)
    orders = [bits[1:][::-1], bits[1:]]
    tile = min(512, width)
    pairs = list(range(count // 2))[::-1]

    def product(slot, store):
        start = pl.multiple_of(flip(me, slot) * rows, rows)
        block = left[pl.ds(start, rows), :]

        def step(index, carry):
            columns = pl.ds(pl.multiple_of(index * tile, tile), tile)
            if flipped:
                value = nt(block, right[columns, :])
            else:
                value = jnp.dot(block, right[:, columns], preferred_element_type=F32)
            store(columns, value)
            return carry

        lax.fori_loop(0, width // tile, step, 0)

    def first(part, slot):
        return [bit for bit in orders[part % 2] if slot & bit][0]

    def near(pair):
        return pltpu.make_async_remote_copy(
            near_out.at[pair],
            near_in.at[pair],
            ns.at[pair],
            nr.at[pair],
            device_id=(flip(me, 1), group),
            device_id_type=MESH,
        )

    def number(part, pair):
        return part * (count // 2 - 1) + pair - 1

    def far(part, pair):
        index = number(part, pair)
        return pltpu.make_async_remote_copy(
            far_out.at[index],
            far_in.at[index],
            fs.at[index],
            fr.at[index],
            device_id=(flip(me, first(part, 2 * pair)), group),
            device_id_type=MESH,
        )

    def needs(part, pair):
        found = []
        for bit in orders[part % 2]:
            if 2 * pair & bit:
                break
            found.append((2 * pair ^ bit) // 2)
        return found

    def settle(part, pair):
        if pair == 0:
            value = kept[pl.ds(part * piece, piece), :]
        else:
            value = far_out[number(part, pair)].astype(F32)
        for other in needs(part, pair):
            far(part, other).wait_recv()
            value = value + far_in[number(part, other)].astype(F32)
        if pair == 0:
            done(part, value)
        else:
            far_out[number(part, pair)] = value.astype(BF16)
            far(part, pair).start()

    def send_near(pair):
        def store(columns, value):
            near_out[pair, :, columns] = value.astype(BF16)

        product(2 * pair + 1, store)
        near(pair).start()

    def batch_parts(batch):
        return (2 * batch, 2 * batch + 1)

    def send_pair(batch, pair):
        for part in batch_parts(batch):
            if pair and not needs(part, pair):
                far(part, pair).start()

    def sum_near(pair):
        near(pair).wait_recv()

        def store(columns, value):
            value = value + near_in[pair, :, columns].astype(F32)
            if pair == 0:
                kept[:, columns] = value
            else:
                for part in range(parts):
                    far_out[number(part, pair), :, columns] = value[
                        part * piece : (part + 1) * piece
                    ].astype(BF16)

        product(2 * pair, store)
        send_pair(0, pair)

    def begin():
        send_near(pairs[0])
        for pair in pairs:
            if pair:
                send_near(pair - 1)
            sum_near(pair)

    def send(batch):
        for pair in pairs:
            send_pair(batch, pair)

    def pass_on(batch):
        for pair in pairs:
            for part in batch_parts(batch):
                if pair and needs(part, pair):
                    settle(part, pair)

    def end(batch):
        for part in batch_parts(batch):
            settle(part, 0)

    def close():
        for pair in pairs:
            near(pair).wait_send()
            for part in range(parts):
                if pair:
                    far(part, pair).wait_send()

    return begin, send, pass_on, end, close


def scatter_scratch(count, rows, width, parts=2):
    pairs = count // 2
    links = parts * (pairs - 1)
    return [
        pltpu.VMEM((rows, width), F32),
        pltpu.VMEM((pairs, rows, width), BF16),
        pltpu.VMEM((pairs, rows, width), BF16),
        pltpu.VMEM((links, rows // parts, width), BF16),
        pltpu.VMEM((links, rows // parts, width), BF16),
        DMA((pairs,)),
        DMA((pairs,)),
        DMA((links,)),
        DMA((links,)),
    ]


SCATTER = 9
PARTS = 4
BACK_PARTS = 2


def comm_params(collective):
    return pltpu.CompilerParams(
        collective_id=collective, has_side_effects=True, vmem_limit_bytes=VMEM_LIMIT
    )


def row_blocks(first, count, step):
    def body(index, carry):
        step(pl.multiple_of(first + index * 32, 32), pl.multiple_of(index * 32, 32))
        return carry

    lax.fori_loop(0, count // 32, body, 0)


def norm_back(values, gain, grad):
    scale = lax.rsqrt(jnp.mean(values * values, axis=-1, keepdims=True) + EPS)
    scaled = values * scale
    pushed = grad * gain
    back = scale * (pushed - scaled * jnp.mean(pushed * scaled, axis=-1, keepdims=True))
    return back, jnp.sum(grad * scaled, axis=0, keepdims=True)


def norm_rows(values, gain):
    return values * lax.rsqrt(jnp.mean(values * values, axis=-1, keepdims=True) + EPS) * gain


def middle_kernel(count, left, right, hidden, gain, middle, gathered, own_rows, sums, *scratch):
    me = lax.axis_index("ctx")
    group = lax.axis_index("fsdp")
    piece = middle.shape[0] // PARTS
    greet([(flip(me, bit), group) for bit in bits_of(count)])
    start, finish = gather_rows(count, me, group, PARTS, own_rows, gathered, *scratch[SCATTER:])

    def done(part, value):
        sums[...] = value

        def step(row, place):
            total_rows = hidden[pl.ds(row, 32), :].astype(F32) + sums[pl.ds(place, 32), :]
            middle[pl.ds(row, 32), :] = total_rows
            own_rows[pl.ds(row, 32), :] = norm_rows(total_rows, gain[...]).astype(BF16)

        row_blocks(part * piece, piece, step)
        start(part)

    begin, send, pass_on, end, close = product_scatter(
        count, me, group, PARTS, False, left, right, done, *scratch[:SCATTER]
    )
    begin()
    pass_on(0)
    send(1)
    end(0)
    pass_on(1)
    end(1)
    finish()
    close()


def gather_scratch(count, parts):
    return [DMA((parts * count,)), DMA((parts * count,)), DMA((parts,))]


def middle_and_second(count, collective, left, right, hidden, gain):
    rows, width = hidden.shape
    return pl.pallas_call(
        functools.partial(middle_kernel, count),
        out_shape=[
            jax.ShapeDtypeStruct((rows, width), F32),
            jax.ShapeDtypeStruct((count * rows, width), BF16),
        ],
        in_specs=[VMEM] * 4,
        out_specs=[VMEM, ANY],
        scratch_shapes=[pltpu.VMEM((rows, width), BF16), pltpu.VMEM((rows // PARTS, width), F32)]
        + scatter_scratch(count, rows, width, PARTS)
        + gather_scratch(count, PARTS),
        compiler_params=comm_params(collective),
        cost_estimate=cost(80),
    )(left, right, hidden, gain)


def back_kernel(
    count,
    left,
    right,
    middle,
    cotangent,
    gain,
    attended,
    out_weight,
    d_middle,
    d_gain,
    d_attended,
    d_out,
    sums,
    gathered,
    turned,
    out_sum,
    *scratch,
):
    me = lax.axis_index("ctx")
    group = lax.axis_index("fsdp")
    piece = middle.shape[0] // BACK_PARTS
    own = me * middle.shape[0]
    greet([(flip(me, bit), group) for bit in bits_of(count)])
    start, finish = gather_rows(count, me, group, BACK_PARTS, None, gathered, *scratch[SCATTER:])
    d_gain[...] = jnp.zeros_like(d_gain)

    def done(part, value):
        sums[...] = value

        def step(row, place):
            span_rows = pl.ds(row, 32)
            back, gain_part = norm_back(middle[span_rows, :], gain[...], sums[pl.ds(place, 32), :])
            back = back + cotangent[span_rows, :].astype(F32)
            d_middle[span_rows, :] = back
            gathered[pl.ds(pl.multiple_of(own + row, 32), 32), :] = back.astype(BF16)
            d_gain[...] += gain_part

        row_blocks(part * piece, piece, step)
        start(part)

    begin, _, pass_on, end, close = product_scatter(
        count, me, group, BACK_PARTS, True, left, right, done, *scratch[:SCATTER]
    )
    begin()
    out_sum[...] = jnp.zeros_like(out_sum)

    def turn(index, carry):
        span_rows = pl.ds(pl.multiple_of(index * 256, 256), 256)
        turned[:, span_rows] = attended[span_rows, :].astype(F32).T.astype(BF16)
        return carry

    lax.fori_loop(0, attended.shape[0] // 256, turn, 0)
    pass_on(0)
    end(0)

    def arrived(row, size):
        block = gathered[pl.ds(row, size), :]
        d_attended[pl.ds(row, size), :] = nt(block, out_weight[...]).astype(BF16)
        if size % 128 == 0:
            out_sum[...] += jnp.dot(turned[:, pl.ds(row, size)], block, preferred_element_type=F32)

    finish(arrived)
    close()
    if 2 * piece % 128:
        out_sum[...] = jnp.dot(turned[...], gathered[...], preferred_element_type=F32)
    d_out[...] = out_sum[...].astype(BF16)


def back_through_middle(count, collective, left, right, middle, cotangent, gain, attended, out_weight):
    rows, width = middle.shape
    tokens, wide = attended.shape
    shape = jax.ShapeDtypeStruct
    return pl.pallas_call(
        functools.partial(back_kernel, count),
        out_shape=[
            shape((rows, width), F32),
            shape((1, width), F32),
            shape((tokens, wide), BF16),
            shape((wide, width), BF16),
        ],
        in_specs=[VMEM] * 7,
        out_specs=[VMEM] * 4,
        scratch_shapes=[
            pltpu.VMEM((rows // BACK_PARTS, width), F32),
            pltpu.VMEM((tokens, width), BF16),
            pltpu.VMEM((wide, tokens), BF16),
            pltpu.VMEM((wide, width), F32),
        ]
        + scatter_scratch(count, rows, width, BACK_PARTS)
        + gather_scratch(count, BACK_PARTS)[:2],
        compiler_params=comm_params(collective),
        cost_estimate=cost(85),
    )(left, right, middle, cotangent, gain, attended, out_weight)


def input_kernel(
    count, left, right, hidden, d_middle, gain, parts, d_hidden, d_gain, d_gate_up, columns, sums, send, recv, *scratch
):
    me = lax.axis_index("ctx")
    group = lax.axis_index("fsdp")
    half = hidden.shape[0] // 2
    greet(everyone(count, me, group))
    finish = trade(count, me, group, incoming(mlp_spans, count), parts, columns, send, recv)
    d_gain[...] = jnp.zeros_like(d_gain)

    def done(part, value):
        sums[...] = value

        def step(row, place):
            span_rows = pl.ds(row, 32)
            values = hidden[span_rows, :].astype(F32)
            back, gain_part = norm_back(values, gain[...], sums[pl.ds(place, 32), :])
            d_hidden[span_rows, :] = d_middle[span_rows, :] + back
            d_gain[...] += gain_part

        row_blocks(part * half, half, step)

    begin, _, pass_on, end, close = product_scatter(
        count, me, group, 2, True, left, right, done, *scratch
    )
    begin()
    pass_on(0)
    end(0)
    finish()
    close()
    d_gate_up[...] = columns[...].astype(F32)


def back_to_input(count, collective, left, right, hidden, d_middle, gain, parts):
    rows, width = hidden.shape
    shape = jax.ShapeDtypeStruct
    return pl.pallas_call(
        functools.partial(input_kernel, count),
        out_shape=[
            shape((rows, width), F32),
            shape((1, width), F32),
            shape((parts.shape[1], 2 * FF), F32),
        ],
        in_specs=[VMEM] * 5 + [ANY],
        out_specs=[VMEM] * 3,
        scratch_shapes=[
            pltpu.VMEM((parts.shape[1], 2 * FF), BF16),
            pltpu.VMEM((rows // 2, width), F32),
            DMA((2 * count,)),
            DMA((2 * count,)),
        ]
        + scatter_scratch(count, rows, width),
        compiler_params=comm_params(collective),
        cost_estimate=cost(60),
    )(left, right, hidden, d_middle, gain, parts)


def mlp_kernel(
    count,
    groups,
    activated,
    weight,
    middle,
    upstream,
    both,
    second,
    output,
    d_both,
    parts,
    up_slots,
    both_slots,
    second_slots,
    part_slots,
    up_in,
    both_in,
    second_in,
    parts_out,
    *scratch,
):
    me = lax.axis_index("ctx")
    group = lax.axis_index("fsdp")
    half = middle.shape[0] // 2
    tokens, own = activated.shape
    block = up_slots.shape[1]
    columns = second_slots.shape[2]
    greet([(flip(me, bit), group) for bit in bits_of(count)])

    def rows_in(index):
        slot = lax.rem(index, 2)
        rows = pl.ds(pl.multiple_of(index * block, block), block)
        return (
            pltpu.make_async_copy(upstream.at[rows], up_slots.at[slot], up_in.at[slot]),
            pltpu.make_async_copy(both.at[rows], both_slots.at[slot], both_in.at[slot]),
        )

    def second_copy(index):
        slot = lax.rem(index, 2)
        span_columns = pl.ds(pl.multiple_of(index * columns, columns), columns)
        return pltpu.make_async_copy(second.at[:, span_columns], second_slots.at[slot], second_in.at[slot])

    def part_copies(index):
        slot = lax.rem(index, 2)
        rows = columns // groups
        return [
            pltpu.make_async_copy(
                part_slots.at[slot, pl.ds(owner * rows, rows)],
                parts.at[owner, index],
                parts_out.at[slot, owner],
            )
            for owner in range(groups)
        ]

    for item in rows_in(0):
        item.start()
    second_copy(0).start()

    def done(part, value):
        span_rows = pl.ds(part * half, half)
        output[span_rows, :] = (middle[span_rows, :] + value).astype(BF16)

    begin, _, pass_on, end, close = product_scatter(
        count, me, group, 2, False, activated, weight, done, *scratch
    )
    begin()
    steps = tokens // block

    def activation(index, carry):
        @pl.when(index + 1 < steps)
        def _():
            for item in rows_in(index + 1):
                item.start()

        for item in rows_in(index):
            item.wait()
        slot = lax.rem(index, 2)
        rows = pl.ds(pl.multiple_of(index * block, block), block)
        grad = nt(up_slots[slot], weight[...]).astype(BF16).astype(F32)
        gate = both_slots[slot, :, :own]
        up = both_slots[slot, :, own:]
        sigmoid = 1.0 / (1.0 + jnp.exp(-gate))
        d_both[rows, :own] = (grad * up * sigmoid * (1.0 + gate * (1.0 - sigmoid))).astype(BF16)
        d_both[rows, own:] = (grad * gate * sigmoid).astype(BF16)
        return carry

    lax.fori_loop(0, steps, activation, 0)

    def weight_grad(index, carry):
        @pl.when(index + 1 < count)
        def _():
            second_copy(index + 1).start()

        second_copy(index).wait()

        @pl.when(index >= 2)
        def _():
            for item in part_copies(index - 2):
                item.wait()

        slot = lax.rem(index, 2)
        value = lax.dot_general(
            second_slots[slot], d_both[...], (((0,), (0,)), ((), ())), preferred_element_type=F32
        )
        part_slots[slot] = value.astype(BF16)
        for item in part_copies(index):
            item.start()
        return carry

    lax.fori_loop(0, count // 2, weight_grad, 0)
    pass_on(0)
    lax.fori_loop(count // 2, count, weight_grad, 0)
    for index in (count - 2, count - 1):
        for item in part_copies(index):
            item.wait()
    end(0)
    close()


def back_through_mlp(count, groups, collective, activated, weight, middle, upstream, both, second):
    rows, width = middle.shape
    tokens, own = activated.shape
    block = 256
    columns = width // count
    shape = jax.ShapeDtypeStruct
    return pl.pallas_call(
        functools.partial(mlp_kernel, count, groups),
        out_shape=[
            shape((rows, width), BF16),
            shape((tokens, 2 * own), BF16),
            shape((groups, count, columns // groups, 2 * own), BF16),
        ],
        in_specs=[VMEM] * 3 + [ANY] * 3,
        out_specs=[VMEM, VMEM, ANY],
        scratch_shapes=[
            pltpu.VMEM((2, block, width), BF16),
            pltpu.VMEM((2, block, 2 * own), F32),
            pltpu.VMEM((2, tokens, columns), BF16),
            pltpu.VMEM((2, columns, 2 * own), BF16),
            DMA((2,)),
            DMA((2,)),
            DMA((2,)),
            DMA((2, groups)),
        ]
        + scatter_scratch(count, rows, width),
        compiler_params=comm_params(collective),
        cost_estimate=cost(48),
    )(activated, weight, middle, upstream, both, second)


def swap_halves(value):
    return jnp.concatenate([value[:, HEAD // 2 :], value[:, : HEAD // 2]], axis=1)


def nt(left, right):
    return lax.dot_general(left, right, (((1,), (1,)), ((), ())), preferred_element_type=F32)


def causal(keys, queries):
    key = lax.broadcasted_iota(jnp.int32, (keys, queries), 0)
    query = lax.rem(lax.broadcasted_iota(jnp.int32, (keys, queries), 1), CONT)
    return key <= query


def attention_kernel(
    heads, runs, joined, cosine, sine, q_gain, k_gain, attended, raw, queries, keys, values, mixed, lse, turned, placed
):
    tokens = joined.shape[0]
    blocks = tokens // CONT
    wide = heads * CONT

    def sort(run, carry):
        origin = pl.multiple_of(run * RUN, RUN)
        place = pl.multiple_of(runs[run] * RUN, RUN)
        raw[pl.ds(place, RUN), :] = joined[pl.ds(origin, RUN), :]
        return carry

    lax.fori_loop(0, tokens // RUN, sort, 0)

    def prepare(block, carry):
        span_rows = pl.ds(pl.multiple_of(block * CONT, CONT), CONT)
        cos_rows = cosine[span_rows, :]
        sin_rows = sine[span_rows, :]

        def turn(value, gain):
            value = value * lax.rsqrt(jnp.mean(value * value, axis=-1, keepdims=True) + EPS) * gain
            return (value * cos_rows + swap_halves(value) * sin_rows).astype(BF16)

        for head in range(heads):
            piece = raw[span_rows, head * HEAD : (head + 1) * HEAD]
            queries[block, head * CONT : (head + 1) * CONT, :] = turn(piece, q_gain[...])
        keys[span_rows, :] = turn(raw[span_rows, wide : wide + HEAD], k_gain[...])
        piece = raw[span_rows, wide + HEAD : wide + 2 * HEAD]
        values[span_rows, :] = piece.astype(BF16)
        turned[:, span_rows] = piece.T.astype(BF16)
        return carry

    lax.fori_loop(0, blocks, prepare, 0)

    def attend(block, own, before):
        query = queries[block]
        own_rows = pl.ds(own, CONT)
        weight = jnp.exp2(nt(keys[own_rows, :], query) * SCALE2)
        weight = jnp.where(causal(CONT, wide), weight, 0.0)
        sums = jnp.sum(weight, axis=0, keepdims=True)
        out = jnp.dot(turned[:, own_rows], weight.astype(BF16), preferred_element_type=F32)
        if before:
            weight = jnp.exp2(nt(keys[:before, :], query) * SCALE2)
            sums = sums + jnp.sum(weight, axis=0, keepdims=True)
            out = out + jnp.dot(turned[:, :before], weight.astype(BF16), preferred_element_type=F32)
        out = out / sums
        mixed[block] = out
        lse[block] = jnp.broadcast_to(jnp.log2(sums), (8, wide))
        for head in range(heads):
            placed[own_rows, head * HEAD : (head + 1) * HEAD] = out[
                :, head * CONT : (head + 1) * CONT
            ].T.astype(BF16)

    for block in range(PROMPT // CONT):
        attend(block, block * CONT, block * CONT)

    def continuation(block, carry):
        attend(block, pl.multiple_of(block * CONT, CONT), PROMPT)
        return carry

    lax.fori_loop(PROMPT // CONT, blocks, continuation, 0)

    def unsort(run, carry):
        origin = pl.multiple_of(run * RUN, RUN)
        place = pl.multiple_of(runs[run] * RUN, RUN)
        attended[pl.ds(origin, RUN), :] = placed[pl.ds(place, RUN), :]
        return carry

    lax.fori_loop(0, tokens // RUN, unsort, 0)


def attention(heads, runs, joined, cosine, sine, q_gain, k_gain):
    tokens = joined.shape[0]
    blocks = tokens // CONT
    wide = heads * CONT
    shape = jax.ShapeDtypeStruct
    return pl.pallas_call(
        functools.partial(attention_kernel, heads),
        out_shape=[
            shape((tokens, wide), BF16),
            shape(joined.shape, F32),
            shape((blocks, wide, HEAD), BF16),
            shape((tokens, HEAD), BF16),
            shape((tokens, HEAD), BF16),
            shape((blocks, HEAD, wide), F32),
            shape((blocks, 8, wide), F32),
        ],
        in_specs=[SMEM, VMEM, VMEM, VMEM, VMEM, VMEM],
        out_specs=[VMEM] * 7,
        scratch_shapes=[pltpu.VMEM((HEAD, tokens), BF16), pltpu.VMEM((tokens, wide), BF16)],
        compiler_params=pltpu.CompilerParams(vmem_limit_bytes=VMEM_LIMIT),
        cost_estimate=cost(15),
    )(runs, joined, cosine, sine, q_gain, k_gain)


def attention_back_kernel(
    heads, runs, d_attended, queries, keys, values, mixed, lse, d_queries, d_keys, d_values, arrived, keys_turned
):
    tokens = keys.shape[0]
    blocks = tokens // CONT
    wide = heads * CONT

    def sort(run, carry):
        origin = pl.multiple_of(run * RUN, RUN)
        place = pl.multiple_of(runs[run] * RUN, RUN)
        arrived[pl.ds(place, RUN), :] = d_attended[pl.ds(origin, RUN), :]
        return carry

    lax.fori_loop(0, tokens // RUN, sort, 0)
    d_keys[...] = jnp.zeros_like(d_keys)
    d_values[...] = jnp.zeros_like(d_values)

    def turn(block, carry):
        span_rows = pl.ds(pl.multiple_of(block * CONT, CONT), CONT)
        keys_turned[:, span_rows] = keys[span_rows, :].astype(F32).T.astype(BF16)
        return carry

    lax.fori_loop(0, blocks, turn, 0)

    def back(block, own, before):
        query = queries[block]
        own_rows = pl.ds(own, CONT)
        grad = jnp.concatenate(
            [arrived[own_rows, head * HEAD : (head + 1) * HEAD] for head in range(heads)], axis=0
        )
        grad_turned = grad.astype(F32).T
        delta = jnp.sum(grad_turned * mixed[block], axis=0, keepdims=True)
        total_row = lse[block][:1, :]

        def part(rows, count, masked):
            prob = jnp.exp2(nt(keys[rows, :], query) * SCALE2 - total_row)
            if masked:
                prob = jnp.where(causal(count, wide), prob, 0.0)
            score = (prob * (nt(values[rows, :], grad) - delta)).astype(BF16)
            d_values[rows, :] += jnp.dot(prob.astype(BF16), grad, preferred_element_type=F32)
            d_keys[rows, :] += jnp.dot(score, query, preferred_element_type=F32)
            return jnp.dot(keys_turned[:, rows], score, preferred_element_type=F32)

        result = part(own_rows, CONT, True)
        if before:
            result = result + part(slice(0, before), before, False)
        result = result * SCALE
        for head in range(heads):
            d_queries[own_rows, head * HEAD : (head + 1) * HEAD] = result[
                :, head * CONT : (head + 1) * CONT
            ].T.astype(BF16)

    for block in range(PROMPT // CONT):
        back(block, block * CONT, block * CONT)

    def continuation(block, carry):
        back(block, pl.multiple_of(block * CONT, CONT), PROMPT)
        return carry

    lax.fori_loop(PROMPT // CONT, blocks, continuation, 0)


def attention_back(heads, runs, d_attended, queries, keys, values, mixed, lse):
    tokens = keys.shape[0]
    wide = heads * CONT
    shape = jax.ShapeDtypeStruct
    return pl.pallas_call(
        functools.partial(attention_back_kernel, heads),
        out_shape=[shape((tokens, wide), BF16), shape((tokens, HEAD), F32), shape((tokens, HEAD), F32)],
        in_specs=[SMEM] + [VMEM] * 6,
        out_specs=[VMEM] * 3,
        scratch_shapes=[pltpu.VMEM((tokens, wide), BF16), pltpu.VMEM((HEAD, tokens), BF16)],
        compiler_params=pltpu.CompilerParams(vmem_limit_bytes=VMEM_LIMIT),
        cost_estimate=cost(25),
    )(runs, d_attended, queries, keys, values, mixed, lse)


def joined_back_kernel(
    heads, runs, raw, d_queries, d_keys, d_values, cosine, sine, q_gain, k_gain, share, d_joined, d_q_gain, d_k_gain, placed
):
    tokens = raw.shape[0]
    blocks = tokens // CONT
    wide = heads * CONT
    d_q_gain[...] = jnp.zeros_like(d_q_gain)
    d_k_gain[...] = jnp.zeros_like(d_k_gain)

    def step(block, carry):
        span_rows = pl.ds(pl.multiple_of(block * CONT, CONT), CONT)
        cos_rows = cosine[span_rows, :]
        sin_rows = sine[span_rows, :]

        def pull(value, grad, gain):
            grad = grad * cos_rows - swap_halves(grad) * sin_rows
            scale = lax.rsqrt(jnp.mean(value * value, axis=-1, keepdims=True) + EPS)
            scaled = value * scale
            gain_grad = jnp.sum(grad * scaled, axis=0, keepdims=True)
            grad = grad * gain
            return scale * (grad - scaled * jnp.mean(grad * scaled, axis=-1, keepdims=True)), gain_grad

        for head in range(heads):
            columns = slice(head * HEAD, (head + 1) * HEAD)
            grad, gain_grad = pull(
                raw[span_rows, columns], d_queries[span_rows, columns].astype(F32), q_gain[...]
            )
            placed[span_rows, columns] = grad.astype(BF16)
            d_q_gain[...] += gain_grad
        key_part, value_part = share[:1, :], share[1:, :]
        grad, gain_grad = pull(
            raw[span_rows, wide : wide + HEAD],
            (d_keys[span_rows, :] * SCALE).astype(BF16).astype(F32),
            k_gain[...],
        )
        placed[span_rows, wide : wide + HEAD] = (grad * key_part).astype(BF16)
        d_k_gain[...] += gain_grad * key_part
        placed[span_rows, wide + HEAD : wide + 2 * HEAD] = (d_values[span_rows, :] * value_part).astype(BF16)
        return carry

    lax.fori_loop(0, blocks, step, 0)

    def unsort(run, carry):
        origin = pl.multiple_of(run * RUN, RUN)
        place = pl.multiple_of(runs[run] * RUN, RUN)
        d_joined[pl.ds(origin, RUN), :] = placed[pl.ds(place, RUN), :]
        return carry

    lax.fori_loop(0, tokens // RUN, unsort, 0)


def attention_and_joined_back_kernel(
    heads,
    runs,
    d_attended,
    queries,
    keys,
    values,
    mixed,
    lse,
    raw,
    cosine,
    sine,
    q_gain,
    k_gain,
    share,
    d_joined,
    d_q_gain,
    d_k_gain,
    d_queries,
    d_keys,
    d_values,
    arrived,
    keys_turned,
    raw_here,
    cosine_here,
    sine_here,
    placed,
    loaded,
):
    loads = [
        pltpu.make_async_copy(source, target, loaded.at[index])
        for index, (source, target) in enumerate(
            [(raw, raw_here), (cosine, cosine_here), (sine, sine_here)]
        )
    ]
    for item in loads:
        item.start()
    attention_back_kernel(
        heads, runs, d_attended, queries, keys, values, mixed, lse, d_queries, d_keys, d_values, arrived, keys_turned
    )
    for item in loads:
        item.wait()
    joined_back_kernel(
        heads,
        runs,
        raw_here,
        d_queries,
        d_keys,
        d_values,
        cosine_here,
        sine_here,
        q_gain,
        k_gain,
        share,
        d_joined,
        d_q_gain,
        d_k_gain,
        placed,
    )


def attention_and_joined_back(
    heads, runs, d_attended, queries, keys, values, mixed, lse, raw, cosine, sine, q_gain, k_gain, share
):
    tokens = keys.shape[0]
    wide = heads * CONT
    shape = jax.ShapeDtypeStruct
    return pl.pallas_call(
        functools.partial(attention_and_joined_back_kernel, heads),
        out_shape=[shape(raw.shape, BF16), shape((1, HEAD), F32), shape((1, HEAD), F32)],
        in_specs=[SMEM] + [VMEM] * 6 + [ANY] * 3 + [VMEM] * 3,
        out_specs=[VMEM] * 3,
        scratch_shapes=[
            pltpu.VMEM((tokens, wide), BF16),
            pltpu.VMEM((tokens, HEAD), F32),
            pltpu.VMEM((tokens, HEAD), F32),
            pltpu.VMEM((tokens, wide), BF16),
            pltpu.VMEM((HEAD, tokens), BF16),
            pltpu.VMEM(raw.shape, F32),
            pltpu.VMEM(cosine.shape, F32),
            pltpu.VMEM(sine.shape, F32),
            pltpu.VMEM(raw.shape, BF16),
            DMA((3,)),
        ],
        compiler_params=pltpu.CompilerParams(vmem_limit_bytes=VMEM_LIMIT),
        cost_estimate=cost(30),
    )(runs, d_attended, queries, keys, values, mixed, lse, raw, cosine, sine, q_gain, k_gain, share)


def joined_back(heads, runs, raw, d_queries, d_keys, d_values, cosine, sine, q_gain, k_gain, share):
    shape = jax.ShapeDtypeStruct
    return pl.pallas_call(
        functools.partial(joined_back_kernel, heads),
        out_shape=[shape(raw.shape, BF16), shape((1, HEAD), F32), shape((1, HEAD), F32)],
        in_specs=[SMEM] + [VMEM] * 9,
        out_specs=[VMEM] * 3,
        scratch_shapes=[pltpu.VMEM(raw.shape, BF16)],
        compiler_params=pltpu.CompilerParams(vmem_limit_bytes=VMEM_LIMIT),
        cost_estimate=cost(8),
    )(runs, raw, d_queries, d_keys, d_values, cosine, sine, q_gain, k_gain, share)


def rotary(tokens):
    index = np.arange(tokens)
    place = np.where(index < PROMPT, index, PROMPT + (index - PROMPT) % CONT).astype(np.float32)
    exponent = np.arange(HEAD // 2, dtype=np.float32) * np.float32(2.0 / HEAD)
    inverse = np.power(np.float32(ROPE_BASE), -exponent).astype(np.float32)
    angles = place[:, None] * inverse[None, :]
    cosine, sine = np.cos(angles), np.sin(angles)
    tables = np.concatenate([cosine, cosine], axis=1), np.concatenate([-sine, sine], axis=1)
    return tuple(jnp.asarray(table, F32) for table in tables)


def body(
    count,
    groups,
    hidden_in,
    segment_ids,
    positions,
    attn_gain,
    qkv_weight,
    query_norm_gain,
    k_gain,
    out_weight,
    mlp_gain,
    gate_up,
    down_weight,
    cotangent,
):
    hidden = hidden_in[0].astype(F32)
    rows, width = hidden.shape
    tokens = rows * count
    heads = QUERY_HEADS // count
    repeat = sharing(count)

    first = segment_ids[0, ::RUN]
    place = positions[0, ::RUN]
    order = jnp.where(first == 0, place, place + (first - 1) * CONT) // RUN
    runs = jnp.zeros((1, 8, 128), jnp.int32).at[0, 0, : rows // RUN].set(order)

    def gather_groups(values, axis):
        return lax.all_gather(values, "fsdp", axis=axis, tiled=True)

    def scatter_groups(values):
        return lax.psum_scatter(values, "fsdp", scatter_dimension=0, tiled=True)

    w_out = gather_groups(out_weight, 0)
    qkv_parts, mlp_parts = spread(count, 1, qkv_weight, gate_up)
    qkv_parts, w_out = lax.optimization_barrier((qkv_parts, w_out))
    w_qkv = gather_groups(qkv_parts, 1).reshape(width, -1)
    normed_local = norm_rows(hidden, attn_gain).astype(BF16)
    normed_local, qkv_parts = lax.optimization_barrier((normed_local, qkv_parts))
    normed, all_runs = opening(count, 2, normed_local, runs)
    mlp_parts, w_qkv, normed, upstream = lax.optimization_barrier((mlp_parts, w_qkv, normed, cotangent[0]))
    w_gu = gather_groups(mlp_parts, 1).reshape(width, -1)
    w_down = gather_groups(down_weight, 0)
    run_order = all_runs[:, 0, : rows // RUN].reshape(-1)
    cosine, sine = rotary(tokens)
    q_gain_row = query_norm_gain[None, :]
    k_gain_row = k_gain[None, :]

    blocks, masks = [upstream[None, : rows // 2], upstream[None, rows // 2 :]], [[0], [0]]
    chip_steps = len(bits_of(count)) - 1
    for step in range(chip_steps - 1):
        arrived, filled = gather_step(count, masks, blocks, step)
        if step == 0:
            joined = jnp.dot(normed, w_qkv, preferred_element_type=F32)
            joined, arrived = lax.optimization_barrier((joined, arrived))
        blocks = [jnp.concatenate(pair) for pair in zip(blocks, arrived)]
        masks = [held + more for held, more in zip(masks, filled)]
    arrived, filled = gather_step(count, masks, blocks, chip_steps - 1)
    attended, raw, queries, keys, values, mixed, lse = attention(
        heads, run_order, joined, cosine, sine, q_gain_row, k_gain_row
    )
    attended, arrived = lax.optimization_barrier((attended, arrived))
    middle, second = middle_and_second(count, 3, attended, w_out, hidden_in[0], mlp_gain[None, :])
    both = jnp.dot(second, w_gu, preferred_element_type=F32)
    own = both.shape[1] // 2
    gate, up = both[:, :own], both[:, own:]
    activated = (gate * jax.nn.sigmoid(gate) * up).astype(BF16)

    activated, arrived = lax.optimization_barrier((activated, arrived))
    upstream = gather_join(count, 5, masks, blocks, filled, arrived)
    d_down = jnp.dot(activated.T, upstream, preferred_element_type=F32).astype(BF16)
    d_down, upstream = lax.optimization_barrier((d_down, upstream))
    d_down = scatter_groups(d_down)
    output, d_both, gu_parts = back_through_mlp(
        count, groups, 9, activated, w_down, middle, upstream, both, second
    )
    gu_parts, d_both = lax.optimization_barrier((gu_parts, d_both))
    gu_parts = scatter_groups(gu_parts.reshape((groups * count,) + gu_parts.shape[2:]))

    def weight_grad(left, right):
        grad = lax.dot_general(left, right, (((0,), (0,)), ((), ())), preferred_element_type=F32)
        grad = grad.astype(BF16).reshape(count, groups, -1, right.shape[1])
        return grad.transpose(1, 0, 2, 3).reshape(groups * count, -1, right.shape[1])

    d_middle, mlp_gain_grad, d_attended, d_out = back_through_middle(
        count, 6, d_both, w_gu, middle, cotangent[0], mlp_gain[None, :], attended, w_out
    )
    d_attended, d_down = lax.optimization_barrier((d_attended, d_down))
    share = jnp.ones((2, HEAD), F32)
    tables = (cosine, sine, q_gain_row, k_gain_row)
    if repeat == 1:
        d_joined, q_gain_grad, k_gain_grad = attention_and_joined_back(
            heads, run_order, d_attended, queries, keys, values, mixed, lse, raw, *tables, share
        )
    else:
        d_queries, d_keys, d_values = attention_back(
            heads, run_order, d_attended, queries, keys, values, mixed, lse
        )
        d_keys = d_keys + across(count, 1, d_keys)
        d_values = d_values + across(count, 1, d_values)
        mine = lax.rem(lax.axis_index("ctx"), 2) == jnp.arange(2)
        share = share * mine[:, None].astype(F32)
        d_joined, q_gain_grad, k_gain_grad = joined_back(
            heads, run_order, raw, d_queries, d_keys, d_values, *tables, share
        )
    normed, d_joined, gu_parts = lax.optimization_barrier((normed, d_joined, gu_parts))
    qkv_grad_parts, d_joined = lax.optimization_barrier((weight_grad(normed, d_joined), d_joined))
    d_out, gu_parts = lax.optimization_barrier((d_out, gu_parts))
    d_out = scatter_groups(d_out)
    qkv_grad_parts = scatter_groups(qkv_grad_parts)
    d_hidden, attn_gain_grad, d_gate_up = back_to_input(
        count, 8, d_joined, w_qkv, hidden_in[0], d_middle, attn_gain[None, :], gu_parts
    )
    d_hidden, qkv_grad_parts = lax.optimization_barrier((d_hidden, qkv_grad_parts))

    small = jnp.concatenate([attn_gain_grad[0], mlp_gain_grad[0], q_gain_grad[0], k_gain_grad[0]])
    padded = -(-small.shape[0] // 1024) * 1024
    small = jnp.pad(small, (0, padded - small.shape[0])).reshape(-1, 128)
    gains = last(count, groups, 11, small, qkv_grad_parts, width, qkv_weight.shape[1])
    attn_gain_sum, mlp_gain_sum, q_gain_sum, k_gain_sum, d_qkv = gains
    return (
        output[None],
        d_hidden[None],
        attn_gain_sum.reshape(-1),
        d_qkv,
        q_gain_sum.reshape(-1),
        k_gain_sum.reshape(-1),
        d_out.astype(F32),
        mlp_gain_sum.reshape(-1),
        d_gate_up,
        d_down.astype(F32),
    )


def solution(mesh):
    return jax.shard_map(
        functools.partial(body, mesh.shape["ctx"], mesh.shape["fsdp"]),
        mesh=mesh,
        in_specs=(
            P("fsdp", "ctx", None),
            P("fsdp", "ctx"),
            P("fsdp", "ctx"),
            P(),
            P(("ctx", "fsdp"), None),
            P(),
            P(),
            P(("ctx", "fsdp"), None),
            P(),
            P(("ctx", "fsdp"), None),
            P(("ctx", "fsdp"), None),
            P("fsdp", "ctx", None),
        ),
        out_specs=(
            P("fsdp", "ctx", None),
            P("fsdp", "ctx", None),
            P(),
            P(("ctx", "fsdp"), None),
            P(),
            P(),
            P(("ctx", "fsdp"), None),
            P(),
            P(("ctx", "fsdp"), None),
            P(("ctx", "fsdp"), None),
        ),
        check_vma=False,
    )
```

```python
import functools
import math

import jax
import jax.numpy as jnp
import numpy as np
from jax import lax
from jax.experimental import pallas as pl
from jax.experimental.pallas import tpu as pltpu
from jax.sharding import PartitionSpec as P

QUERY_HEADS = 16
KEY_VALUE_HEADS = 8
HEAD = 128
FF = 6144
PROMPT = 1024
CONT = 128
RUN = 32
EPS = 1e-06
ROPE_BASE = 1000000.0
SCALE = HEAD ** (-0.5)
SCALE2 = SCALE * math.log2(math.e)
MESH = pl.DeviceIdType.MESH
ANY = pl.BlockSpec(memory_space=pl.ANY)
VMEM = pl.BlockSpec(memory_space=pltpu.VMEM)
SMEM = pl.BlockSpec(memory_space=pltpu.SMEM)
BF16 = jnp.bfloat16
F32 = jnp.float32
DMA = pltpu.SemaphoreType.DMA
VMEM_LIMIT = 60 * 2**20


def cost(us):
    return pl.CostEstimate(flops=0, bytes_accessed=int(us * 1e6), transcendentals=0)


def flip(me, mask):
    result = me
    bit = 1
    while bit <= mask:
        if mask & bit:
            result = result + bit - 2 * bit * lax.rem(lax.div(me, bit), 2)
        bit *= 2
    return result


def bits_of(count):
    bits = []
    bit = 1
    while bit < count:
        bits.append(bit)
        bit *= 2
    return bits


def greet(peers):
    barrier = pltpu.get_barrier_semaphore()
    for peer in peers:
        pl.semaphore_signal(barrier, inc=1, device_id=peer, device_id_type=MESH)
    pl.semaphore_wait(barrier, len(peers))


def gather_orders(count):
    chip_bits = bits_of(count)[1:]
    return [chip_bits + [1], chip_bits[::-1] + [1]]


def last_bit(order, slot):
    return [bit for bit in order if slot & bit][-1]


def gather_rows(count, me, group, parts, source, target, send, recv, own=None):
    rows = target.shape[0] // count
    piece = rows // parts
    orders = gather_orders(count)
    copies = []

    def place(part, slot):
        return pl.multiple_of(flip(me, slot) * rows + part * piece, piece)

    def copy(part, slot, bit):
        there = target.at[pl.ds(place(part, slot), piece)]
        own_place = slot == 0 and source is not None
        origin = source.at[pl.ds(part * piece, piece)] if own_place else there
        number = part * count + (slot ^ bit)
        return pltpu.make_async_remote_copy(
            origin,
            there,
            send.at[number],
            recv.at[number],
            device_id=(flip(me, bit), group),
            device_id_type=MESH,
        )

    def keep(part):
        there = target.at[pl.ds(place(part, 0), piece)]
        return pltpu.make_async_copy(source.at[pl.ds(part * piece, piece)], there, own.at[part])

    def start(part):
        for bit in orders[part % 2]:
            item = copy(part, 0, bit)
            item.start()
            copies.append(item)
        if source is not None:
            keep(part).start()

    def wait(part, slot):
        there = target.at[pl.ds(place(part, slot), piece)]
        number = part * count + slot
        pltpu.make_async_remote_copy(
            there,
            there,
            send.at[number],
            recv.at[number],
            device_id=(flip(me, last_bit(orders[part % 2], slot)), group),
            device_id_type=MESH,
        ).wait_recv()

    def finish(arrived=None):
        waits = []
        for part in range(parts):
            order = orders[part % 2]
            for slot in range(1, count):
                last = order.index(last_bit(order, slot))
                waits.append((part // 2 + last, last, bin(slot).count("1"), part, slot))
        if arrived:
            for part in range(0, parts, 2):
                arrived(place(part, 0), 2 * piece)
        there = set()
        for _, last, _, part, slot in sorted(waits):
            wait(part, slot)
            for bit in orders[part % 2][last + 1 :]:
                item = copy(part, slot, bit)
                item.start()
                copies.append(item)
            there.add((part, slot))
            if arrived and (part ^ 1, slot) in there:
                arrived(place(part // 2 * 2, slot), 2 * piece)
        for part in range(parts):
            if source is not None:
                keep(part).wait()
        for item in copies:
            item.wait_send()

    return start, finish


def trade(count, me, group, pieces, source, target, send, recv):
    copies = []
    local = []
    for slot in list(range(1, count)) + [0]:
        peer = flip(me, slot)
        for number, (origin, place) in enumerate(pieces(peer, me)):
            total = len(pieces(peer, me))
            index = slot * total + number
            if slot == 0:
                item = pltpu.make_async_copy(source.at[origin], target.at[place], send.at[index])
                local.append(item)
            else:
                item = pltpu.make_async_remote_copy(
                    source.at[origin],
                    target.at[place],
                    send.at[index],
                    recv.at[index],
                    device_id=(peer, group),
                    device_id_type=MESH,
                )
                copies.append(item)
            item.start()

    def finish():
        for item in local:
            item.wait()
        for slot in range(1, count):
            peer = flip(me, slot)
            listed = pieces(me, peer)
            for number, (origin, place) in enumerate(listed):
                index = slot * len(listed) + number
                pltpu.make_async_remote_copy(
                    source.at[origin],
                    target.at[place],
                    send.at[index],
                    recv.at[index],
                    device_id=(peer, group),
                    device_id_type=MESH,
                ).wait_recv()
        for item in copies:
            item.wait_send()

    return finish


def span(start, width):
    return pl.ds(pl.multiple_of(start, HEAD), width)


def sharing(count):
    if count not in (KEY_VALUE_HEADS, QUERY_HEADS):
        raise ValueError(count)
    return count // KEY_VALUE_HEADS


def qkv_spans(count, device, gradients=False):
    own = QUERY_HEADS // count * HEAD
    repeat = sharing(count)
    queries = QUERY_HEADS * HEAD
    shared = lax.div(device, repeat) * HEAD
    if repeat == 2 and gradients:
        which = lax.rem(device, 2)
        return [
            (device * own, 0, own),
            (queries + which * (KEY_VALUE_HEADS * HEAD) + shared, own + which * HEAD, HEAD),
        ]
    return [
        (device * own, 0, own),
        (queries + shared, own, HEAD),
        (queries + KEY_VALUE_HEADS * HEAD + shared, own + HEAD, HEAD),
    ]


def mlp_spans(count, device, gradients=False):
    own = FF // count
    return [(device * own, 0, own), (FF + device * own, own, own)]


def outgoing(spans, count):
    def pieces(device, owner):
        return [
            ((slice(None), span(whole, width)), (owner, slice(None), pl.ds(part, width)))
            for whole, part, width in spans(count, device)
        ]

    return pieces


def incoming(spans, count):
    def pieces(device, owner):
        return [
            ((device, slice(None), span(part, width)), (slice(None), span(whole, width)))
            for whole, part, width in spans(count, owner, True)
        ]

    return pieces


def everyone(count, me, group):
    return [(flip(me, slot), group) for slot in range(1, count)]


def spread_kernel(count, qkv, mlp, qkv_parts, mlp_parts, send, recv, mlp_send, mlp_recv):
    me = lax.axis_index("ctx")
    group = lax.axis_index("fsdp")
    greet(everyone(count, me, group))
    finish = trade(count, me, group, outgoing(qkv_spans, count), qkv, qkv_parts, send, recv)
    finish_mlp = trade(count, me, group, outgoing(mlp_spans, count), mlp, mlp_parts, mlp_send, mlp_recv)
    finish()
    finish_mlp()


def spread(count, collective, qkv, mlp):
    rows = qkv.shape[0]
    width = QUERY_HEADS // count * HEAD + 2 * HEAD
    return pl.pallas_call(
        functools.partial(spread_kernel, count),
        out_shape=[
            jax.ShapeDtypeStruct((count, rows, width), BF16),
            jax.ShapeDtypeStruct((count, rows, 2 * FF // count), BF16),
        ],
        in_specs=[ANY, ANY],
        out_specs=[ANY, ANY],
        scratch_shapes=[DMA((3 * count,)), DMA((3 * count,)), DMA((2 * count,)), DMA((2 * count,))],
        compiler_params=pltpu.CompilerParams(collective_id=collective, has_side_effects=True),
        cost_estimate=cost(28),
    )(qkv, mlp)


def opening_kernel(count, normed, runs, rows, all_runs, send, recv, own, run_send, run_recv):
    me = lax.axis_index("ctx")
    group = lax.axis_index("fsdp")
    greet(everyone(count, me, group))
    finish_runs = trade(
        count, me, group, lambda device, owner: [((0,), (owner,))], runs, all_runs, run_send, run_recv
    )
    start, finish = gather_rows(count, me, group, 2, normed, rows, send, recv, own)
    start(0)
    start(1)
    finish()
    finish_runs()


def opening(count, collective, normed, runs):
    tokens, width = normed.shape
    return pl.pallas_call(
        functools.partial(opening_kernel, count),
        out_shape=[
            jax.ShapeDtypeStruct((count * tokens, width), BF16),
            jax.ShapeDtypeStruct((count, 8, 128), jnp.int32),
        ],
        in_specs=[VMEM, ANY],
        out_specs=[ANY, ANY],
        scratch_shapes=[DMA((2 * count,)), DMA((2 * count,)), DMA((2,)), DMA((count,)), DMA((count,))],
        compiler_params=pltpu.CompilerParams(collective_id=collective, has_side_effects=True),
        cost_estimate=cost(45),
    )(normed, runs)


def across(count, bit, values):
    return lax.ppermute(values, "ctx", [(index, index ^ bit) for index in range(count)])


def join_kernel(count, slots, *refs):
    blocks, (target, send, recv) = refs[:-3], refs[-3:]
    me = lax.axis_index("ctx")
    group = lax.axis_index("fsdp")
    other = flip(me, 1)
    greet([(other, group)])
    half = blocks[0].shape[1]
    items = []
    for block, (part, masks) in zip(blocks, slots):
        items += [(block, index, part, mask) for index, mask in enumerate(masks)]

    def place(number, owner):
        _, _, part, mask = items[number]
        return pl.ds(pl.multiple_of(flip(owner, mask) * 2 * half + part * half, half), half)

    def copy(number, owner):
        block, index = items[number][:2]
        return pltpu.make_async_remote_copy(
            block.at[index],
            target.at[place(number, owner)],
            send.at[number],
            recv.at[number],
            device_id=(other, group),
            device_id_type=MESH,
        )

    for number in range(len(items)):
        copy(number, me).start()
    for number in range(len(items)):
        block, index = items[number][:2]
        target[place(number, me), :] = block[index]
    for number in range(len(items)):
        copy(number, other).wait_recv()
    for number in range(len(items)):
        copy(number, me).wait_send()


def gather_step(count, masks, blocks, step):
    arrived, filled = [], []
    for part, order in enumerate(gather_orders(count)):
        arrived.append(across(count, order[step], blocks[part]))
        filled.append([mask ^ order[step] for mask in masks[part]])
    return arrived, filled


def gather_join(count, collective, masks, blocks, filled, arrived):
    slots = []
    for part in (0, 1):
        slots += [(part, masks[part]), (part, filled[part])]
    held = [block for pair in zip(blocks, arrived) for block in pair]
    half, width = held[0].shape[1:]
    return pl.pallas_call(
        functools.partial(join_kernel, count, slots),
        out_shape=jax.ShapeDtypeStruct((count * 2 * half, width), BF16),
        in_specs=[VMEM] * len(held),
        out_specs=VMEM,
        scratch_shapes=[DMA((count,)), DMA((count,))],
        compiler_params=pltpu.CompilerParams(
            collective_id=collective, has_side_effects=True, vmem_limit_bytes=VMEM_LIMIT
        ),
        cost_estimate=cost(13),
    )(*held)


def last_kernel(
    count,
    groups,
    values,
    parts,
    attn_gain,
    mlp_gain,
    q_gain,
    k_gain,
    d_qkv,
    columns,
    near,
    far,
    send,
    recv,
    far_send,
    far_recv,
    part_send,
    part_recv,
):
    me = lax.axis_index("ctx")
    group = lax.axis_index("fsdp")
    others = [lax.rem(group + step, groups) for step in range(1, groups)]
    greet(everyone(count, me, group) + [(me, other) for other in others])
    copies = []
    for slot in range(1, count):
        item = pltpu.make_async_remote_copy(
            values,
            near.at[me],
            send.at[slot],
            recv.at[slot],
            device_id=(flip(me, slot), group),
            device_id_type=MESH,
        )
        item.start()
        copies.append(item)
    finish = trade(count, me, group, incoming(qkv_spans, count), parts, columns, part_send, part_recv)
    near[me] = values[...]
    for item in copies:
        item.wait()
    summed = near[0]
    for index in range(1, count):
        summed = summed + near[index]
    far[group] = summed
    copies = []
    for step, other in enumerate(others):
        item = pltpu.make_async_remote_copy(
            far.at[group],
            far.at[group],
            far_send.at[step],
            far_recv.at[step],
            device_id=(me, other),
            device_id_type=MESH,
        )
        item.start()
        copies.append(item)
    for item in copies:
        item.wait()
    summed = far[0]
    for index in range(1, groups):
        summed = summed + far[index]
    rows = attn_gain.shape[0]
    attn_gain[...] = summed[:rows]
    mlp_gain[...] = summed[rows : 2 * rows]
    q_gain[...] = summed[2 * rows : 2 * rows + 1]
    k_gain[...] = summed[2 * rows + 1 : 2 * rows + 2]
    finish()
    d_qkv[...] = columns[...].astype(F32)


def last(count, groups, collective, values, parts, width, columns):
    shape = values.shape
    long, short = (width // 128, 128), (1, 128)
    pieces = len(qkv_spans(count, 0, True))
    return pl.pallas_call(
        functools.partial(last_kernel, count, groups),
        out_shape=[
            jax.ShapeDtypeStruct(size, F32)
            for size in (long, long, short, short, (parts.shape[1], columns))
        ],
        in_specs=[VMEM, ANY],
        out_specs=[VMEM] * 5,
        scratch_shapes=[
            pltpu.VMEM((parts.shape[1], columns), BF16),
            pltpu.VMEM((count,) + shape, F32),
            pltpu.VMEM((groups,) + shape, F32),
            DMA((count,)),
            DMA((count,)),
            DMA((groups,)),
            DMA((groups,)),
            DMA((pieces * count,)),
            DMA((pieces * count,)),
        ],
        compiler_params=pltpu.CompilerParams(collective_id=collective, has_side_effects=True),
        cost_estimate=cost(14),
    )(values, parts)


def product_slots(count):
    slots = []
    for pair in range(count // 2)[::-1]:
        slots += [2 * pair - 1, 2 * pair] if slots and pair else [2 * pair + 1, 2 * pair - 1, 2 * pair] if pair else [0]
    return slots


def load_operands(count, me, flipped, left_from, right_from, left, right, left_in, right_in):
    rows = left.shape[0] // count
    width = right.shape[0] if flipped else right.shape[1]
    tile = min(512, width)

    def left_copy(slot):
        span_rows = pl.ds(pl.multiple_of(flip(me, slot) * rows, rows), rows)
        return pltpu.make_async_copy(left_from.at[span_rows], left.at[span_rows], left_in.at[slot])

    def right_copy(index):
        span_tile = pl.ds(pl.multiple_of(index * tile, tile), tile)
        place = (span_tile,) if flipped else (slice(None), span_tile)
        return pltpu.make_async_copy(right_from.at[place], right.at[place], right_in.at[index])

    slots = product_slots(count)
    right_copy(0).start()
    left_copy(slots[0]).start()
    for index in range(1, width // tile):
        right_copy(index).start()
    for slot in slots[1:]:
        left_copy(slot).start()
    return lambda slot: left_copy(slot).wait(), lambda index: right_copy(index).wait()


def operand_scratch(count, left, right, flipped):
    width = right.shape[0] if flipped else right.shape[1]
    return [
        pltpu.VMEM(left.shape, BF16),
        pltpu.VMEM(right.shape, BF16),
        DMA((count,)),
        DMA((width // min(512, width),)),
    ]


def fetch(sources, targets, arrived):
    items = [
        pltpu.make_async_copy(source, target, arrived.at[index])
        for index, (source, target) in enumerate(zip(sources, targets))
    ]
    for item in items:
        item.start()

    def wait():
        for item in items:
            item.wait()

    return wait


def product_scatter(
    count,
    me,
    group,
    parts,
    flipped,
    left,
    right,
    done,
    kept,
    near_out,
    near_in,
    far_out,
    far_in,
    ns,
    nr,
    fs,
    fr,
    ready=None,
):
    rows, width = kept.shape
    piece = rows // parts
    bits = bits_of(count)
    orders = [bits[1:][::-1], bits[1:]]
    tile = min(512, width)
    pairs = list(range(count // 2))[::-1]

    def product(slot, store):
        start = pl.multiple_of(flip(me, slot) * rows, rows)
        if ready:
            ready[0](slot)
        block = left[pl.ds(start, rows), :]

        def step(index, carry):
            columns = pl.ds(pl.multiple_of(index * tile, tile), tile)
            if ready and slot == count - 1:
                ready[1](index)
            if flipped:
                value = nt(block, right[columns, :])
            else:
                value = jnp.dot(block, right[:, columns], preferred_element_type=F32)
            store(columns, value)
            return carry

        lax.fori_loop(0, width // tile, step, 0)

    def first(part, slot):
        return [bit for bit in orders[part % 2] if slot & bit][0]

    def near(pair):
        return pltpu.make_async_remote_copy(
            near_out.at[pair],
            near_in.at[pair],
            ns.at[pair],
            nr.at[pair],
            device_id=(flip(me, 1), group),
            device_id_type=MESH,
        )

    def number(part, pair):
        return part * (count // 2 - 1) + pair - 1

    def far(part, pair):
        index = number(part, pair)
        return pltpu.make_async_remote_copy(
            far_out.at[index],
            far_in.at[index],
            fs.at[index],
            fr.at[index],
            device_id=(flip(me, first(part, 2 * pair)), group),
            device_id_type=MESH,
        )

    def needs(part, pair):
        found = []
        for bit in orders[part % 2]:
            if 2 * pair & bit:
                break
            found.append((2 * pair ^ bit) // 2)
        return found

    def settle(part, pair):
        if pair == 0:
            value = kept[pl.ds(part * piece, piece), :]
        else:
            value = far_out[number(part, pair)].astype(F32)
        for other in needs(part, pair):
            far(part, other).wait_recv()
            value = value + far_in[number(part, other)].astype(F32)
        if pair == 0:
            done(part, value)
        else:
            far_out[number(part, pair)] = value.astype(BF16)
            far(part, pair).start()

    def send_near(pair):
        def store(columns, value):
            near_out[pair, :, columns] = value.astype(BF16)

        product(2 * pair + 1, store)
        near(pair).start()

    def batch_parts(batch):
        return (2 * batch, 2 * batch + 1)

    def send_pair(batch, pair):
        for part in batch_parts(batch):
            if pair and not needs(part, pair):
                far(part, pair).start()

    def sum_near(pair):
        near(pair).wait_recv()

        def store(columns, value):
            value = value + near_in[pair, :, columns].astype(F32)
            if pair == 0:
                kept[:, columns] = value
            else:
                for part in range(parts):
                    far_out[number(part, pair), :, columns] = value[
                        part * piece : (part + 1) * piece
                    ].astype(BF16)

        product(2 * pair, store)
        send_pair(0, pair)

    def begin():
        send_near(pairs[0])
        for pair in pairs:
            if pair:
                send_near(pair - 1)
            sum_near(pair)

    def send(batch):
        for pair in pairs:
            send_pair(batch, pair)

    def pass_on(batch):
        for pair in pairs:
            for part in batch_parts(batch):
                if pair and needs(part, pair):
                    settle(part, pair)

    def end(batch):
        for part in batch_parts(batch):
            settle(part, 0)

    def close():
        for pair in pairs:
            near(pair).wait_send()
            for part in range(parts):
                if pair:
                    far(part, pair).wait_send()

    return begin, send, pass_on, end, close


def scatter_scratch(count, rows, width, parts=2):
    pairs = count // 2
    links = parts * (pairs - 1)
    return [
        pltpu.VMEM((rows, width), F32),
        pltpu.VMEM((pairs, rows, width), BF16),
        pltpu.VMEM((pairs, rows, width), BF16),
        pltpu.VMEM((links, rows // parts, width), BF16),
        pltpu.VMEM((links, rows // parts, width), BF16),
        DMA((pairs,)),
        DMA((pairs,)),
        DMA((links,)),
        DMA((links,)),
    ]


SCATTER = 9
PARTS = 4
BACK_PARTS = 2


def comm_params(collective):
    return pltpu.CompilerParams(
        collective_id=collective, has_side_effects=True, vmem_limit_bytes=VMEM_LIMIT
    )


def row_blocks(first, count, step):
    def body(index, carry):
        step(pl.multiple_of(first + index * 32, 32), pl.multiple_of(index * 32, 32))
        return carry

    lax.fori_loop(0, count // 32, body, 0)


def norm_back(values, gain, grad):
    scale = lax.rsqrt(jnp.mean(values * values, axis=-1, keepdims=True) + EPS)
    scaled = values * scale
    pushed = grad * gain
    back = scale * (pushed - scaled * jnp.mean(pushed * scaled, axis=-1, keepdims=True))
    return back, jnp.sum(grad * scaled, axis=0, keepdims=True)


def norm_rows(values, gain):
    return values * lax.rsqrt(jnp.mean(values * values, axis=-1, keepdims=True) + EPS) * gain


def middle_kernel(count, left, right, hidden, gain, middle, gathered, own_rows, sums, *scratch):
    me = lax.axis_index("ctx")
    group = lax.axis_index("fsdp")
    piece = middle.shape[0] // PARTS
    greet([(flip(me, bit), group) for bit in bits_of(count)])
    start, finish = gather_rows(count, me, group, PARTS, own_rows, gathered, *scratch[SCATTER:])

    def done(part, value):
        sums[...] = value

        def step(row, place):
            total_rows = hidden[pl.ds(row, 32), :].astype(F32) + sums[pl.ds(place, 32), :]
            middle[pl.ds(row, 32), :] = total_rows
            own_rows[pl.ds(row, 32), :] = norm_rows(total_rows, gain[...]).astype(BF16)

        row_blocks(part * piece, piece, step)
        start(part)

    begin, send, pass_on, end, close = product_scatter(
        count, me, group, PARTS, False, left, right, done, *scratch[:SCATTER]
    )
    begin()
    pass_on(0)
    send(1)
    end(0)
    pass_on(1)
    end(1)
    finish()
    close()


def gather_scratch(count, parts):
    return [DMA((parts * count,)), DMA((parts * count,)), DMA((parts,))]


def middle_and_second(count, collective, left, right, hidden, gain):
    rows, width = hidden.shape
    return pl.pallas_call(
        functools.partial(middle_kernel, count),
        out_shape=[
            jax.ShapeDtypeStruct((rows, width), F32),
            jax.ShapeDtypeStruct((count * rows, width), BF16),
        ],
        in_specs=[VMEM] * 4,
        out_specs=[VMEM, ANY],
        scratch_shapes=[pltpu.VMEM((rows, width), BF16), pltpu.VMEM((rows // PARTS, width), F32)]
        + scatter_scratch(count, rows, width, PARTS)
        + gather_scratch(count, PARTS),
        compiler_params=comm_params(collective),
        cost_estimate=cost(80),
    )(left, right, hidden, gain)


def back_kernel(
    count,
    left_from,
    right_from,
    middle_from,
    cotangent_from,
    gain,
    attended_from,
    out_weight_from,
    d_middle,
    d_gain,
    d_attended,
    d_out,
    sums,
    gathered,
    turned,
    out_sum,
    left,
    right,
    left_in,
    right_in,
    middle,
    cotangent,
    attended,
    out_weight,
    others_in,
    *scratch,
):
    me = lax.axis_index("ctx")
    group = lax.axis_index("fsdp")
    piece = middle.shape[0] // BACK_PARTS
    own = me * middle.shape[0]
    ready = load_operands(count, me, True, left_from, right_from, left, right, left_in, right_in)
    fetched = fetch(
        (middle_from, cotangent_from, attended_from, out_weight_from),
        (middle, cotangent, attended, out_weight),
        others_in,
    )
    greet([(flip(me, bit), group) for bit in bits_of(count)])
    start, finish = gather_rows(count, me, group, BACK_PARTS, None, gathered, *scratch[SCATTER:])
    d_gain[...] = jnp.zeros_like(d_gain)

    def done(part, value):
        sums[...] = value

        def step(row, place):
            span_rows = pl.ds(row, 32)
            back, gain_part = norm_back(middle[span_rows, :], gain[...], sums[pl.ds(place, 32), :])
            back = back + cotangent[span_rows, :].astype(F32)
            d_middle[span_rows, :] = back
            gathered[pl.ds(pl.multiple_of(own + row, 32), 32), :] = back.astype(BF16)
            d_gain[...] += gain_part

        row_blocks(part * piece, piece, step)
        start(part)

    begin, _, pass_on, end, close = product_scatter(
        count, me, group, BACK_PARTS, True, left, right, done, *scratch[:SCATTER], ready=ready
    )
    begin()
    fetched()
    out_sum[...] = jnp.zeros_like(out_sum)

    def turn(index, carry):
        span_rows = pl.ds(pl.multiple_of(index * 256, 256), 256)
        turned[:, span_rows] = attended[span_rows, :].astype(F32).T.astype(BF16)
        return carry

    lax.fori_loop(0, attended.shape[0] // 256, turn, 0)
    pass_on(0)
    end(0)

    def arrived(row, size):
        block = gathered[pl.ds(row, size), :]
        d_attended[pl.ds(row, size), :] = nt(block, out_weight[...]).astype(BF16)
        if size % 128 == 0:
            out_sum[...] += jnp.dot(turned[:, pl.ds(row, size)], block, preferred_element_type=F32)

    finish(arrived)
    close()
    if 2 * piece % 128:
        out_sum[...] = jnp.dot(turned[...], gathered[...], preferred_element_type=F32)
    d_out[...] = out_sum[...].astype(BF16)


def back_through_middle(count, collective, left, right, middle, cotangent, gain, attended, out_weight):
    rows, width = middle.shape
    tokens, wide = attended.shape
    shape = jax.ShapeDtypeStruct
    return pl.pallas_call(
        functools.partial(back_kernel, count),
        out_shape=[
            shape((rows, width), F32),
            shape((1, width), F32),
            shape((tokens, wide), BF16),
            shape((wide, width), BF16),
        ],
        in_specs=[ANY] * 4 + [VMEM] + [ANY] * 2,
        out_specs=[VMEM] * 4,
        scratch_shapes=[
            pltpu.VMEM((rows // BACK_PARTS, width), F32),
            pltpu.VMEM((tokens, width), BF16),
            pltpu.VMEM((wide, tokens), BF16),
            pltpu.VMEM((wide, width), F32),
        ]
        + operand_scratch(count, left, right, True)
        + [
            pltpu.VMEM((rows, width), F32),
            pltpu.VMEM((rows, width), BF16),
            pltpu.VMEM((tokens, wide), BF16),
            pltpu.VMEM((wide, width), BF16),
            DMA((4,)),
        ]
        + scatter_scratch(count, rows, width, BACK_PARTS)
        + gather_scratch(count, BACK_PARTS)[:2],
        compiler_params=comm_params(collective),
        cost_estimate=cost(85),
    )(left, right, middle, cotangent, gain, attended, out_weight)


def input_kernel(
    count, left, right, hidden, d_middle, gain, parts, d_hidden, d_gain, d_gate_up, columns, sums, send, recv, *scratch
):
    me = lax.axis_index("ctx")
    group = lax.axis_index("fsdp")
    half = hidden.shape[0] // 2
    greet(everyone(count, me, group))
    finish = trade(count, me, group, incoming(mlp_spans, count), parts, columns, send, recv)
    d_gain[...] = jnp.zeros_like(d_gain)

    def done(part, value):
        sums[...] = value

        def step(row, place):
            span_rows = pl.ds(row, 32)
            values = hidden[span_rows, :].astype(F32)
            back, gain_part = norm_back(values, gain[...], sums[pl.ds(place, 32), :])
            d_hidden[span_rows, :] = d_middle[span_rows, :] + back
            d_gain[...] += gain_part

        row_blocks(part * half, half, step)

    begin, _, pass_on, end, close = product_scatter(
        count, me, group, 2, True, left, right, done, *scratch
    )
    begin()
    pass_on(0)
    end(0)
    finish()
    close()
    d_gate_up[...] = columns[...].astype(F32)


def back_to_input(count, collective, left, right, hidden, d_middle, gain, parts):
    rows, width = hidden.shape
    shape = jax.ShapeDtypeStruct
    return pl.pallas_call(
        functools.partial(input_kernel, count),
        out_shape=[
            shape((rows, width), F32),
            shape((1, width), F32),
            shape((parts.shape[1], 2 * FF), F32),
        ],
        in_specs=[VMEM] * 5 + [ANY],
        out_specs=[VMEM] * 3,
        scratch_shapes=[
            pltpu.VMEM((parts.shape[1], 2 * FF), BF16),
            pltpu.VMEM((rows // 2, width), F32),
            DMA((2 * count,)),
            DMA((2 * count,)),
        ]
        + scatter_scratch(count, rows, width),
        compiler_params=comm_params(collective),
        cost_estimate=cost(60),
    )(left, right, hidden, d_middle, gain, parts)


def mlp_kernel(
    count,
    groups,
    activated_from,
    weight_from,
    middle_from,
    upstream,
    both,
    second,
    output,
    d_both,
    parts,
    up_slots,
    both_slots,
    second_slots,
    part_slots,
    up_in,
    both_in,
    second_in,
    parts_out,
    activated,
    weight,
    activated_in,
    weight_in,
    middle,
    others_in,
    *scratch,
):
    me = lax.axis_index("ctx")
    group = lax.axis_index("fsdp")
    half = middle.shape[0] // 2
    tokens, own = activated.shape
    block = up_slots.shape[1]
    columns = second_slots.shape[2]
    ready = load_operands(
        count, me, False, activated_from, weight_from, activated, weight, activated_in, weight_in
    )
    fetched = fetch((middle_from,), (middle,), others_in)
    greet([(flip(me, bit), group) for bit in bits_of(count)])

    def rows_in(index):
        slot = lax.rem(index, 4)
        rows = pl.ds(pl.multiple_of(index * block, block), block)
        return (
            pltpu.make_async_copy(upstream.at[rows], up_slots.at[slot], up_in.at[slot]),
            pltpu.make_async_copy(both.at[rows], both_slots.at[slot], both_in.at[slot]),
        )

    def second_copy(index):
        slot = lax.rem(index, 2)
        span_columns = pl.ds(pl.multiple_of(index * columns, columns), columns)
        return pltpu.make_async_copy(second.at[:, span_columns], second_slots.at[slot], second_in.at[slot])

    def part_copies(index):
        slot = lax.rem(index, 2)
        rows = columns // groups
        return [
            pltpu.make_async_copy(
                part_slots.at[slot, pl.ds(owner * rows, rows)],
                parts.at[owner, index],
                parts_out.at[slot, owner],
            )
            for owner in range(groups)
        ]

    for item in rows_in(0) + rows_in(1):
        item.start()
    second_copy(0).start()

    def done(part, value):
        span_rows = pl.ds(part * half, half)
        output[span_rows, :] = (middle[span_rows, :] + value).astype(BF16)

    begin, _, pass_on, end, close = product_scatter(
        count, me, group, 2, False, activated, weight, done, *scratch, ready=ready
    )
    begin()
    fetched()
    steps = tokens // block

    def activation(index, carry):
        @pl.when(2 * index + 2 < steps)
        def _():
            for item in rows_in(2 * index + 2) + rows_in(2 * index + 3):
                item.start()

        for item in rows_in(2 * index) + rows_in(2 * index + 1):
            item.wait()
        slots = [lax.rem(2 * index + turn, 4) for turn in (0, 1)]
        grads = [nt(up_slots[slot], weight[...]).astype(BF16).astype(F32) for slot in slots]
        for turn, (slot, grad) in enumerate(zip(slots, grads)):
            rows = pl.ds(pl.multiple_of((2 * index + turn) * block, block), block)
            gate = both_slots[slot, :, :own]
            up = both_slots[slot, :, own:]
            sigmoid = 1.0 / (1.0 + jnp.exp(-gate))
            d_both[rows, :own] = (grad * up * sigmoid * (1.0 + gate * (1.0 - sigmoid))).astype(BF16)
            d_both[rows, own:] = (grad * gate * sigmoid).astype(BF16)
        return carry

    lax.fori_loop(0, steps // 2, activation, 0)

    def weight_grad(index, carry):
        @pl.when(index + 1 < count)
        def _():
            second_copy(index + 1).start()

        second_copy(index).wait()

        @pl.when(index >= 2)
        def _():
            for item in part_copies(index - 2):
                item.wait()

        slot = lax.rem(index, 2)
        value = lax.dot_general(
            second_slots[slot], d_both[...], (((0,), (0,)), ((), ())), preferred_element_type=F32
        )
        part_slots[slot] = value.astype(BF16)
        for item in part_copies(index):
            item.start()
        return carry

    lax.fori_loop(0, count // 2, weight_grad, 0)
    pass_on(0)
    lax.fori_loop(count // 2, count, weight_grad, 0)
    for index in (count - 2, count - 1):
        for item in part_copies(index):
            item.wait()
    end(0)
    close()


def back_through_mlp(count, groups, collective, activated, weight, middle, upstream, both, second):
    rows, width = middle.shape
    tokens, own = activated.shape
    block = 256
    columns = width // count
    shape = jax.ShapeDtypeStruct
    return pl.pallas_call(
        functools.partial(mlp_kernel, count, groups),
        out_shape=[
            shape((rows, width), BF16),
            shape((tokens, 2 * own), BF16),
            shape((groups, count, columns // groups, 2 * own), BF16),
        ],
        in_specs=[ANY] * 6,
        out_specs=[VMEM, VMEM, ANY],
        scratch_shapes=[
            pltpu.VMEM((4, block, width), BF16),
            pltpu.VMEM((4, block, 2 * own), F32),
            pltpu.VMEM((2, tokens, columns), BF16),
            pltpu.VMEM((2, columns, 2 * own), BF16),
            DMA((4,)),
            DMA((4,)),
            DMA((2,)),
            DMA((2, groups)),
        ]
        + operand_scratch(count, activated, weight, False)
        + [pltpu.VMEM((rows, width), F32), DMA((1,))]
        + scatter_scratch(count, rows, width),
        compiler_params=comm_params(collective),
        cost_estimate=cost(48),
    )(activated, weight, middle, upstream, both, second)


def swap_halves(value):
    return jnp.concatenate([value[:, HEAD // 2 :], value[:, : HEAD // 2]], axis=1)


def nt(left, right):
    return lax.dot_general(left, right, (((1,), (1,)), ((), ())), preferred_element_type=F32)


def causal(keys, queries):
    key = lax.broadcasted_iota(jnp.int32, (keys, queries), 0)
    query = lax.rem(lax.broadcasted_iota(jnp.int32, (keys, queries), 1), CONT)
    return key <= query


def attention_kernel(
    heads, runs, joined, cosine, sine, q_gain, k_gain, attended, raw, queries, keys, values, mixed, lse, turned, placed
):
    tokens = joined.shape[0]
    blocks = tokens // CONT
    wide = heads * CONT

    def sort(run, carry):
        origin = pl.multiple_of(run * RUN, RUN)
        place = pl.multiple_of(runs[run] * RUN, RUN)
        raw[pl.ds(place, RUN), :] = joined[pl.ds(origin, RUN), :]
        return carry

    lax.fori_loop(0, tokens // RUN, sort, 0)

    def prepare(block, carry):
        span_rows = pl.ds(pl.multiple_of(block * CONT, CONT), CONT)
        cos_rows = cosine[span_rows, :]
        sin_rows = sine[span_rows, :]

        def turn(value, gain):
            value = value * lax.rsqrt(jnp.mean(value * value, axis=-1, keepdims=True) + EPS) * gain
            return (value * cos_rows + swap_halves(value) * sin_rows).astype(BF16)

        for head in range(heads):
            piece = raw[span_rows, head * HEAD : (head + 1) * HEAD]
            queries[block, head * CONT : (head + 1) * CONT, :] = turn(piece, q_gain[...])
        keys[span_rows, :] = turn(raw[span_rows, wide : wide + HEAD], k_gain[...])
        piece = raw[span_rows, wide + HEAD : wide + 2 * HEAD]
        values[span_rows, :] = piece.astype(BF16)
        turned[:, span_rows] = piece.T.astype(BF16)
        return carry

    lax.fori_loop(0, blocks, prepare, 0)

    def attend(block, own, before):
        query = queries[block]
        own_rows = pl.ds(own, CONT)
        weight = jnp.exp2(nt(keys[own_rows, :], query) * SCALE2)
        weight = jnp.where(causal(CONT, wide), weight, 0.0)
        sums = jnp.sum(weight, axis=0, keepdims=True)
        out = jnp.dot(turned[:, own_rows], weight.astype(BF16), preferred_element_type=F32)
        if before:
            weight = jnp.exp2(nt(keys[:before, :], query) * SCALE2)
            sums = sums + jnp.sum(weight, axis=0, keepdims=True)
            out = out + jnp.dot(turned[:, :before], weight.astype(BF16), preferred_element_type=F32)
        out = out / sums
        mixed[block] = out
        lse[block] = jnp.broadcast_to(jnp.log2(sums), (8, wide))
        for head in range(heads):
            placed[own_rows, head * HEAD : (head + 1) * HEAD] = out[
                :, head * CONT : (head + 1) * CONT
            ].T.astype(BF16)

    for block in range(PROMPT // CONT):
        attend(block, block * CONT, block * CONT)

    def continuation(block, carry):
        attend(block, pl.multiple_of(block * CONT, CONT), PROMPT)
        return carry

    lax.fori_loop(PROMPT // CONT, blocks, continuation, 0)

    def unsort(run, carry):
        origin = pl.multiple_of(run * RUN, RUN)
        place = pl.multiple_of(runs[run] * RUN, RUN)
        attended[pl.ds(origin, RUN), :] = placed[pl.ds(place, RUN), :]
        return carry

    lax.fori_loop(0, tokens // RUN, unsort, 0)


def attention(heads, runs, joined, cosine, sine, q_gain, k_gain):
    tokens = joined.shape[0]
    blocks = tokens // CONT
    wide = heads * CONT
    shape = jax.ShapeDtypeStruct
    return pl.pallas_call(
        functools.partial(attention_kernel, heads),
        out_shape=[
            shape((tokens, wide), BF16),
            shape(joined.shape, F32),
            shape((blocks, wide, HEAD), BF16),
            shape((tokens, HEAD), BF16),
            shape((tokens, HEAD), BF16),
            shape((blocks, HEAD, wide), F32),
            shape((blocks, 8, wide), F32),
        ],
        in_specs=[SMEM, VMEM, VMEM, VMEM, VMEM, VMEM],
        out_specs=[VMEM] * 7,
        scratch_shapes=[pltpu.VMEM((HEAD, tokens), BF16), pltpu.VMEM((tokens, wide), BF16)],
        compiler_params=pltpu.CompilerParams(vmem_limit_bytes=VMEM_LIMIT),
        cost_estimate=cost(15),
    )(runs, joined, cosine, sine, q_gain, k_gain)


def attention_back_kernel(
    heads, runs, d_attended, queries, keys, values, mixed, lse, d_queries, d_keys, d_values, arrived, keys_turned
):
    tokens = keys.shape[0]
    blocks = tokens // CONT
    wide = heads * CONT

    def sort(run, carry):
        origin = pl.multiple_of(run * RUN, RUN)
        place = pl.multiple_of(runs[run] * RUN, RUN)
        arrived[pl.ds(place, RUN), :] = d_attended[pl.ds(origin, RUN), :]
        return carry

    lax.fori_loop(0, tokens // RUN, sort, 0)
    d_keys[...] = jnp.zeros_like(d_keys)
    d_values[...] = jnp.zeros_like(d_values)

    def turn(block, carry):
        span_rows = pl.ds(pl.multiple_of(block * CONT, CONT), CONT)
        keys_turned[:, span_rows] = keys[span_rows, :].astype(F32).T.astype(BF16)
        return carry

    lax.fori_loop(0, blocks, turn, 0)

    def back(block, own, before):
        query = queries[block]
        own_rows = pl.ds(own, CONT)
        grad = jnp.concatenate(
            [arrived[own_rows, head * HEAD : (head + 1) * HEAD] for head in range(heads)], axis=0
        )
        grad_turned = grad.astype(F32).T
        delta = jnp.sum(grad_turned * mixed[block], axis=0, keepdims=True)
        total_row = lse[block][:1, :]

        def part(rows, count, masked):
            prob = jnp.exp2(nt(keys[rows, :], query) * SCALE2 - total_row)
            if masked:
                prob = jnp.where(causal(count, wide), prob, 0.0)
            score = (prob * (nt(values[rows, :], grad) - delta)).astype(BF16)
            d_values[rows, :] += jnp.dot(prob.astype(BF16), grad, preferred_element_type=F32)
            d_keys[rows, :] += jnp.dot(score, query, preferred_element_type=F32)
            return jnp.dot(keys_turned[:, rows], score, preferred_element_type=F32)

        result = part(own_rows, CONT, True)
        if before:
            result = result + part(slice(0, before), before, False)
        result = result * SCALE
        for head in range(heads):
            d_queries[own_rows, head * HEAD : (head + 1) * HEAD] = result[
                :, head * CONT : (head + 1) * CONT
            ].T.astype(BF16)

    for block in range(PROMPT // CONT):
        back(block, block * CONT, block * CONT)

    def continuation(block, carry):
        back(block, pl.multiple_of(block * CONT, CONT), PROMPT)
        return carry

    lax.fori_loop(PROMPT // CONT, blocks, continuation, 0)


def attention_back(heads, runs, d_attended, queries, keys, values, mixed, lse):
    tokens = keys.shape[0]
    wide = heads * CONT
    shape = jax.ShapeDtypeStruct
    return pl.pallas_call(
        functools.partial(attention_back_kernel, heads),
        out_shape=[shape((tokens, wide), BF16), shape((tokens, HEAD), F32), shape((tokens, HEAD), F32)],
        in_specs=[SMEM] + [VMEM] * 6,
        out_specs=[VMEM] * 3,
        scratch_shapes=[pltpu.VMEM((tokens, wide), BF16), pltpu.VMEM((HEAD, tokens), BF16)],
        compiler_params=pltpu.CompilerParams(vmem_limit_bytes=VMEM_LIMIT),
        cost_estimate=cost(25),
    )(runs, d_attended, queries, keys, values, mixed, lse)


def joined_back_kernel(
    heads, runs, raw, d_queries, d_keys, d_values, cosine, sine, q_gain, k_gain, share, d_joined, d_q_gain, d_k_gain, placed
):
    tokens = raw.shape[0]
    blocks = tokens // CONT
    wide = heads * CONT
    d_q_gain[...] = jnp.zeros_like(d_q_gain)
    d_k_gain[...] = jnp.zeros_like(d_k_gain)

    def step(block, carry):
        span_rows = pl.ds(pl.multiple_of(block * CONT, CONT), CONT)
        cos_rows = cosine[span_rows, :]
        sin_rows = sine[span_rows, :]

        def pull(value, grad, gain):
            grad = grad * cos_rows - swap_halves(grad) * sin_rows
            scale = lax.rsqrt(jnp.mean(value * value, axis=-1, keepdims=True) + EPS)
            scaled = value * scale
            gain_grad = jnp.sum(grad * scaled, axis=0, keepdims=True)
            grad = grad * gain
            return scale * (grad - scaled * jnp.mean(grad * scaled, axis=-1, keepdims=True)), gain_grad

        for head in range(heads):
            columns = slice(head * HEAD, (head + 1) * HEAD)
            grad, gain_grad = pull(
                raw[span_rows, columns], d_queries[span_rows, columns].astype(F32), q_gain[...]
            )
            placed[span_rows, columns] = grad.astype(BF16)
            d_q_gain[...] += gain_grad
        key_part, value_part = share[:1, :], share[1:, :]
        grad, gain_grad = pull(
            raw[span_rows, wide : wide + HEAD],
            (d_keys[span_rows, :] * SCALE).astype(BF16).astype(F32),
            k_gain[...],
        )
        placed[span_rows, wide : wide + HEAD] = (grad * key_part).astype(BF16)
        d_k_gain[...] += gain_grad * key_part
        placed[span_rows, wide + HEAD : wide + 2 * HEAD] = (d_values[span_rows, :] * value_part).astype(BF16)
        return carry

    lax.fori_loop(0, blocks, step, 0)

    def unsort(run, carry):
        origin = pl.multiple_of(run * RUN, RUN)
        place = pl.multiple_of(runs[run] * RUN, RUN)
        d_joined[pl.ds(origin, RUN), :] = placed[pl.ds(place, RUN), :]
        return carry

    lax.fori_loop(0, tokens // RUN, unsort, 0)


def attention_and_joined_back_kernel(
    heads,
    count,
    groups,
    runs,
    d_attended,
    queries,
    keys,
    values,
    mixed,
    lse,
    raw,
    cosine,
    sine,
    q_gain,
    k_gain,
    share,
    normed,
    d_out,
    d_joined,
    d_q_gain,
    d_k_gain,
    parts,
    d_queries,
    d_keys,
    d_values,
    arrived,
    keys_turned,
    raw_here,
    cosine_here,
    sine_here,
    placed,
    normed_slots,
    loaded,
    normed_in,
):
    columns = normed_slots.shape[2]

    def normed_copy(index):
        slot = lax.rem(index, 2)
        span_columns = pl.ds(pl.multiple_of(index * columns, columns), columns)
        return pltpu.make_async_copy(normed.at[:, span_columns], normed_slots.at[slot], normed_in.at[slot])

    loads = [
        pltpu.make_async_copy(source, target, loaded.at[index])
        for index, (source, target) in enumerate(
            [(raw, raw_here), (cosine, cosine_here), (sine, sine_here)]
        )
    ]
    for item in loads:
        item.start()
    normed_copy(0).start()
    attention_back_kernel(
        heads, runs, d_attended, queries, keys, values, mixed, lse, d_queries, d_keys, d_values, arrived, keys_turned
    )
    for item in loads:
        item.wait()
    joined_back_kernel(
        heads,
        runs,
        raw_here,
        d_queries,
        d_keys,
        d_values,
        cosine_here,
        sine_here,
        q_gain,
        k_gain,
        share,
        d_joined,
        d_q_gain,
        d_k_gain,
        placed,
    )
    rows = columns // groups
    width = d_joined.shape[1]

    def weight_grad(index, carry):
        @pl.when(index + 1 < count)
        def _():
            normed_copy(index + 1).start()

        normed_copy(index).wait()
        value = lax.dot_general(
            normed_slots[lax.rem(index, 2)], d_joined[...], (((0,), (0,)), ((), ())), preferred_element_type=F32
        ).astype(BF16)
        for owner in range(groups):
            parts[owner, index] = value[owner * rows : (owner + 1) * rows]
        return carry

    lax.fori_loop(0, count, weight_grad, 0)
    for owner in range(groups):
        for extra in range(d_out.shape[1] // width):
            parts[owner, count + extra] = d_out[
                owner * rows : (owner + 1) * rows, extra * width : (extra + 1) * width
            ]


def attention_and_joined_back(
    heads,
    count,
    groups,
    runs,
    d_attended,
    queries,
    keys,
    values,
    mixed,
    lse,
    raw,
    cosine,
    sine,
    q_gain,
    k_gain,
    share,
    normed,
    d_out,
):
    tokens = keys.shape[0]
    columns = normed.shape[1] // count
    blocks = count + d_out.shape[1] // raw.shape[1]
    wide = heads * CONT
    shape = jax.ShapeDtypeStruct
    return pl.pallas_call(
        functools.partial(attention_and_joined_back_kernel, heads, count, groups),
        out_shape=[
            shape(raw.shape, BF16),
            shape((1, HEAD), F32),
            shape((1, HEAD), F32),
            shape((groups, blocks, columns // groups, raw.shape[1]), BF16),
        ],
        in_specs=[SMEM] + [VMEM] * 6 + [ANY] * 3 + [VMEM] * 3 + [ANY, VMEM],
        out_specs=[VMEM] * 4,
        scratch_shapes=[
            pltpu.VMEM((tokens, wide), BF16),
            pltpu.VMEM((tokens, HEAD), F32),
            pltpu.VMEM((tokens, HEAD), F32),
            pltpu.VMEM((tokens, wide), BF16),
            pltpu.VMEM((HEAD, tokens), BF16),
            pltpu.VMEM(raw.shape, F32),
            pltpu.VMEM(cosine.shape, F32),
            pltpu.VMEM(sine.shape, F32),
            pltpu.VMEM(raw.shape, BF16),
            pltpu.VMEM((2, tokens, columns), BF16),
            DMA((3,)),
            DMA((2,)),
        ],
        compiler_params=pltpu.CompilerParams(vmem_limit_bytes=VMEM_LIMIT),
        cost_estimate=cost(30),
    )(runs, d_attended, queries, keys, values, mixed, lse, raw, cosine, sine, q_gain, k_gain, share, normed, d_out)


def joined_back(heads, runs, raw, d_queries, d_keys, d_values, cosine, sine, q_gain, k_gain, share):
    shape = jax.ShapeDtypeStruct
    return pl.pallas_call(
        functools.partial(joined_back_kernel, heads),
        out_shape=[shape(raw.shape, BF16), shape((1, HEAD), F32), shape((1, HEAD), F32)],
        in_specs=[SMEM] + [VMEM] * 9,
        out_specs=[VMEM] * 3,
        scratch_shapes=[pltpu.VMEM(raw.shape, BF16)],
        compiler_params=pltpu.CompilerParams(vmem_limit_bytes=VMEM_LIMIT),
        cost_estimate=cost(8),
    )(runs, raw, d_queries, d_keys, d_values, cosine, sine, q_gain, k_gain, share)


def rotary(tokens):
    index = np.arange(tokens)
    place = np.where(index < PROMPT, index, PROMPT + (index - PROMPT) % CONT).astype(np.float32)
    exponent = np.arange(HEAD // 2, dtype=np.float32) * np.float32(2.0 / HEAD)
    inverse = np.power(np.float32(ROPE_BASE), -exponent).astype(np.float32)
    angles = place[:, None] * inverse[None, :]
    cosine, sine = np.cos(angles), np.sin(angles)
    tables = np.concatenate([cosine, cosine], axis=1), np.concatenate([-sine, sine], axis=1)
    return tuple(jnp.asarray(table, F32) for table in tables)


def body(
    count,
    groups,
    hidden_in,
    segment_ids,
    positions,
    attn_gain,
    qkv_weight,
    query_norm_gain,
    k_gain,
    out_weight,
    mlp_gain,
    gate_up,
    down_weight,
    cotangent,
):
    hidden = hidden_in[0].astype(F32)
    rows, width = hidden.shape
    tokens = rows * count
    heads = QUERY_HEADS // count
    repeat = sharing(count)

    first = segment_ids[0, ::RUN]
    place = positions[0, ::RUN]
    order = jnp.where(first == 0, place, place + (first - 1) * CONT) // RUN
    runs = jnp.zeros((1, 8, 128), jnp.int32).at[0, 0, : rows // RUN].set(order)

    def gather_groups(values, axis):
        return lax.all_gather(values, "fsdp", axis=axis, tiled=True)

    def scatter_groups(values):
        return lax.psum_scatter(values, "fsdp", scatter_dimension=0, tiled=True)

    w_out = gather_groups(out_weight, 0)
    qkv_parts, mlp_parts = spread(count, 1, qkv_weight, gate_up)
    qkv_parts, w_out = lax.optimization_barrier((qkv_parts, w_out))
    w_qkv = gather_groups(qkv_parts, 1).reshape(width, -1)
    normed_local = norm_rows(hidden, attn_gain).astype(BF16)
    normed_local, qkv_parts = lax.optimization_barrier((normed_local, qkv_parts))
    normed, all_runs = opening(count, 2, normed_local, runs)
    mlp_parts, w_qkv, normed, upstream = lax.optimization_barrier((mlp_parts, w_qkv, normed, cotangent[0]))
    w_gu = gather_groups(mlp_parts, 1).reshape(width, -1)
    w_down = gather_groups(down_weight, 0)
    run_order = all_runs[:, 0, : rows // RUN].reshape(-1)
    cosine, sine = rotary(tokens)
    q_gain_row = query_norm_gain[None, :]
    k_gain_row = k_gain[None, :]

    blocks, masks = [upstream[None, : rows // 2], upstream[None, rows // 2 :]], [[0], [0]]
    chip_steps = len(bits_of(count)) - 1
    for step in range(chip_steps - 1):
        arrived, filled = gather_step(count, masks, blocks, step)
        if step == 0:
            joined = jnp.dot(normed, w_qkv, preferred_element_type=F32)
            joined, arrived = lax.optimization_barrier((joined, arrived))
        blocks = [jnp.concatenate(pair) for pair in zip(blocks, arrived)]
        masks = [held + more for held, more in zip(masks, filled)]
    arrived, filled = gather_step(count, masks, blocks, chip_steps - 1)
    attended, raw, queries, keys, values, mixed, lse = attention(
        heads, run_order, joined, cosine, sine, q_gain_row, k_gain_row
    )
    attended, arrived = lax.optimization_barrier((attended, arrived))
    middle, second = middle_and_second(count, 3, attended, w_out, hidden_in[0], mlp_gain[None, :])
    both = jnp.dot(second, w_gu, preferred_element_type=F32)
    own = both.shape[1] // 2
    gate, up = both[:, :own], both[:, own:]
    activated = (gate * jax.nn.sigmoid(gate) * up).astype(BF16)

    activated, arrived = lax.optimization_barrier((activated, arrived))
    upstream = gather_join(count, 5, masks, blocks, filled, arrived)
    d_down = jnp.dot(activated.T, upstream, preferred_element_type=F32).astype(BF16)
    d_down, upstream = lax.optimization_barrier((d_down, upstream))
    d_down = scatter_groups(d_down)
    output, d_both, gu_parts = back_through_mlp(
        count, groups, 9, activated, w_down, middle, upstream, both, second
    )
    gu_parts, d_both = lax.optimization_barrier((gu_parts, d_both))
    gu_parts = scatter_groups(gu_parts.reshape((groups * count,) + gu_parts.shape[2:]))

    def weight_grad(left, right):
        grad = lax.dot_general(left, right, (((0,), (0,)), ((), ())), preferred_element_type=F32)
        grad = grad.astype(BF16).reshape(count, groups, -1, right.shape[1])
        return grad.transpose(1, 0, 2, 3).reshape(groups * count, -1, right.shape[1])

    d_middle, mlp_gain_grad, d_attended, d_out = back_through_middle(
        count, 6, d_both, w_gu, middle, cotangent[0], mlp_gain[None, :], attended, w_out
    )
    d_attended, d_down = lax.optimization_barrier((d_attended, d_down))
    share = jnp.ones((2, HEAD), F32)
    tables = (cosine, sine, q_gain_row, k_gain_row)
    if repeat == 1:
        d_joined, q_gain_grad, k_gain_grad, parts = attention_and_joined_back(
            heads,
            count,
            groups,
            run_order,
            d_attended,
            queries,
            keys,
            values,
            mixed,
            lse,
            raw,
            *tables,
            share,
            normed,
            d_out,
        )
        parts, gu_parts, d_joined = lax.optimization_barrier((parts, gu_parts, d_joined))
        qkv_grad_parts = scatter_groups(parts.reshape((-1,) + parts.shape[2:]))
        d_out = qkv_grad_parts[count:].transpose(1, 0, 2).reshape(-1, width)
    else:
        d_queries, d_keys, d_values = attention_back(
            heads, run_order, d_attended, queries, keys, values, mixed, lse
        )
        d_keys = d_keys + across(count, 1, d_keys)
        d_values = d_values + across(count, 1, d_values)
        mine = lax.rem(lax.axis_index("ctx"), 2) == jnp.arange(2)
        share = share * mine[:, None].astype(F32)
        d_joined, q_gain_grad, k_gain_grad = joined_back(
            heads, run_order, raw, d_queries, d_keys, d_values, *tables, share
        )
        d_out = scatter_groups(d_out)
        qkv_grad_parts = scatter_groups(weight_grad(normed, d_joined))
    d_hidden, attn_gain_grad, d_gate_up = back_to_input(
        count, 8, d_joined, w_qkv, hidden_in[0], d_middle, attn_gain[None, :], gu_parts
    )
    d_hidden, qkv_grad_parts = lax.optimization_barrier((d_hidden, qkv_grad_parts))

    small = jnp.concatenate([attn_gain_grad[0], mlp_gain_grad[0], q_gain_grad[0], k_gain_grad[0]])
    padded = -(-small.shape[0] // 1024) * 1024
    small = jnp.pad(small, (0, padded - small.shape[0])).reshape(-1, 128)
    gains = last(count, groups, 11, small, qkv_grad_parts, width, qkv_weight.shape[1])
    attn_gain_sum, mlp_gain_sum, q_gain_sum, k_gain_sum, d_qkv = gains
    return (
        output[None],
        d_hidden[None],
        attn_gain_sum.reshape(-1),
        d_qkv,
        q_gain_sum.reshape(-1),
        k_gain_sum.reshape(-1),
        d_out.astype(F32),
        mlp_gain_sum.reshape(-1),
        d_gate_up,
        d_down.astype(F32),
    )


def solution(mesh):
    return jax.shard_map(
        functools.partial(body, mesh.shape["ctx"], mesh.shape["fsdp"]),
        mesh=mesh,
        in_specs=(
            P("fsdp", "ctx", None),
            P("fsdp", "ctx"),
            P("fsdp", "ctx"),
            P(),
            P(("ctx", "fsdp"), None),
            P(),
            P(),
            P(("ctx", "fsdp"), None),
            P(),
            P(("ctx", "fsdp"), None),
            P(("ctx", "fsdp"), None),
            P("fsdp", "ctx", None),
        ),
        out_specs=(
            P("fsdp", "ctx", None),
            P("fsdp", "ctx", None),
            P(),
            P(("ctx", "fsdp"), None),
            P(),
            P(),
            P(("ctx", "fsdp"), None),
            P(),
            P(("ctx", "fsdp"), None),
            P(("ctx", "fsdp"), None),
        ),
        check_vma=False,
    )
```

```python
import functools
import math

import jax
import jax.numpy as jnp
import numpy as np
from jax import lax
from jax.experimental import pallas as pl
from jax.experimental.pallas import tpu as pltpu
from jax.sharding import PartitionSpec as P

QUERY_HEADS = 16
KEY_VALUE_HEADS = 8
HEAD = 128
FF = 6144
PROMPT = 1024
CONT = 128
RUN = 32
EPS = 1e-06
ROPE_BASE = 1000000.0
SCALE = HEAD ** (-0.5)
SCALE2 = SCALE * math.log2(math.e)
MESH = pl.DeviceIdType.MESH
ANY = pl.BlockSpec(memory_space=pl.ANY)
VMEM = pl.BlockSpec(memory_space=pltpu.VMEM)
SMEM = pl.BlockSpec(memory_space=pltpu.SMEM)
BF16 = jnp.bfloat16
F32 = jnp.float32
DMA = pltpu.SemaphoreType.DMA
VMEM_LIMIT = 60 * 2**20


def cost(us):
    return pl.CostEstimate(flops=0, bytes_accessed=int(us * 1e6), transcendentals=0)


def flip(me, mask):
    result = me
    bit = 1
    while bit <= mask:
        if mask & bit:
            result = result + bit - 2 * bit * lax.rem(lax.div(me, bit), 2)
        bit *= 2
    return result


def bits_of(count):
    bits = []
    bit = 1
    while bit < count:
        bits.append(bit)
        bit *= 2
    return bits


def greet(peers):
    barrier = pltpu.get_barrier_semaphore()
    for peer in peers:
        pl.semaphore_signal(barrier, inc=1, device_id=peer, device_id_type=MESH)
    pl.semaphore_wait(barrier, len(peers))


def gather_orders(count):
    chip_bits = bits_of(count)[1:]
    return [chip_bits + [1], chip_bits[::-1] + [1]]


def last_bit(order, slot):
    return [bit for bit in order if slot & bit][-1]


def gather_rows(count, me, group, parts, source, target, send, recv, own=None):
    rows = target.shape[0] // count
    piece = rows // parts
    orders = gather_orders(count)
    copies = []

    def place(part, slot):
        return pl.multiple_of(flip(me, slot) * rows + part * piece, piece)

    def copy(part, slot, bit):
        there = target.at[pl.ds(place(part, slot), piece)]
        own_place = slot == 0 and source is not None
        origin = source.at[pl.ds(part * piece, piece)] if own_place else there
        number = part * count + (slot ^ bit)
        return pltpu.make_async_remote_copy(
            origin,
            there,
            send.at[number],
            recv.at[number],
            device_id=(flip(me, bit), group),
            device_id_type=MESH,
        )

    def keep(part):
        there = target.at[pl.ds(place(part, 0), piece)]
        return pltpu.make_async_copy(source.at[pl.ds(part * piece, piece)], there, own.at[part])

    def start(part):
        for bit in orders[part % 2]:
            item = copy(part, 0, bit)
            item.start()
            copies.append(item)
        if source is not None:
            keep(part).start()

    def wait(part, slot):
        there = target.at[pl.ds(place(part, slot), piece)]
        number = part * count + slot
        pltpu.make_async_remote_copy(
            there,
            there,
            send.at[number],
            recv.at[number],
            device_id=(flip(me, last_bit(orders[part % 2], slot)), group),
            device_id_type=MESH,
        ).wait_recv()

    def finish(arrived=None):
        waits = []
        for part in range(parts):
            order = orders[part % 2]
            for slot in range(1, count):
                last = order.index(last_bit(order, slot))
                waits.append((part // 2 + last, last, bin(slot).count("1"), part, slot))
        if arrived:
            for part in range(0, parts, 2):
                arrived(place(part, 0), 2 * piece)
        there = set()
        for _, last, _, part, slot in sorted(waits):
            wait(part, slot)
            for bit in orders[part % 2][last + 1 :]:
                item = copy(part, slot, bit)
                item.start()
                copies.append(item)
            there.add((part, slot))
            if arrived and (part ^ 1, slot) in there:
                arrived(place(part // 2 * 2, slot), 2 * piece)
        for part in range(parts):
            if source is not None:
                keep(part).wait()
        for item in copies:
            item.wait_send()

    return start, finish


def trade(count, me, group, pieces, source, target, send, recv):
    copies = []
    local = []

    def start(slots):
        for slot in slots:
            peer = flip(me, slot)
            for number, (origin, place) in enumerate(pieces(peer, me)):
                total = len(pieces(peer, me))
                index = slot * total + number
                if slot == 0:
                    item = pltpu.make_async_copy(source.at[origin], target.at[place], send.at[index])
                    local.append(item)
                else:
                    item = pltpu.make_async_remote_copy(
                        source.at[origin],
                        target.at[place],
                        send.at[index],
                        recv.at[index],
                        device_id=(peer, group),
                        device_id_type=MESH,
                    )
                    copies.append(item)
                item.start()

    def finish():
        for item in local:
            item.wait()
        for slot in range(1, count):
            peer = flip(me, slot)
            listed = pieces(me, peer)
            for number, (origin, place) in enumerate(listed):
                index = slot * len(listed) + number
                pltpu.make_async_remote_copy(
                    source.at[origin],
                    target.at[place],
                    send.at[index],
                    recv.at[index],
                    device_id=(peer, group),
                    device_id_type=MESH,
                ).wait_recv()
        for item in copies:
            item.wait_send()

    return start, finish


def all_slots(count):
    return list(range(1, count)) + [0]


def span(start, width):
    return pl.ds(pl.multiple_of(start, HEAD), width)


def sharing(count):
    if count not in (KEY_VALUE_HEADS, QUERY_HEADS):
        raise ValueError(count)
    return count // KEY_VALUE_HEADS


def qkv_spans(count, device, gradients=False):
    own = QUERY_HEADS // count * HEAD
    repeat = sharing(count)
    queries = QUERY_HEADS * HEAD
    shared = lax.div(device, repeat) * HEAD
    if repeat == 2 and gradients:
        which = lax.rem(device, 2)
        return [
            (device * own, 0, own),
            (queries + which * (KEY_VALUE_HEADS * HEAD) + shared, own + which * HEAD, HEAD),
        ]
    return [
        (device * own, 0, own),
        (queries + shared, own, HEAD),
        (queries + KEY_VALUE_HEADS * HEAD + shared, own + HEAD, HEAD),
    ]


def mlp_spans(count, device, gradients=False):
    own = FF // count
    return [(device * own, 0, own), (FF + device * own, own, own)]


def outgoing(spans, count):
    def pieces(device, owner):
        return [
            ((slice(None), span(whole, width)), (owner, slice(None), pl.ds(part, width)))
            for whole, part, width in spans(count, device)
        ]

    return pieces


def incoming(spans, count):
    def pieces(device, owner):
        return [
            ((device, slice(None), span(part, width)), (slice(None), span(whole, width)))
            for whole, part, width in spans(count, owner, True)
        ]

    return pieces


def everyone(count, me, group):
    return [(flip(me, slot), group) for slot in range(1, count)]


def spread_qkv_kernel(count, qkv, out, parts, send, recv, local):
    me = lax.axis_index("ctx")
    group = lax.axis_index("fsdp")
    width = parts.shape[2]
    greet(everyone(count, me, group))
    start, finish = trade(count, me, group, outgoing(qkv_spans, count), qkv, parts, send, recv)
    start(all_slots(count))
    items = [
        pltpu.make_async_copy(
            out.at[:, pl.ds(index * width, width)], parts.at[count + index], local.at[index]
        )
        for index in range(parts.shape[0] - count)
    ]
    for item in items:
        item.start()
    finish()
    for item in items:
        item.wait()


def spread_qkv(count, collective, qkv, out):
    rows = qkv.shape[0]
    width = qkv_width(count)
    extra = out.shape[1] // width if merges(count, out.shape[1]) else 0
    return pl.pallas_call(
        functools.partial(spread_qkv_kernel, count),
        out_shape=jax.ShapeDtypeStruct((count + extra, rows, width), BF16),
        in_specs=[ANY, VMEM],
        out_specs=ANY,
        scratch_shapes=[DMA((3 * count,)), DMA((3 * count,)), DMA((max(1, extra),))],
        compiler_params=pltpu.CompilerParams(collective_id=collective, has_side_effects=True),
        cost_estimate=cost(12),
    )(qkv, out)


def qkv_width(count):
    return QUERY_HEADS // count * HEAD + 2 * HEAD


def merges(count, width):
    return width % qkv_width(count) == 0


def spread_mlp_kernel(count, weight, parts, send, recv):
    me = lax.axis_index("ctx")
    group = lax.axis_index("fsdp")
    greet(everyone(count, me, group))
    start, finish = trade(count, me, group, outgoing(mlp_spans, count), weight, parts, send, recv)
    start(all_slots(count))
    finish()


def spread_mlp(count, collective, weight):
    return pl.pallas_call(
        functools.partial(spread_mlp_kernel, count),
        out_shape=jax.ShapeDtypeStruct((count, weight.shape[0], 2 * FF // count), BF16),
        in_specs=[ANY],
        out_specs=ANY,
        scratch_shapes=[DMA((2 * count,)), DMA((2 * count,))],
        compiler_params=pltpu.CompilerParams(collective_id=collective, has_side_effects=True),
        cost_estimate=cost(22),
    )(weight)


def opening_kernel(count, normed, runs, rows, all_runs, send, recv, own, run_send, run_recv):
    me = lax.axis_index("ctx")
    group = lax.axis_index("fsdp")
    greet(everyone(count, me, group))
    start, finish_runs = trade(
        count, me, group, lambda device, owner: [((0,), (owner,))], runs, all_runs, run_send, run_recv
    )
    start(all_slots(count))
    start, finish = gather_rows(count, me, group, 2, normed, rows, send, recv, own)
    start(0)
    start(1)
    finish()
    finish_runs()


def opening(count, collective, normed, runs):
    tokens, width = normed.shape
    return pl.pallas_call(
        functools.partial(opening_kernel, count),
        out_shape=[
            jax.ShapeDtypeStruct((count * tokens, width), BF16),
            jax.ShapeDtypeStruct((count, 8, 128), jnp.int32),
        ],
        in_specs=[VMEM, ANY],
        out_specs=[ANY, ANY],
        scratch_shapes=[DMA((2 * count,)), DMA((2 * count,)), DMA((2,)), DMA((count,)), DMA((count,))],
        compiler_params=pltpu.CompilerParams(collective_id=collective, has_side_effects=True),
        cost_estimate=cost(45),
    )(normed, runs)


def across(count, bit, values):
    return lax.ppermute(values, "ctx", [(index, index ^ bit) for index in range(count)])


def join_rows(count, me, group, slots, blocks, target, send, recv, local):
    other = flip(me, 1)
    half = blocks[0].shape[1]
    items = []
    for block, (part, masks) in zip(blocks, slots):
        items += [(block, index, part, mask) for index, mask in enumerate(masks)]

    def place(number, owner):
        _, _, part, mask = items[number]
        return pl.ds(pl.multiple_of(flip(owner, mask) * 2 * half + part * half, half), half)

    def copy(number, owner):
        block, index = items[number][:2]
        return pltpu.make_async_remote_copy(
            block.at[index],
            target.at[place(number, owner)],
            send.at[number],
            recv.at[number],
            device_id=(other, group),
            device_id_type=MESH,
        )

    def keep(number):
        block, index = items[number][:2]
        return pltpu.make_async_copy(block.at[index], target.at[place(number, me)], local.at[number])

    def start():
        for number in range(len(items)):
            copy(number, me).start()
            keep(number).start()

    def finish():
        for number in range(len(items)):
            keep(number).wait()
            copy(number, other).wait_recv()
            copy(number, me).wait_send()

    return start, finish


def gather_step(count, masks, blocks, step):
    arrived, filled = [], []
    for part, order in enumerate(gather_orders(count)):
        arrived.append(across(count, order[step], blocks[part]))
        filled.append([mask ^ order[step] for mask in masks[part]])
    return arrived, filled


def last_kernel(
    count,
    groups,
    attn_part,
    mlp_part,
    q_part,
    k_part,
    parts,
    attn_gain,
    mlp_gain,
    q_gain,
    k_gain,
    d_qkv,
    d_out,
    columns,
    out_parts,
    values,
    near,
    far,
    send,
    recv,
    far_send,
    far_recv,
    part_send,
    part_recv,
    out_in,
):
    me = lax.axis_index("ctx")
    group = lax.axis_index("fsdp")
    others = [lax.rem(group + step, groups) for step in range(1, groups)]
    greet(everyone(count, me, group) + [(me, other) for other in others])
    fetched = fetch([parts.at[pl.ds(count, out_parts.shape[0])]], [out_parts], out_in)
    rows = attn_gain.shape[0]
    for row in range(rows):
        values[row : row + 1] = attn_part[:, row * 128 : (row + 1) * 128]
        values[rows + row : rows + row + 1] = mlp_part[:, row * 128 : (row + 1) * 128]
    values[2 * rows : 2 * rows + 1] = q_part[...]
    values[2 * rows + 1 : 2 * rows + 2] = k_part[...]
    values[2 * rows + 2 :] = jnp.zeros((6, 128), F32)
    copies = []
    for slot in range(1, count):
        item = pltpu.make_async_remote_copy(
            values,
            near.at[me],
            send.at[slot],
            recv.at[slot],
            device_id=(flip(me, slot), group),
            device_id_type=MESH,
        )
        item.start()
        copies.append(item)
    start, finish = trade(
        count, me, group, incoming(qkv_spans, count), parts, columns, part_send, part_recv
    )
    start(all_slots(count))
    near[me] = values[...]
    for item in copies:
        item.wait()
    summed = near[0]
    for index in range(1, count):
        summed = summed + near[index]
    far[group] = summed
    copies = []
    for step, other in enumerate(others):
        item = pltpu.make_async_remote_copy(
            far.at[group],
            far.at[group],
            far_send.at[step],
            far_recv.at[step],
            device_id=(me, other),
            device_id_type=MESH,
        )
        item.start()
        copies.append(item)
    for item in copies:
        item.wait()
    summed = far[0]
    for index in range(1, groups):
        summed = summed + far[index]
    attn_gain[...] = summed[:rows]
    mlp_gain[...] = summed[rows : 2 * rows]
    q_gain[...] = summed[2 * rows : 2 * rows + 1]
    k_gain[...] = summed[2 * rows + 1 : 2 * rows + 2]
    fetched()
    width = out_parts.shape[2]
    for index in range(out_parts.shape[0]):
        d_out[:, index * width : (index + 1) * width] = out_parts[index].astype(F32)
    finish()
    d_qkv[...] = columns[...].astype(F32)


def last(count, groups, collective, gains, parts, columns):
    width = gains[0].shape[1]
    rows = width // 128
    shape = (2 * rows + 8, 128)
    long, short = (rows, 128), (1, 128)
    pieces = len(qkv_spans(count, 0, True))
    out_shape = (parts.shape[0] - count,) + parts.shape[1:]
    return pl.pallas_call(
        functools.partial(last_kernel, count, groups),
        out_shape=[jax.ShapeDtypeStruct(size, F32) for size in (long, long, short, short)]
        + [
            jax.ShapeDtypeStruct((parts.shape[1], columns), F32),
            jax.ShapeDtypeStruct((parts.shape[1], out_shape[0] * out_shape[2]), F32),
        ],
        in_specs=[VMEM] * 4 + [ANY],
        out_specs=[VMEM] * 6,
        scratch_shapes=[
            pltpu.VMEM((parts.shape[1], columns), BF16),
            pltpu.VMEM(out_shape, BF16),
            pltpu.VMEM(shape, F32),
            pltpu.VMEM((count,) + shape, F32),
            pltpu.VMEM((groups,) + shape, F32),
            DMA((count,)),
            DMA((count,)),
            DMA((groups,)),
            DMA((groups,)),
            DMA((pieces * count,)),
            DMA((pieces * count,)),
            DMA((1,)),
        ],
        compiler_params=pltpu.CompilerParams(collective_id=collective, has_side_effects=True),
        cost_estimate=cost(14),
    )(*gains, parts)


def product_slots(count):
    slots = []
    for pair in range(count // 2)[::-1]:
        slots += [2 * pair - 1, 2 * pair] if slots and pair else [2 * pair + 1, 2 * pair - 1, 2 * pair] if pair else [0]
    return slots


def load_operands(count, me, flipped, left_from, right_from, left, right, left_in, right_in):
    rows = left.shape[0] // count
    width = right.shape[0] if flipped else right.shape[1]
    tile = min(512, width)

    def left_copy(slot):
        span_rows = pl.ds(pl.multiple_of(flip(me, slot) * rows, rows), rows)
        return pltpu.make_async_copy(left_from.at[span_rows], left.at[span_rows], left_in.at[slot])

    def right_copy(index):
        span_tile = pl.ds(pl.multiple_of(index * tile, tile), tile)
        place = (span_tile,) if flipped else (slice(None), span_tile)
        return pltpu.make_async_copy(right_from.at[place], right.at[place], right_in.at[index])

    slots = product_slots(count)
    right_copy(0).start()
    left_copy(slots[0]).start()
    for index in range(1, width // tile):
        right_copy(index).start()
    for slot in slots[1:]:
        left_copy(slot).start()
    return lambda slot: left_copy(slot).wait(), lambda index: right_copy(index).wait()


def operand_scratch(count, left, right, flipped):
    width = right.shape[0] if flipped else right.shape[1]
    return [
        pltpu.VMEM(left.shape, BF16),
        pltpu.VMEM(right.shape, BF16),
        DMA((count,)),
        DMA((width // min(512, width),)),
    ]


def fetch(sources, targets, arrived):
    items = [
        pltpu.make_async_copy(source, target, arrived.at[index])
        for index, (source, target) in enumerate(zip(sources, targets))
    ]
    for item in items:
        item.start()

    def wait():
        for item in items:
            item.wait()

    return wait


def product_scatter(
    count,
    me,
    group,
    parts,
    flipped,
    left,
    right,
    done,
    kept,
    near_out,
    near_in,
    far_out,
    far_in,
    ns,
    nr,
    fs,
    fr,
    ready=None,
):
    rows, width = kept.shape
    piece = rows // parts
    bits = bits_of(count)
    orders = [bits[1:][::-1], bits[1:]]
    tile = min(512, width)
    pairs = list(range(count // 2))[::-1]

    def product(slot, store):
        start = pl.multiple_of(flip(me, slot) * rows, rows)
        if ready:
            ready[0](slot)
        block = left[pl.ds(start, rows), :]

        def step(index, carry):
            columns = pl.ds(pl.multiple_of(index * tile, tile), tile)
            if ready and slot == count - 1:
                ready[1](index)
            if flipped:
                value = nt(block, right[columns, :])
            else:
                value = jnp.dot(block, right[:, columns], preferred_element_type=F32)
            store(columns, value)
            return carry

        lax.fori_loop(0, width // tile, step, 0)

    def first(part, slot):
        return [bit for bit in orders[part % 2] if slot & bit][0]

    def near(pair):
        return pltpu.make_async_remote_copy(
            near_out.at[pair],
            near_in.at[pair],
            ns.at[pair],
            nr.at[pair],
            device_id=(flip(me, 1), group),
            device_id_type=MESH,
        )

    def number(part, pair):
        return part * (count // 2 - 1) + pair - 1

    def far(part, pair):
        index = number(part, pair)
        return pltpu.make_async_remote_copy(
            far_out.at[index],
            far_in.at[index],
            fs.at[index],
            fr.at[index],
            device_id=(flip(me, first(part, 2 * pair)), group),
            device_id_type=MESH,
        )

    def needs(part, pair):
        found = []
        for bit in orders[part % 2]:
            if 2 * pair & bit:
                break
            found.append((2 * pair ^ bit) // 2)
        return found

    def settle(part, pair):
        if pair == 0:
            value = kept[pl.ds(part * piece, piece), :]
        else:
            value = far_out[number(part, pair)].astype(F32)
        for other in needs(part, pair):
            far(part, other).wait_recv()
            value = value + far_in[number(part, other)].astype(F32)
        if pair == 0:
            done(part, value)
        else:
            far_out[number(part, pair)] = value.astype(BF16)
            far(part, pair).start()

    def send_near(pair):
        def store(columns, value):
            near_out[pair, :, columns] = value.astype(BF16)

        product(2 * pair + 1, store)
        near(pair).start()

    def batch_parts(batch):
        return (2 * batch, 2 * batch + 1)

    def send_pair(batch, pair):
        for part in batch_parts(batch):
            if pair and not needs(part, pair):
                far(part, pair).start()

    def sum_near(pair):
        near(pair).wait_recv()

        def store(columns, value):
            value = value + near_in[pair, :, columns].astype(F32)
            if pair == 0:
                kept[:, columns] = value
            else:
                for part in range(parts):
                    far_out[number(part, pair), :, columns] = value[
                        part * piece : (part + 1) * piece
                    ].astype(BF16)

        product(2 * pair, store)
        send_pair(0, pair)

    def begin():
        send_near(pairs[0])
        for pair in pairs:
            if pair:
                send_near(pair - 1)
            sum_near(pair)

    def send(batch):
        for pair in pairs:
            send_pair(batch, pair)

    def pass_on(batch):
        for pair in pairs:
            for part in batch_parts(batch):
                if pair and needs(part, pair):
                    settle(part, pair)

    def end(batch):
        for part in batch_parts(batch):
            settle(part, 0)

    def close():
        for pair in pairs:
            near(pair).wait_send()
            for part in range(parts):
                if pair:
                    far(part, pair).wait_send()

    return begin, send, pass_on, end, close


def scatter_scratch(count, rows, width, parts=2):
    pairs = count // 2
    links = parts * (pairs - 1)
    return [
        pltpu.VMEM((rows, width), F32),
        pltpu.VMEM((pairs, rows, width), BF16),
        pltpu.VMEM((pairs, rows, width), BF16),
        pltpu.VMEM((links, rows // parts, width), BF16),
        pltpu.VMEM((links, rows // parts, width), BF16),
        DMA((pairs,)),
        DMA((pairs,)),
        DMA((links,)),
        DMA((links,)),
    ]


SCATTER = 9
PARTS = 4
BACK_PARTS = 2


def comm_params(collective):
    return pltpu.CompilerParams(
        collective_id=collective, has_side_effects=True, vmem_limit_bytes=VMEM_LIMIT
    )


def row_blocks(first, count, step):
    def body(index, carry):
        step(pl.multiple_of(first + index * 32, 32), pl.multiple_of(index * 32, 32))
        return carry

    lax.fori_loop(0, count // 32, body, 0)


def norm_back(values, gain, grad):
    scale = lax.rsqrt(jnp.mean(values * values, axis=-1, keepdims=True) + EPS)
    scaled = values * scale
    pushed = grad * gain
    back = scale * (pushed - scaled * jnp.mean(pushed * scaled, axis=-1, keepdims=True))
    return back, jnp.sum(grad * scaled, axis=0, keepdims=True)


def norm_rows(values, gain):
    return values * lax.rsqrt(jnp.mean(values * values, axis=-1, keepdims=True) + EPS) * gain


def middle_kernel(count, slots, left, right, hidden, gain, *refs):
    held, refs = refs[: len(slots)], refs[len(slots) :]
    (middle, gathered, joined, own_rows, sums), refs = refs[:5], refs[5:]
    blocks, refs = refs[: len(slots)], refs[len(slots) :]
    (held_in, send, recv, local), scratch = refs[:4], refs[4:]
    me = lax.axis_index("ctx")
    group = lax.axis_index("fsdp")
    piece = middle.shape[0] // PARTS
    fetched = fetch(held, blocks, held_in)
    greet([(flip(me, bit), group) for bit in bits_of(count)])
    start, finish = gather_rows(count, me, group, PARTS, own_rows, gathered, *scratch[SCATTER:])
    start_join, finish_join = join_rows(count, me, group, slots, blocks, joined, send, recv, local)

    def done(part, value):
        sums[...] = value

        def step(row, place):
            total_rows = hidden[pl.ds(row, 32), :].astype(F32) + sums[pl.ds(place, 32), :]
            middle[pl.ds(row, 32), :] = total_rows
            own_rows[pl.ds(row, 32), :] = norm_rows(total_rows, gain[...]).astype(BF16)

        row_blocks(part * piece, piece, step)
        start(part)

    begin, send_batch, pass_on, end, close = product_scatter(
        count, me, group, PARTS, False, left, right, done, *scratch[:SCATTER]
    )
    begin()
    fetched()
    start_join()
    pass_on(0)
    send_batch(1)
    end(0)
    pass_on(1)
    end(1)
    finish()
    finish_join()
    close()


def gather_scratch(count, parts):
    return [DMA((parts * count,)), DMA((parts * count,)), DMA((parts,))]


def middle_and_second(count, collective, left, right, hidden, gain, masks, blocks, filled, arrived):
    rows, width = hidden.shape
    slots, held = [], []
    for part in (0, 1):
        slots += [(part, masks[part]), (part, filled[part])]
        held += [blocks[part], arrived[part]]
    return pl.pallas_call(
        functools.partial(middle_kernel, count, slots),
        out_shape=[
            jax.ShapeDtypeStruct((rows, width), F32),
            jax.ShapeDtypeStruct((count * rows, width), BF16),
            jax.ShapeDtypeStruct((count * rows, width), BF16),
        ],
        in_specs=[VMEM] * 4 + [ANY] * len(held),
        out_specs=[VMEM, ANY, ANY],
        scratch_shapes=[pltpu.VMEM((rows, width), BF16), pltpu.VMEM((rows // PARTS, width), F32)]
        + [pltpu.VMEM(block.shape, BF16) for block in held]
        + [DMA((len(held),)), DMA((count,)), DMA((count,)), DMA((count,))]
        + scatter_scratch(count, rows, width, PARTS)
        + gather_scratch(count, PARTS),
        compiler_params=comm_params(collective),
        cost_estimate=cost(80),
    )(left, right, hidden, gain, *held)


def back_kernel(
    count,
    left_from,
    right_from,
    middle_from,
    cotangent_from,
    gain,
    attended_from,
    out_weight_from,
    d_middle,
    d_gain,
    d_attended,
    d_out,
    sums,
    gathered,
    turned,
    out_sum,
    left,
    right,
    left_in,
    right_in,
    middle,
    cotangent,
    attended,
    out_weight,
    others_in,
    *scratch,
):
    me = lax.axis_index("ctx")
    group = lax.axis_index("fsdp")
    piece = middle.shape[0] // BACK_PARTS
    own = me * middle.shape[0]
    ready = load_operands(count, me, True, left_from, right_from, left, right, left_in, right_in)
    fetched = fetch(
        (middle_from, cotangent_from, attended_from, out_weight_from),
        (middle, cotangent, attended, out_weight),
        others_in,
    )
    greet([(flip(me, bit), group) for bit in bits_of(count)])
    start, finish = gather_rows(count, me, group, BACK_PARTS, None, gathered, *scratch[SCATTER:])
    d_gain[...] = jnp.zeros_like(d_gain)

    def done(part, value):
        sums[...] = value

        def step(row, place):
            span_rows = pl.ds(row, 32)
            back, gain_part = norm_back(middle[span_rows, :], gain[...], sums[pl.ds(place, 32), :])
            back = back + cotangent[span_rows, :].astype(F32)
            d_middle[span_rows, :] = back
            gathered[pl.ds(pl.multiple_of(own + row, 32), 32), :] = back.astype(BF16)
            d_gain[...] += gain_part

        row_blocks(part * piece, piece, step)
        start(part)

    begin, _, pass_on, end, close = product_scatter(
        count, me, group, BACK_PARTS, True, left, right, done, *scratch[:SCATTER], ready=ready
    )
    begin()
    fetched()
    out_sum[...] = jnp.zeros_like(out_sum)

    def turn(index, carry):
        span_rows = pl.ds(pl.multiple_of(index * 256, 256), 256)
        turned[:, span_rows] = attended[span_rows, :].astype(F32).T.astype(BF16)
        return carry

    lax.fori_loop(0, attended.shape[0] // 256, turn, 0)
    pass_on(0)
    end(0)

    def arrived(row, size):
        block = gathered[pl.ds(row, size), :]
        d_attended[pl.ds(row, size), :] = nt(block, out_weight[...]).astype(BF16)
        if size % 128 == 0:
            out_sum[...] += jnp.dot(turned[:, pl.ds(row, size)], block, preferred_element_type=F32)

    finish(arrived)
    close()
    if 2 * piece % 128:
        out_sum[...] = jnp.dot(turned[...], gathered[...], preferred_element_type=F32)
    d_out[...] = out_sum[...].astype(BF16)


def back_through_middle(count, collective, left, right, middle, cotangent, gain, attended, out_weight):
    rows, width = middle.shape
    tokens, wide = attended.shape
    shape = jax.ShapeDtypeStruct
    return pl.pallas_call(
        functools.partial(back_kernel, count),
        out_shape=[
            shape((rows, width), F32),
            shape((1, width), F32),
            shape((tokens, wide), BF16),
            shape((wide, width), BF16),
        ],
        in_specs=[ANY] * 4 + [VMEM] + [ANY] * 2,
        out_specs=[VMEM] * 4,
        scratch_shapes=[
            pltpu.VMEM((rows // BACK_PARTS, width), F32),
            pltpu.VMEM((tokens, width), BF16),
            pltpu.VMEM((wide, tokens), BF16),
            pltpu.VMEM((wide, width), F32),
        ]
        + operand_scratch(count, left, right, True)
        + [
            pltpu.VMEM((rows, width), F32),
            pltpu.VMEM((rows, width), BF16),
            pltpu.VMEM((tokens, wide), BF16),
            pltpu.VMEM((wide, width), BF16),
            DMA((4,)),
        ]
        + scatter_scratch(count, rows, width, BACK_PARTS)
        + gather_scratch(count, BACK_PARTS)[:2],
        compiler_params=comm_params(collective),
        cost_estimate=cost(85),
    )(left, right, middle, cotangent, gain, attended, out_weight)


def input_kernel(
    count, left, right, hidden, d_middle, gain, parts, d_hidden, d_gain, columns, sums, send, recv, *scratch
):
    me = lax.axis_index("ctx")
    group = lax.axis_index("fsdp")
    half = hidden.shape[0] // 2
    greet(everyone(count, me, group))
    start, finish = trade(count, me, group, incoming(mlp_spans, count), parts, columns, send, recv)
    early = [0, 1, 2, 4]
    start(early)
    d_gain[...] = jnp.zeros_like(d_gain)

    def done(part, value):
        sums[...] = value

        def step(row, place):
            span_rows = pl.ds(row, 32)
            values = hidden[span_rows, :].astype(F32)
            back, gain_part = norm_back(values, gain[...], sums[pl.ds(place, 32), :])
            d_hidden[span_rows, :] = d_middle[span_rows, :] + back
            d_gain[...] += gain_part

        row_blocks(part * half, half, step)

    begin, _, pass_on, end, close = product_scatter(
        count, me, group, 2, True, left, right, done, *scratch
    )
    begin()
    pass_on(0)
    start([slot for slot in range(count) if slot not in early])
    end(0)
    finish()
    close()


def back_to_input(count, collective, left, right, hidden, d_middle, gain, parts):
    rows, width = hidden.shape
    shape = jax.ShapeDtypeStruct
    return pl.pallas_call(
        functools.partial(input_kernel, count),
        out_shape=[
            shape((rows, width), F32),
            shape((1, width), F32),
            shape((parts.shape[1], 2 * FF), BF16),
        ],
        in_specs=[VMEM] * 5 + [ANY],
        out_specs=[VMEM, VMEM, ANY],
        scratch_shapes=[
            pltpu.VMEM((rows // 2, width), F32),
            DMA((2 * count,)),
            DMA((2 * count,)),
        ]
        + scatter_scratch(count, rows, width),
        compiler_params=comm_params(collective),
        cost_estimate=cost(60),
    )(left, right, hidden, d_middle, gain, parts)


def mlp_kernel(
    count,
    groups,
    activated_from,
    weight_from,
    middle_from,
    upstream,
    both,
    second,
    output,
    d_both,
    parts,
    up_slots,
    both_slots,
    second_slots,
    part_slots,
    up_in,
    both_in,
    second_in,
    parts_out,
    activated,
    weight,
    activated_in,
    weight_in,
    middle,
    others_in,
    *scratch,
):
    me = lax.axis_index("ctx")
    group = lax.axis_index("fsdp")
    half = middle.shape[0] // 2
    tokens, own = activated.shape
    block = up_slots.shape[1]
    columns = second_slots.shape[2]
    ready = load_operands(
        count, me, False, activated_from, weight_from, activated, weight, activated_in, weight_in
    )
    fetched = fetch((middle_from,), (middle,), others_in)
    greet([(flip(me, bit), group) for bit in bits_of(count)])

    def rows_in(index):
        slot = lax.rem(index, 4)
        rows = pl.ds(pl.multiple_of(index * block, block), block)
        return (
            pltpu.make_async_copy(upstream.at[rows], up_slots.at[slot], up_in.at[slot]),
            pltpu.make_async_copy(both.at[rows], both_slots.at[slot], both_in.at[slot]),
        )

    def second_copy(index):
        slot = lax.rem(index, 2)
        span_columns = pl.ds(pl.multiple_of(index * columns, columns), columns)
        return pltpu.make_async_copy(second.at[:, span_columns], second_slots.at[slot], second_in.at[slot])

    def part_copies(index):
        slot = lax.rem(index, 2)
        rows = columns // groups
        return [
            pltpu.make_async_copy(
                part_slots.at[slot, pl.ds(owner * rows, rows)],
                parts.at[owner, index],
                parts_out.at[slot, owner],
            )
            for owner in range(groups)
        ]

    for item in rows_in(0) + rows_in(1):
        item.start()
    second_copy(0).start()

    def done(part, value):
        span_rows = pl.ds(part * half, half)
        output[span_rows, :] = (middle[span_rows, :] + value).astype(BF16)

    begin, _, pass_on, end, close = product_scatter(
        count, me, group, 2, False, activated, weight, done, *scratch, ready=ready
    )
    begin()
    fetched()
    steps = tokens // block

    def activation(index, carry):
        @pl.when(2 * index + 2 < steps)
        def _():
            for item in rows_in(2 * index + 2) + rows_in(2 * index + 3):
                item.start()

        for item in rows_in(2 * index) + rows_in(2 * index + 1):
            item.wait()
        slots = [lax.rem(2 * index + turn, 4) for turn in (0, 1)]
        grads = [nt(up_slots[slot], weight[...]).astype(BF16).astype(F32) for slot in slots]
        for turn, (slot, grad) in enumerate(zip(slots, grads)):
            rows = pl.ds(pl.multiple_of((2 * index + turn) * block, block), block)
            gate = both_slots[slot, :, :own]
            up = both_slots[slot, :, own:]
            sigmoid = 1.0 / (1.0 + jnp.exp(-gate))
            d_both[rows, :own] = (grad * up * sigmoid * (1.0 + gate * (1.0 - sigmoid))).astype(BF16)
            d_both[rows, own:] = (grad * gate * sigmoid).astype(BF16)
        return carry

    lax.fori_loop(0, steps // 2, activation, 0)

    def weight_grad(index, carry):
        @pl.when(index + 1 < count)
        def _():
            second_copy(index + 1).start()

        second_copy(index).wait()

        @pl.when(index >= 2)
        def _():
            for item in part_copies(index - 2):
                item.wait()

        slot = lax.rem(index, 2)
        value = lax.dot_general(
            second_slots[slot], d_both[...], (((0,), (0,)), ((), ())), preferred_element_type=F32
        )
        part_slots[slot] = value.astype(BF16)
        for item in part_copies(index):
            item.start()
        return carry

    lax.fori_loop(0, count // 2, weight_grad, 0)
    pass_on(0)
    lax.fori_loop(count // 2, count, weight_grad, 0)
    for index in (count - 2, count - 1):
        for item in part_copies(index):
            item.wait()
    end(0)
    close()


def back_through_mlp(count, groups, collective, activated, weight, middle, upstream, both, second):
    rows, width = middle.shape
    tokens, own = activated.shape
    block = 256
    columns = width // count
    shape = jax.ShapeDtypeStruct
    return pl.pallas_call(
        functools.partial(mlp_kernel, count, groups),
        out_shape=[
            shape((rows, width), BF16),
            shape((tokens, 2 * own), BF16),
            shape((groups, count, columns // groups, 2 * own), BF16),
        ],
        in_specs=[ANY] * 6,
        out_specs=[VMEM, VMEM, ANY],
        scratch_shapes=[
            pltpu.VMEM((4, block, width), BF16),
            pltpu.VMEM((4, block, 2 * own), F32),
            pltpu.VMEM((2, tokens, columns), BF16),
            pltpu.VMEM((2, columns, 2 * own), BF16),
            DMA((4,)),
            DMA((4,)),
            DMA((2,)),
            DMA((2, groups)),
        ]
        + operand_scratch(count, activated, weight, False)
        + [pltpu.VMEM((rows, width), F32), DMA((1,))]
        + scatter_scratch(count, rows, width),
        compiler_params=comm_params(collective),
        cost_estimate=cost(48),
    )(activated, weight, middle, upstream, both, second)


def swap_halves(value):
    return jnp.concatenate([value[:, HEAD // 2 :], value[:, : HEAD // 2]], axis=1)


def nt(left, right):
    return lax.dot_general(left, right, (((1,), (1,)), ((), ())), preferred_element_type=F32)


def causal(keys, queries):
    key = lax.broadcasted_iota(jnp.int32, (keys, queries), 0)
    query = lax.rem(lax.broadcasted_iota(jnp.int32, (keys, queries), 1), CONT)
    return key <= query


def attention_kernel(
    heads, runs, joined, cosine, sine, q_gain, k_gain, attended, raw, queries, keys, values, mixed, lse, turned, placed
):
    tokens = joined.shape[0]
    blocks = tokens // CONT
    wide = heads * CONT

    def sort(run, carry):
        origin = pl.multiple_of(run * RUN, RUN)
        place = pl.multiple_of(runs[run] * RUN, RUN)
        raw[pl.ds(place, RUN), :] = joined[pl.ds(origin, RUN), :]
        return carry

    lax.fori_loop(0, tokens // RUN, sort, 0)

    def prepare(block, carry):
        span_rows = pl.ds(pl.multiple_of(block * CONT, CONT), CONT)
        cos_rows = cosine[span_rows, :]
        sin_rows = sine[span_rows, :]

        def turn(value, gain):
            value = value * lax.rsqrt(jnp.mean(value * value, axis=-1, keepdims=True) + EPS) * gain
            return (value * cos_rows + swap_halves(value) * sin_rows).astype(BF16)

        for head in range(heads):
            piece = raw[span_rows, head * HEAD : (head + 1) * HEAD]
            queries[block, head * CONT : (head + 1) * CONT, :] = turn(piece, q_gain[...])
        keys[span_rows, :] = turn(raw[span_rows, wide : wide + HEAD], k_gain[...])
        piece = raw[span_rows, wide + HEAD : wide + 2 * HEAD]
        values[span_rows, :] = piece.astype(BF16)
        turned[:, span_rows] = piece.T.astype(BF16)
        return carry

    lax.fori_loop(0, blocks, prepare, 0)

    def attend(block, own, before):
        query = queries[block]
        own_rows = pl.ds(own, CONT)
        weight = jnp.exp2(nt(keys[own_rows, :], query) * SCALE2)
        weight = jnp.where(causal(CONT, wide), weight, 0.0)
        sums = jnp.sum(weight, axis=0, keepdims=True)
        out = jnp.dot(turned[:, own_rows], weight.astype(BF16), preferred_element_type=F32)
        if before:
            weight = jnp.exp2(nt(keys[:before, :], query) * SCALE2)
            sums = sums + jnp.sum(weight, axis=0, keepdims=True)
            out = out + jnp.dot(turned[:, :before], weight.astype(BF16), preferred_element_type=F32)
        out = out / sums
        mixed[block] = out
        lse[block] = jnp.broadcast_to(jnp.log2(sums), (8, wide))
        for head in range(heads):
            placed[own_rows, head * HEAD : (head + 1) * HEAD] = out[
                :, head * CONT : (head + 1) * CONT
            ].T.astype(BF16)

    for block in range(PROMPT // CONT):
        attend(block, block * CONT, block * CONT)

    def continuation(block, carry):
        attend(block, pl.multiple_of(block * CONT, CONT), PROMPT)
        return carry

    lax.fori_loop(PROMPT // CONT, blocks, continuation, 0)

    def unsort(run, carry):
        origin = pl.multiple_of(run * RUN, RUN)
        place = pl.multiple_of(runs[run] * RUN, RUN)
        attended[pl.ds(origin, RUN), :] = placed[pl.ds(place, RUN), :]
        return carry

    lax.fori_loop(0, tokens // RUN, unsort, 0)


def attention(heads, runs, joined, cosine, sine, q_gain, k_gain):
    tokens = joined.shape[0]
    blocks = tokens // CONT
    wide = heads * CONT
    shape = jax.ShapeDtypeStruct
    return pl.pallas_call(
        functools.partial(attention_kernel, heads),
        out_shape=[
            shape((tokens, wide), BF16),
            shape(joined.shape, F32),
            shape((blocks, wide, HEAD), BF16),
            shape((tokens, HEAD), BF16),
            shape((tokens, HEAD), BF16),
            shape((blocks, HEAD, wide), F32),
            shape((blocks, 8, wide), F32),
        ],
        in_specs=[SMEM, VMEM, VMEM, VMEM, VMEM, VMEM],
        out_specs=[VMEM] * 7,
        scratch_shapes=[pltpu.VMEM((HEAD, tokens), BF16), pltpu.VMEM((tokens, wide), BF16)],
        compiler_params=pltpu.CompilerParams(vmem_limit_bytes=VMEM_LIMIT),
        cost_estimate=cost(15),
    )(runs, joined, cosine, sine, q_gain, k_gain)


def attention_back_kernel(
    heads, runs, d_attended, queries, keys, values, mixed, lse, d_queries, d_keys, d_values, arrived, keys_turned
):
    tokens = keys.shape[0]
    blocks = tokens // CONT
    wide = heads * CONT

    def sort(run, carry):
        origin = pl.multiple_of(run * RUN, RUN)
        place = pl.multiple_of(runs[run] * RUN, RUN)
        arrived[pl.ds(place, RUN), :] = d_attended[pl.ds(origin, RUN), :]
        return carry

    lax.fori_loop(0, tokens // RUN, sort, 0)
    d_keys[...] = jnp.zeros_like(d_keys)
    d_values[...] = jnp.zeros_like(d_values)

    def turn(block, carry):
        span_rows = pl.ds(pl.multiple_of(block * CONT, CONT), CONT)
        keys_turned[:, span_rows] = keys[span_rows, :].astype(F32).T.astype(BF16)
        return carry

    lax.fori_loop(0, blocks, turn, 0)

    def back(block, own, before):
        query = queries[block]
        own_rows = pl.ds(own, CONT)
        grad = jnp.concatenate(
            [arrived[own_rows, head * HEAD : (head + 1) * HEAD] for head in range(heads)], axis=0
        )
        grad_turned = grad.astype(F32).T
        delta = jnp.sum(grad_turned * mixed[block], axis=0, keepdims=True)
        total_row = lse[block][:1, :]

        def part(rows, count, masked):
            prob = jnp.exp2(nt(keys[rows, :], query) * SCALE2 - total_row)
            if masked:
                prob = jnp.where(causal(count, wide), prob, 0.0)
            score = (prob * (nt(values[rows, :], grad) - delta)).astype(BF16)
            d_values[rows, :] += jnp.dot(prob.astype(BF16), grad, preferred_element_type=F32)
            d_keys[rows, :] += jnp.dot(score, query, preferred_element_type=F32)
            return jnp.dot(keys_turned[:, rows], score, preferred_element_type=F32)

        result = part(own_rows, CONT, True)
        if before:
            result = result + part(slice(0, before), before, False)
        result = result * SCALE
        for head in range(heads):
            d_queries[own_rows, head * HEAD : (head + 1) * HEAD] = result[
                :, head * CONT : (head + 1) * CONT
            ].T.astype(BF16)

    for block in range(PROMPT // CONT):
        back(block, block * CONT, block * CONT)

    def continuation(block, carry):
        back(block, pl.multiple_of(block * CONT, CONT), PROMPT)
        return carry

    lax.fori_loop(PROMPT // CONT, blocks, continuation, 0)


def attention_back(heads, runs, d_attended, queries, keys, values, mixed, lse):
    tokens = keys.shape[0]
    wide = heads * CONT
    shape = jax.ShapeDtypeStruct
    return pl.pallas_call(
        functools.partial(attention_back_kernel, heads),
        out_shape=[shape((tokens, wide), BF16), shape((tokens, HEAD), F32), shape((tokens, HEAD), F32)],
        in_specs=[SMEM] + [VMEM] * 6,
        out_specs=[VMEM] * 3,
        scratch_shapes=[pltpu.VMEM((tokens, wide), BF16), pltpu.VMEM((HEAD, tokens), BF16)],
        compiler_params=pltpu.CompilerParams(vmem_limit_bytes=VMEM_LIMIT),
        cost_estimate=cost(25),
    )(runs, d_attended, queries, keys, values, mixed, lse)


def joined_back_kernel(
    heads, runs, raw, d_queries, d_keys, d_values, cosine, sine, q_gain, k_gain, share, d_joined, d_q_gain, d_k_gain, placed
):
    tokens = raw.shape[0]
    blocks = tokens // CONT
    wide = heads * CONT
    d_q_gain[...] = jnp.zeros_like(d_q_gain)
    d_k_gain[...] = jnp.zeros_like(d_k_gain)

    def step(block, carry):
        span_rows = pl.ds(pl.multiple_of(block * CONT, CONT), CONT)
        cos_rows = cosine[span_rows, :]
        sin_rows = sine[span_rows, :]

        def pull(value, grad, gain):
            grad = grad * cos_rows - swap_halves(grad) * sin_rows
            scale = lax.rsqrt(jnp.mean(value * value, axis=-1, keepdims=True) + EPS)
            scaled = value * scale
            gain_grad = jnp.sum(grad * scaled, axis=0, keepdims=True)
            grad = grad * gain
            return scale * (grad - scaled * jnp.mean(grad * scaled, axis=-1, keepdims=True)), gain_grad

        for head in range(heads):
            columns = slice(head * HEAD, (head + 1) * HEAD)
            grad, gain_grad = pull(
                raw[span_rows, columns], d_queries[span_rows, columns].astype(F32), q_gain[...]
            )
            placed[span_rows, columns] = grad.astype(BF16)
            d_q_gain[...] += gain_grad
        key_part, value_part = share[:1, :], share[1:, :]
        grad, gain_grad = pull(
            raw[span_rows, wide : wide + HEAD],
            (d_keys[span_rows, :] * SCALE).astype(BF16).astype(F32),
            k_gain[...],
        )
        placed[span_rows, wide : wide + HEAD] = (grad * key_part).astype(BF16)
        d_k_gain[...] += gain_grad * key_part
        placed[span_rows, wide + HEAD : wide + 2 * HEAD] = (d_values[span_rows, :] * value_part).astype(BF16)
        return carry

    lax.fori_loop(0, blocks, step, 0)

    def unsort(run, carry):
        origin = pl.multiple_of(run * RUN, RUN)
        place = pl.multiple_of(runs[run] * RUN, RUN)
        d_joined[pl.ds(origin, RUN), :] = placed[pl.ds(place, RUN), :]
        return carry

    lax.fori_loop(0, tokens // RUN, unsort, 0)


def attention_and_joined_back_kernel(
    heads,
    count,
    groups,
    runs,
    d_attended,
    queries,
    keys,
    values,
    mixed,
    lse,
    raw,
    cosine,
    sine,
    q_gain,
    k_gain,
    share,
    normed,
    d_out,
    d_joined,
    d_q_gain,
    d_k_gain,
    parts,
    d_queries,
    d_keys,
    d_values,
    arrived,
    keys_turned,
    raw_here,
    cosine_here,
    sine_here,
    placed,
    normed_slots,
    loaded,
    normed_in,
):
    columns = normed_slots.shape[2]

    def normed_copy(index):
        slot = lax.rem(index, 2)
        span_columns = pl.ds(pl.multiple_of(index * columns, columns), columns)
        return pltpu.make_async_copy(normed.at[:, span_columns], normed_slots.at[slot], normed_in.at[slot])

    loads = [
        pltpu.make_async_copy(source, target, loaded.at[index])
        for index, (source, target) in enumerate(
            [(raw, raw_here), (cosine, cosine_here), (sine, sine_here)]
        )
    ]
    for item in loads:
        item.start()
    normed_copy(0).start()
    attention_back_kernel(
        heads, runs, d_attended, queries, keys, values, mixed, lse, d_queries, d_keys, d_values, arrived, keys_turned
    )
    for item in loads:
        item.wait()
    joined_back_kernel(
        heads,
        runs,
        raw_here,
        d_queries,
        d_keys,
        d_values,
        cosine_here,
        sine_here,
        q_gain,
        k_gain,
        share,
        d_joined,
        d_q_gain,
        d_k_gain,
        placed,
    )
    rows = columns // groups
    width = d_joined.shape[1]

    def weight_grad(index, carry):
        @pl.when(index + 1 < count)
        def _():
            normed_copy(index + 1).start()

        normed_copy(index).wait()
        value = lax.dot_general(
            normed_slots[lax.rem(index, 2)], d_joined[...], (((0,), (0,)), ((), ())), preferred_element_type=F32
        ).astype(BF16)
        for owner in range(groups):
            parts[owner, index] = value[owner * rows : (owner + 1) * rows]
        return carry

    lax.fori_loop(0, count, weight_grad, 0)
    for owner in range(groups):
        for extra in range(d_out.shape[1] // width):
            parts[owner, count + extra] = d_out[
                owner * rows : (owner + 1) * rows, extra * width : (extra + 1) * width
            ]


def attention_and_joined_back(
    heads,
    count,
    groups,
    runs,
    d_attended,
    queries,
    keys,
    values,
    mixed,
    lse,
    raw,
    cosine,
    sine,
    q_gain,
    k_gain,
    share,
    normed,
    d_out,
):
    tokens = keys.shape[0]
    columns = normed.shape[1] // count
    blocks = count + d_out.shape[1] // raw.shape[1]
    wide = heads * CONT
    shape = jax.ShapeDtypeStruct
    return pl.pallas_call(
        functools.partial(attention_and_joined_back_kernel, heads, count, groups),
        out_shape=[
            shape(raw.shape, BF16),
            shape((1, HEAD), F32),
            shape((1, HEAD), F32),
            shape((groups, blocks, columns // groups, raw.shape[1]), BF16),
        ],
        in_specs=[SMEM] + [VMEM] * 6 + [ANY] * 3 + [VMEM] * 3 + [ANY, VMEM],
        out_specs=[VMEM] * 4,
        scratch_shapes=[
            pltpu.VMEM((tokens, wide), BF16),
            pltpu.VMEM((tokens, HEAD), F32),
            pltpu.VMEM((tokens, HEAD), F32),
            pltpu.VMEM((tokens, wide), BF16),
            pltpu.VMEM((HEAD, tokens), BF16),
            pltpu.VMEM(raw.shape, F32),
            pltpu.VMEM(cosine.shape, F32),
            pltpu.VMEM(sine.shape, F32),
            pltpu.VMEM(raw.shape, BF16),
            pltpu.VMEM((2, tokens, columns), BF16),
            DMA((3,)),
            DMA((2,)),
        ],
        compiler_params=pltpu.CompilerParams(vmem_limit_bytes=VMEM_LIMIT),
        cost_estimate=cost(30),
    )(runs, d_attended, queries, keys, values, mixed, lse, raw, cosine, sine, q_gain, k_gain, share, normed, d_out)


def joined_back(heads, runs, raw, d_queries, d_keys, d_values, cosine, sine, q_gain, k_gain, share):
    shape = jax.ShapeDtypeStruct
    return pl.pallas_call(
        functools.partial(joined_back_kernel, heads),
        out_shape=[shape(raw.shape, BF16), shape((1, HEAD), F32), shape((1, HEAD), F32)],
        in_specs=[SMEM] + [VMEM] * 9,
        out_specs=[VMEM] * 3,
        scratch_shapes=[pltpu.VMEM(raw.shape, BF16)],
        compiler_params=pltpu.CompilerParams(vmem_limit_bytes=VMEM_LIMIT),
        cost_estimate=cost(8),
    )(runs, raw, d_queries, d_keys, d_values, cosine, sine, q_gain, k_gain, share)


def rotary(tokens):
    index = np.arange(tokens)
    place = np.where(index < PROMPT, index, PROMPT + (index - PROMPT) % CONT).astype(np.float32)
    exponent = np.arange(HEAD // 2, dtype=np.float32) * np.float32(2.0 / HEAD)
    inverse = np.power(np.float32(ROPE_BASE), -exponent).astype(np.float32)
    angles = place[:, None] * inverse[None, :]
    cosine, sine = np.cos(angles), np.sin(angles)
    tables = np.concatenate([cosine, cosine], axis=1), np.concatenate([-sine, sine], axis=1)
    return tuple(jnp.asarray(table, F32) for table in tables)


def body(
    count,
    groups,
    hidden_in,
    segment_ids,
    positions,
    attn_gain,
    qkv_weight,
    query_norm_gain,
    k_gain,
    out_weight,
    mlp_gain,
    gate_up,
    down_weight,
    cotangent,
):
    hidden = hidden_in[0].astype(F32)
    rows, width = hidden.shape
    tokens = rows * count
    heads = QUERY_HEADS // count
    repeat = sharing(count)

    first = segment_ids[0, ::RUN]
    place = positions[0, ::RUN]
    order = jnp.where(first == 0, place, place + (first - 1) * CONT) // RUN
    runs = jnp.zeros((1, 8, 128), jnp.int32).at[0, 0, : rows // RUN].set(order)

    def gather_groups(values, axis):
        return lax.all_gather(values, "fsdp", axis=axis, tiled=True)

    def scatter_groups(values):
        return lax.psum_scatter(values, "fsdp", scatter_dimension=0, tiled=True)

    qkv_parts = spread_qkv(count, 1, qkv_weight, out_weight)
    gate_up, qkv_parts = lax.optimization_barrier((gate_up, qkv_parts))
    w_qkv = gather_groups(qkv_parts, 1)
    if merges(count, width):
        w_out = w_qkv[count:].transpose(1, 0, 2).reshape(-1, width)
        w_qkv = w_qkv[:count]
    else:
        w_out = gather_groups(out_weight, 0)
    w_qkv = w_qkv.reshape(width, -1)
    mlp_parts = spread_mlp(count, 5, gate_up)
    normed_local = norm_rows(hidden, attn_gain).astype(BF16)
    normed_local, mlp_parts = lax.optimization_barrier((normed_local, mlp_parts))
    normed, all_runs = opening(count, 2, normed_local, runs)
    w_qkv, normed, upstream = lax.optimization_barrier((w_qkv, normed, cotangent[0]))
    w_gu = gather_groups(mlp_parts, 1).reshape(width, -1)
    w_down = gather_groups(down_weight, 0)
    run_order = all_runs[:, 0, : rows // RUN].reshape(-1)
    cosine, sine = rotary(tokens)
    q_gain_row = query_norm_gain[None, :]
    k_gain_row = k_gain[None, :]

    blocks, masks = [upstream[None, : rows // 2], upstream[None, rows // 2 :]], [[0], [0]]
    chip_steps = len(bits_of(count)) - 1
    for step in range(chip_steps - 1):
        arrived, filled = gather_step(count, masks, blocks, step)
        if step == 0:
            joined = jnp.dot(normed, w_qkv, preferred_element_type=F32)
            joined, arrived = lax.optimization_barrier((joined, arrived))
        blocks = [jnp.concatenate(pair) for pair in zip(blocks, arrived)]
        masks = [held + more for held, more in zip(masks, filled)]
    arrived, filled = gather_step(count, masks, blocks, chip_steps - 1)
    attended, raw, queries, keys, values, mixed, lse = attention(
        heads, run_order, joined, cosine, sine, q_gain_row, k_gain_row
    )
    attended, arrived = lax.optimization_barrier((attended, arrived))
    middle, second, upstream = middle_and_second(
        count, 3, attended, w_out, hidden_in[0], mlp_gain[None, :], masks, blocks, filled, arrived
    )
    both = jnp.dot(second, w_gu, preferred_element_type=F32)
    own = both.shape[1] // 2
    gate, up = both[:, :own], both[:, own:]
    activated = (gate * jax.nn.sigmoid(gate) * up).astype(BF16)

    d_down = jnp.dot(activated.T, upstream, preferred_element_type=F32).astype(BF16)
    d_down, upstream = lax.optimization_barrier((d_down, upstream))
    d_down = scatter_groups(d_down)
    output, d_both, gu_parts = back_through_mlp(
        count, groups, 9, activated, w_down, middle, upstream, both, second
    )
    gu_parts, d_both = lax.optimization_barrier((gu_parts, d_both))
    gu_parts = scatter_groups(gu_parts.reshape((groups * count,) + gu_parts.shape[2:]))

    def weight_grad(left, right):
        grad = lax.dot_general(left, right, (((0,), (0,)), ((), ())), preferred_element_type=F32)
        grad = grad.astype(BF16).reshape(count, groups, -1, right.shape[1])
        return grad.transpose(1, 0, 2, 3).reshape(groups * count, -1, right.shape[1])

    d_middle, mlp_gain_grad, d_attended, d_out = back_through_middle(
        count, 6, d_both, w_gu, middle, cotangent[0], mlp_gain[None, :], attended, w_out
    )
    d_attended, d_down = lax.optimization_barrier((d_attended, d_down))
    share = jnp.ones((2, HEAD), F32)
    tables = (cosine, sine, q_gain_row, k_gain_row)
    if repeat == 1:
        d_joined, q_gain_grad, k_gain_grad, parts = attention_and_joined_back(
            heads,
            count,
            groups,
            run_order,
            d_attended,
            queries,
            keys,
            values,
            mixed,
            lse,
            raw,
            *tables,
            share,
            normed,
            d_out,
        )
        parts, gu_parts, d_joined = lax.optimization_barrier((parts, gu_parts, d_joined))
        qkv_grad_parts = scatter_groups(parts.reshape((-1,) + parts.shape[2:]))
    else:
        d_queries, d_keys, d_values = attention_back(
            heads, run_order, d_attended, queries, keys, values, mixed, lse
        )
        d_keys = d_keys + across(count, 1, d_keys)
        d_values = d_values + across(count, 1, d_values)
        mine = lax.rem(lax.axis_index("ctx"), 2) == jnp.arange(2)
        share = share * mine[:, None].astype(F32)
        d_joined, q_gain_grad, k_gain_grad = joined_back(
            heads, run_order, raw, d_queries, d_keys, d_values, *tables, share
        )
        d_out = scatter_groups(d_out)
        qkv_grad_parts = scatter_groups(weight_grad(normed, d_joined))
    d_hidden, attn_gain_grad, d_gate_up = back_to_input(
        count, 8, d_joined, w_qkv, hidden_in[0], d_middle, attn_gain[None, :], gu_parts
    )
    d_hidden, qkv_grad_parts = lax.optimization_barrier((d_hidden, qkv_grad_parts))

    gains = (attn_gain_grad, mlp_gain_grad, q_gain_grad, k_gain_grad)
    if repeat > 1:
        extra = jnp.zeros((1,) + qkv_grad_parts.shape[1:], BF16)
        qkv_grad_parts = jnp.concatenate([qkv_grad_parts, extra])
    *gains, d_qkv, out_rows = last(count, groups, 11, gains, qkv_grad_parts, qkv_weight.shape[1])
    if repeat == 1:
        d_out = out_rows
    return (
        output[None],
        d_hidden[None],
        gains[0].reshape(-1),
        d_qkv,
        gains[2].reshape(-1),
        gains[3].reshape(-1),
        d_out.astype(F32),
        gains[1].reshape(-1),
        d_gate_up.astype(F32),
        d_down.astype(F32),
    )


def solution(mesh):
    return jax.shard_map(
        functools.partial(body, mesh.shape["ctx"], mesh.shape["fsdp"]),
        mesh=mesh,
        in_specs=(
            P("fsdp", "ctx", None),
            P("fsdp", "ctx"),
            P("fsdp", "ctx"),
            P(),
            P(("ctx", "fsdp"), None),
            P(),
            P(),
            P(("ctx", "fsdp"), None),
            P(),
            P(("ctx", "fsdp"), None),
            P(("ctx", "fsdp"), None),
            P("fsdp", "ctx", None),
        ),
        out_specs=(
            P("fsdp", "ctx", None),
            P("fsdp", "ctx", None),
            P(),
            P(("ctx", "fsdp"), None),
            P(),
            P(),
            P(("ctx", "fsdp"), None),
            P(),
            P(("ctx", "fsdp"), None),
            P(("ctx", "fsdp"), None),
        ),
        check_vma=False,
    )
```

```python
import functools
import math

import jax
import jax.numpy as jnp
import numpy as np
from jax import lax
from jax.experimental import pallas as pl
from jax.experimental.pallas import tpu as pltpu
from jax.sharding import PartitionSpec as P

QUERY_HEADS = 16
KEY_VALUE_HEADS = 8
HEAD = 128
FF = 6144
PROMPT = 1024
CONT = 128
RUN = 32
EPS = 1e-06
ROPE_BASE = 1000000.0
SCALE = HEAD ** (-0.5)
SCALE2 = SCALE * math.log2(math.e)
MESH = pl.DeviceIdType.MESH
ANY = pl.BlockSpec(memory_space=pl.ANY)
VMEM = pl.BlockSpec(memory_space=pltpu.VMEM)
SMEM = pl.BlockSpec(memory_space=pltpu.SMEM)
BF16 = jnp.bfloat16
F32 = jnp.float32
DMA = pltpu.SemaphoreType.DMA
VMEM_LIMIT = 60 * 2**20


def cost(us):
    return pl.CostEstimate(flops=0, bytes_accessed=int(us * 1e6), transcendentals=0)


def flip(me, mask):
    result = me
    bit = 1
    while bit <= mask:
        if mask & bit:
            result = result + bit - 2 * bit * lax.rem(lax.div(me, bit), 2)
        bit *= 2
    return result


def bits_of(count):
    bits = []
    bit = 1
    while bit < count:
        bits.append(bit)
        bit *= 2
    return bits


def greet(peers):
    barrier = pltpu.get_barrier_semaphore()
    for peer in peers:
        pl.semaphore_signal(barrier, inc=1, device_id=peer, device_id_type=MESH)
    pl.semaphore_wait(barrier, len(peers))


def gather_orders(count):
    chip_bits = bits_of(count)[1:]
    return [chip_bits + [1], chip_bits[::-1] + [1]]


def last_bit(order, slot):
    return [bit for bit in order if slot & bit][-1]


def gather_rows(count, me, group, parts, source, target, send, recv, own=None):
    rows = target.shape[0] // count
    piece = rows // parts
    orders = gather_orders(count)
    copies = []

    def place(part, slot):
        return pl.multiple_of(flip(me, slot) * rows + part * piece, piece)

    def copy(part, slot, bit):
        there = target.at[pl.ds(place(part, slot), piece)]
        own_place = slot == 0 and source is not None
        origin = source.at[pl.ds(part * piece, piece)] if own_place else there
        number = part * count + (slot ^ bit)
        return pltpu.make_async_remote_copy(
            origin,
            there,
            send.at[number],
            recv.at[number],
            device_id=(flip(me, bit), group),
            device_id_type=MESH,
        )

    def keep(part):
        there = target.at[pl.ds(place(part, 0), piece)]
        return pltpu.make_async_copy(source.at[pl.ds(part * piece, piece)], there, own.at[part])

    def start(part):
        for bit in orders[part % 2]:
            item = copy(part, 0, bit)
            item.start()
            copies.append(item)
        if source is not None:
            keep(part).start()

    def wait(part, slot):
        there = target.at[pl.ds(place(part, slot), piece)]
        number = part * count + slot
        pltpu.make_async_remote_copy(
            there,
            there,
            send.at[number],
            recv.at[number],
            device_id=(flip(me, last_bit(orders[part % 2], slot)), group),
            device_id_type=MESH,
        ).wait_recv()

    def finish(arrived=None):
        waits = []
        for part in range(parts):
            order = orders[part % 2]
            for slot in range(1, count):
                last = order.index(last_bit(order, slot))
                waits.append((part // 2 + last, last, bin(slot).count("1"), part, slot))
        if arrived:
            for part in range(0, parts, 2):
                arrived(place(part, 0), 2 * piece)
        there = set()
        for _, last, _, part, slot in sorted(waits):
            wait(part, slot)
            for bit in orders[part % 2][last + 1 :]:
                item = copy(part, slot, bit)
                item.start()
                copies.append(item)
            there.add((part, slot))
            if arrived and (part ^ 1, slot) in there:
                arrived(place(part // 2 * 2, slot), 2 * piece)
        for part in range(parts):
            if source is not None:
                keep(part).wait()
        for item in copies:
            item.wait_send()

    return start, finish


def trade(count, me, group, pieces, source, target, send, recv):
    copies = []
    local = []

    def start(slots):
        for slot in slots:
            peer = flip(me, slot)
            for number, (origin, place) in enumerate(pieces(peer, me)):
                total = len(pieces(peer, me))
                index = slot * total + number
                if slot == 0:
                    item = pltpu.make_async_copy(source.at[origin], target.at[place], send.at[index])
                    local.append(item)
                else:
                    item = pltpu.make_async_remote_copy(
                        source.at[origin],
                        target.at[place],
                        send.at[index],
                        recv.at[index],
                        device_id=(peer, group),
                        device_id_type=MESH,
                    )
                    copies.append(item)
                item.start()

    def finish(arrived=None):
        for item in local:
            item.wait()
        if arrived:
            arrived(me)
        for slot in range(1, count):
            peer = flip(me, slot)
            listed = pieces(me, peer)
            for number, (origin, place) in enumerate(listed):
                index = slot * len(listed) + number
                pltpu.make_async_remote_copy(
                    source.at[origin],
                    target.at[place],
                    send.at[index],
                    recv.at[index],
                    device_id=(peer, group),
                    device_id_type=MESH,
                ).wait_recv()
            if arrived:
                arrived(peer)
        for item in copies:
            item.wait_send()

    return start, finish


def all_slots(count):
    return list(range(1, count)) + [0]


def span(start, width):
    return pl.ds(pl.multiple_of(start, HEAD), width)


def sharing(count):
    if count not in (KEY_VALUE_HEADS, QUERY_HEADS):
        raise ValueError(count)
    return count // KEY_VALUE_HEADS


def qkv_spans(count, device, gradients=False):
    own = QUERY_HEADS // count * HEAD
    repeat = sharing(count)
    queries = QUERY_HEADS * HEAD
    shared = lax.div(device, repeat) * HEAD
    if repeat == 2 and gradients:
        which = lax.rem(device, 2)
        return [
            (device * own, 0, own),
            (queries + which * (KEY_VALUE_HEADS * HEAD) + shared, own + which * HEAD, HEAD),
        ]
    return [
        (device * own, 0, own),
        (queries + shared, own, HEAD),
        (queries + KEY_VALUE_HEADS * HEAD + shared, own + HEAD, HEAD),
    ]


def mlp_spans(count, device, gradients=False):
    own = FF // count
    return [(device * own, 0, own), (FF + device * own, own, own)]


def outgoing(spans, count):
    def pieces(device, owner):
        return [
            ((slice(None), span(whole, width)), (owner, slice(None), pl.ds(part, width)))
            for whole, part, width in spans(count, device)
        ]

    return pieces


def incoming(device, owner):
    return [((device,), (owner,))]


def place_columns(count, spans, arrived, target):
    def place(peer):
        for whole, part, width in spans(count, peer, True):
            target[:, span(whole, width)] = arrived[peer, :, span(part, width)].astype(F32)

    return place


def everyone(count, me, group):
    return [(flip(me, slot), group) for slot in range(1, count)]


def spread_qkv_kernel(count, qkv, out, parts, send, recv, local):
    me = lax.axis_index("ctx")
    group = lax.axis_index("fsdp")
    width = parts.shape[2]
    greet(everyone(count, me, group))
    start, finish = trade(count, me, group, outgoing(qkv_spans, count), qkv, parts, send, recv)
    start(all_slots(count))
    items = [
        pltpu.make_async_copy(
            out.at[:, pl.ds(index * width, width)], parts.at[count + index], local.at[index]
        )
        for index in range(parts.shape[0] - count)
    ]
    for item in items:
        item.start()
    finish()
    for item in items:
        item.wait()


def spread_qkv(count, collective, qkv, out):
    rows = qkv.shape[0]
    width = qkv_width(count)
    extra = out.shape[1] // width if merges(count, out.shape[1]) else 0
    return pl.pallas_call(
        functools.partial(spread_qkv_kernel, count),
        out_shape=jax.ShapeDtypeStruct((count + extra, rows, width), BF16),
        in_specs=[ANY, VMEM],
        out_specs=ANY,
        scratch_shapes=[DMA((3 * count,)), DMA((3 * count,)), DMA((max(1, extra),))],
        compiler_params=pltpu.CompilerParams(collective_id=collective, has_side_effects=True),
        cost_estimate=cost(12),
    )(qkv, out)


def qkv_width(count):
    return QUERY_HEADS // count * HEAD + 2 * HEAD


def merges(count, width):
    return width % qkv_width(count) == 0


def spread_mlp_kernel(count, weight, parts, send, recv):
    me = lax.axis_index("ctx")
    group = lax.axis_index("fsdp")
    greet(everyone(count, me, group))
    start, finish = trade(count, me, group, outgoing(mlp_spans, count), weight, parts, send, recv)
    start(all_slots(count))
    finish()


def spread_mlp(count, collective, weight):
    return pl.pallas_call(
        functools.partial(spread_mlp_kernel, count),
        out_shape=jax.ShapeDtypeStruct((count, weight.shape[0], 2 * FF // count), BF16),
        in_specs=[ANY],
        out_specs=ANY,
        scratch_shapes=[DMA((2 * count,)), DMA((2 * count,))],
        compiler_params=pltpu.CompilerParams(collective_id=collective, has_side_effects=True),
        cost_estimate=cost(22),
    )(weight)


def opening_kernel(count, normed, runs, rows, all_runs, send, recv, own, run_send, run_recv):
    me = lax.axis_index("ctx")
    group = lax.axis_index("fsdp")
    greet(everyone(count, me, group))
    start, finish_runs = trade(
        count, me, group, lambda device, owner: [((0,), (owner,))], runs, all_runs, run_send, run_recv
    )
    start(all_slots(count))
    start, finish = gather_rows(count, me, group, 2, normed, rows, send, recv, own)
    start(0)
    start(1)
    finish()
    finish_runs()


def opening(count, collective, normed, runs):
    tokens, width = normed.shape
    return pl.pallas_call(
        functools.partial(opening_kernel, count),
        out_shape=[
            jax.ShapeDtypeStruct((count * tokens, width), BF16),
            jax.ShapeDtypeStruct((count, 8, 128), jnp.int32),
        ],
        in_specs=[VMEM, ANY],
        out_specs=[ANY, ANY],
        scratch_shapes=[DMA((2 * count,)), DMA((2 * count,)), DMA((2,)), DMA((count,)), DMA((count,))],
        compiler_params=pltpu.CompilerParams(collective_id=collective, has_side_effects=True),
        cost_estimate=cost(45),
    )(normed, runs)


def across(count, bit, values):
    return lax.ppermute(values, "ctx", [(index, index ^ bit) for index in range(count)])


def join_rows(count, me, group, slots, blocks, target, send, recv, local):
    other = flip(me, 1)
    half = blocks[0].shape[1]
    items = []
    for block, (part, masks) in zip(blocks, slots):
        items += [(block, index, part, mask) for index, mask in enumerate(masks)]

    def place(number, owner):
        _, _, part, mask = items[number]
        return pl.ds(pl.multiple_of(flip(owner, mask) * 2 * half + part * half, half), half)

    def copy(number, owner):
        block, index = items[number][:2]
        return pltpu.make_async_remote_copy(
            block.at[index],
            target.at[place(number, owner)],
            send.at[number],
            recv.at[number],
            device_id=(other, group),
            device_id_type=MESH,
        )

    def keep(number):
        block, index = items[number][:2]
        return pltpu.make_async_copy(block.at[index], target.at[place(number, me)], local.at[number])

    def start():
        for number in range(len(items)):
            copy(number, me).start()
            keep(number).start()

    def finish():
        for number in range(len(items)):
            keep(number).wait()
            copy(number, other).wait_recv()
            copy(number, me).wait_send()

    return start, finish


def gather_step(count, masks, blocks, step):
    arrived, filled = [], []
    for part, order in enumerate(gather_orders(count)):
        arrived.append(across(count, order[step], blocks[part]))
        filled.append([mask ^ order[step] for mask in masks[part]])
    return arrived, filled


def last_kernel(
    count,
    groups,
    attn_part,
    mlp_part,
    q_part,
    k_part,
    parts,
    attn_gain,
    mlp_gain,
    q_gain,
    k_gain,
    d_qkv,
    d_out,
    columns,
    out_parts,
    values,
    near,
    far,
    send,
    recv,
    far_send,
    far_recv,
    part_send,
    part_recv,
    out_in,
):
    me = lax.axis_index("ctx")
    group = lax.axis_index("fsdp")
    others = [lax.rem(group + step, groups) for step in range(1, groups)]
    greet(everyone(count, me, group) + [(me, other) for other in others])
    fetched = fetch([parts.at[pl.ds(count, out_parts.shape[0])]], [out_parts], out_in)
    rows = attn_gain.shape[0]
    for row in range(rows):
        values[row : row + 1] = attn_part[:, row * 128 : (row + 1) * 128]
        values[rows + row : rows + row + 1] = mlp_part[:, row * 128 : (row + 1) * 128]
    values[2 * rows : 2 * rows + 1] = q_part[...]
    values[2 * rows + 1 : 2 * rows + 2] = k_part[...]
    values[2 * rows + 2 :] = jnp.zeros((6, 128), F32)
    copies = []
    for slot in range(1, count):
        item = pltpu.make_async_remote_copy(
            values,
            near.at[me],
            send.at[slot],
            recv.at[slot],
            device_id=(flip(me, slot), group),
            device_id_type=MESH,
        )
        item.start()
        copies.append(item)
    start, finish = trade(count, me, group, incoming, parts, columns, part_send, part_recv)
    start(all_slots(count))
    near[me] = values[...]
    for item in copies:
        item.wait()
    summed = near[0]
    for index in range(1, count):
        summed = summed + near[index]
    far[group] = summed
    copies = []
    for step, other in enumerate(others):
        item = pltpu.make_async_remote_copy(
            far.at[group],
            far.at[group],
            far_send.at[step],
            far_recv.at[step],
            device_id=(me, other),
            device_id_type=MESH,
        )
        item.start()
        copies.append(item)
    for item in copies:
        item.wait()
    summed = far[0]
    for index in range(1, groups):
        summed = summed + far[index]
    attn_gain[...] = summed[:rows]
    mlp_gain[...] = summed[rows : 2 * rows]
    q_gain[...] = summed[2 * rows : 2 * rows + 1]
    k_gain[...] = summed[2 * rows + 1 : 2 * rows + 2]
    fetched()
    width = out_parts.shape[2]
    for index in range(out_parts.shape[0]):
        d_out[:, index * width : (index + 1) * width] = out_parts[index].astype(F32)
    finish(place_columns(count, qkv_spans, columns, d_qkv))


def last(count, groups, collective, gains, parts, columns):
    width = gains[0].shape[1]
    rows = width // 128
    shape = (2 * rows + 8, 128)
    long, short = (rows, 128), (1, 128)
    out_shape = (parts.shape[0] - count,) + parts.shape[1:]
    return pl.pallas_call(
        functools.partial(last_kernel, count, groups),
        out_shape=[jax.ShapeDtypeStruct(size, F32) for size in (long, long, short, short)]
        + [
            jax.ShapeDtypeStruct((parts.shape[1], columns), F32),
            jax.ShapeDtypeStruct((parts.shape[1], out_shape[0] * out_shape[2]), F32),
        ],
        in_specs=[VMEM] * 4 + [ANY],
        out_specs=[VMEM] * 6,
        scratch_shapes=[
            pltpu.VMEM((count,) + parts.shape[1:], BF16),
            pltpu.VMEM(out_shape, BF16),
            pltpu.VMEM(shape, F32),
            pltpu.VMEM((count,) + shape, F32),
            pltpu.VMEM((groups,) + shape, F32),
            DMA((count,)),
            DMA((count,)),
            DMA((groups,)),
            DMA((groups,)),
            DMA((count,)),
            DMA((count,)),
            DMA((1,)),
        ],
        compiler_params=pltpu.CompilerParams(collective_id=collective, has_side_effects=True),
        cost_estimate=cost(14),
    )(*gains, parts)


def product_slots(count):
    slots = []
    for pair in range(count // 2)[::-1]:
        slots += [2 * pair - 1, 2 * pair] if slots and pair else [2 * pair + 1, 2 * pair - 1, 2 * pair] if pair else [0]
    return slots


def load_operands(count, me, flipped, left_from, right_from, left, right, left_in, right_in):
    rows = left.shape[0] // count
    width = right.shape[0] if flipped else right.shape[1]
    tile = min(512, width)

    def left_copy(slot):
        span_rows = pl.ds(pl.multiple_of(flip(me, slot) * rows, rows), rows)
        return pltpu.make_async_copy(left_from.at[span_rows], left.at[span_rows], left_in.at[slot])

    def right_copy(index):
        span_tile = pl.ds(pl.multiple_of(index * tile, tile), tile)
        place = (span_tile,) if flipped else (slice(None), span_tile)
        return pltpu.make_async_copy(right_from.at[place], right.at[place], right_in.at[index])

    slots = product_slots(count)
    right_copy(0).start()
    left_copy(slots[0]).start()
    for index in range(1, width // tile):
        right_copy(index).start()
    for slot in slots[1:]:
        left_copy(slot).start()
    return lambda slot: left_copy(slot).wait(), lambda index: right_copy(index).wait()


def operand_scratch(count, left, right, flipped):
    width = right.shape[0] if flipped else right.shape[1]
    return [
        pltpu.VMEM(left.shape, BF16),
        pltpu.VMEM(right.shape, BF16),
        DMA((count,)),
        DMA((width // min(512, width),)),
    ]


def fetch(sources, targets, arrived):
    items = [
        pltpu.make_async_copy(source, target, arrived.at[index])
        for index, (source, target) in enumerate(zip(sources, targets))
    ]
    for item in items:
        item.start()

    def wait():
        for item in items:
            item.wait()

    return wait


def product_scatter(
    count,
    me,
    group,
    parts,
    flipped,
    left,
    right,
    done,
    kept,
    near_out,
    near_in,
    far_out,
    far_in,
    ns,
    nr,
    fs,
    fr,
    ready=None,
):
    rows, width = kept.shape
    piece = rows // parts
    bits = bits_of(count)
    orders = [bits[1:][::-1], bits[1:]]
    tile = min(512, width)
    pairs = list(range(count // 2))[::-1]

    def product(slot, store):
        start = pl.multiple_of(flip(me, slot) * rows, rows)
        if ready:
            ready[0](slot)
        block = left[pl.ds(start, rows), :]

        def step(index, carry):
            columns = pl.ds(pl.multiple_of(index * tile, tile), tile)
            if ready and slot == count - 1:
                ready[1](index)
            if flipped:
                value = nt(block, right[columns, :])
            else:
                value = jnp.dot(block, right[:, columns], preferred_element_type=F32)
            store(columns, value)
            return carry

        lax.fori_loop(0, width // tile, step, 0)

    def first(part, slot):
        return [bit for bit in orders[part % 2] if slot & bit][0]

    def near(pair):
        return pltpu.make_async_remote_copy(
            near_out.at[pair],
            near_in.at[pair],
            ns.at[pair],
            nr.at[pair],
            device_id=(flip(me, 1), group),
            device_id_type=MESH,
        )

    def number(part, pair):
        return part * (count // 2 - 1) + pair - 1

    def far(part, pair):
        index = number(part, pair)
        return pltpu.make_async_remote_copy(
            far_out.at[index],
            far_in.at[index],
            fs.at[index],
            fr.at[index],
            device_id=(flip(me, first(part, 2 * pair)), group),
            device_id_type=MESH,
        )

    def needs(part, pair):
        found = []
        for bit in orders[part % 2]:
            if 2 * pair & bit:
                break
            found.append((2 * pair ^ bit) // 2)
        return found

    def settle(part, pair):
        if pair == 0:
            value = kept[pl.ds(part * piece, piece), :]
        else:
            value = far_out[number(part, pair)].astype(F32)
        for other in needs(part, pair):
            far(part, other).wait_recv()
            value = value + far_in[number(part, other)].astype(F32)
        if pair == 0:
            done(part, value)
        else:
            far_out[number(part, pair)] = value.astype(BF16)
            far(part, pair).start()

    def send_near(pair):
        def store(columns, value):
            near_out[pair, :, columns] = value.astype(BF16)

        product(2 * pair + 1, store)
        near(pair).start()

    def batch_parts(batch):
        return (2 * batch, 2 * batch + 1)

    def send_pair(batch, pair):
        for part in batch_parts(batch):
            if pair and not needs(part, pair):
                far(part, pair).start()

    def sum_near(pair):
        near(pair).wait_recv()

        def store(columns, value):
            value = value + near_in[pair, :, columns].astype(F32)
            if pair == 0:
                kept[:, columns] = value
            else:
                for part in range(parts):
                    far_out[number(part, pair), :, columns] = value[
                        part * piece : (part + 1) * piece
                    ].astype(BF16)

        product(2 * pair, store)
        send_pair(0, pair)

    def begin():
        send_near(pairs[0])
        for pair in pairs:
            if pair:
                send_near(pair - 1)
            sum_near(pair)

    def send(batch):
        for pair in pairs:
            send_pair(batch, pair)

    def pass_on(batch):
        for pair in pairs:
            for part in batch_parts(batch):
                if pair and needs(part, pair):
                    settle(part, pair)

    def end(batch):
        for part in batch_parts(batch):
            settle(part, 0)

    def close():
        for pair in pairs:
            near(pair).wait_send()
            for part in range(parts):
                if pair:
                    far(part, pair).wait_send()

    return begin, send, pass_on, end, close


def scatter_scratch(count, rows, width, parts=2):
    pairs = count // 2
    links = parts * (pairs - 1)
    return [
        pltpu.VMEM((rows, width), F32),
        pltpu.VMEM((pairs, rows, width), BF16),
        pltpu.VMEM((pairs, rows, width), BF16),
        pltpu.VMEM((links, rows // parts, width), BF16),
        pltpu.VMEM((links, rows // parts, width), BF16),
        DMA((pairs,)),
        DMA((pairs,)),
        DMA((links,)),
        DMA((links,)),
    ]


SCATTER = 9
PARTS = 4
BACK_PARTS = 2


def comm_params(collective):
    return pltpu.CompilerParams(
        collective_id=collective, has_side_effects=True, vmem_limit_bytes=VMEM_LIMIT
    )


def row_blocks(first, count, step):
    def body(index, carry):
        step(pl.multiple_of(first + index * 32, 32), pl.multiple_of(index * 32, 32))
        return carry

    lax.fori_loop(0, count // 32, body, 0)


def norm_back(values, gain, grad):
    scale = lax.rsqrt(jnp.mean(values * values, axis=-1, keepdims=True) + EPS)
    scaled = values * scale
    pushed = grad * gain
    back = scale * (pushed - scaled * jnp.mean(pushed * scaled, axis=-1, keepdims=True))
    return back, jnp.sum(grad * scaled, axis=0, keepdims=True)


def norm_rows(values, gain):
    return values * lax.rsqrt(jnp.mean(values * values, axis=-1, keepdims=True) + EPS) * gain


def middle_kernel(count, slots, left, right, hidden, gain, *refs):
    held, refs = refs[: len(slots)], refs[len(slots) :]
    (middle, gathered, joined, own_rows, sums), refs = refs[:5], refs[5:]
    blocks, refs = refs[: len(slots)], refs[len(slots) :]
    (held_in, send, recv, local), scratch = refs[:4], refs[4:]
    me = lax.axis_index("ctx")
    group = lax.axis_index("fsdp")
    piece = middle.shape[0] // PARTS
    fetched = fetch(held, blocks, held_in)
    greet([(flip(me, bit), group) for bit in bits_of(count)])
    start, finish = gather_rows(count, me, group, PARTS, own_rows, gathered, *scratch[SCATTER:])
    start_join, finish_join = join_rows(count, me, group, slots, blocks, joined, send, recv, local)

    def done(part, value):
        sums[...] = value

        def step(row, place):
            total_rows = hidden[pl.ds(row, 32), :].astype(F32) + sums[pl.ds(place, 32), :]
            middle[pl.ds(row, 32), :] = total_rows
            own_rows[pl.ds(row, 32), :] = norm_rows(total_rows, gain[...]).astype(BF16)

        row_blocks(part * piece, piece, step)
        start(part)

    begin, send_batch, pass_on, end, close = product_scatter(
        count, me, group, PARTS, False, left, right, done, *scratch[:SCATTER]
    )
    begin()
    fetched()
    start_join()
    pass_on(0)
    send_batch(1)
    end(0)
    pass_on(1)
    end(1)
    finish()
    finish_join()
    close()


def gather_scratch(count, parts):
    return [DMA((parts * count,)), DMA((parts * count,)), DMA((parts,))]


def middle_and_second(count, collective, left, right, hidden, gain, masks, blocks, filled, arrived):
    rows, width = hidden.shape
    slots, held = [], []
    for part in (0, 1):
        slots += [(part, masks[part]), (part, filled[part])]
        held += [blocks[part], arrived[part]]
    return pl.pallas_call(
        functools.partial(middle_kernel, count, slots),
        out_shape=[
            jax.ShapeDtypeStruct((rows, width), F32),
            jax.ShapeDtypeStruct((count * rows, width), BF16),
            jax.ShapeDtypeStruct((count * rows, width), BF16),
        ],
        in_specs=[VMEM] * 4 + [ANY] * len(held),
        out_specs=[VMEM, ANY, ANY],
        scratch_shapes=[pltpu.VMEM((rows, width), BF16), pltpu.VMEM((rows // PARTS, width), F32)]
        + [pltpu.VMEM(block.shape, BF16) for block in held]
        + [DMA((len(held),)), DMA((count,)), DMA((count,)), DMA((count,))]
        + scatter_scratch(count, rows, width, PARTS)
        + gather_scratch(count, PARTS),
        compiler_params=comm_params(collective),
        cost_estimate=cost(80),
    )(left, right, hidden, gain, *held)


def back_kernel(
    count,
    left_from,
    right_from,
    middle_from,
    cotangent_from,
    gain,
    attended_from,
    out_weight_from,
    d_middle,
    d_gain,
    d_attended,
    d_out,
    sums,
    gathered,
    turned,
    out_sum,
    left,
    right,
    left_in,
    right_in,
    middle,
    cotangent,
    attended,
    out_weight,
    others_in,
    *scratch,
):
    me = lax.axis_index("ctx")
    group = lax.axis_index("fsdp")
    piece = middle.shape[0] // BACK_PARTS
    own = me * middle.shape[0]
    ready = load_operands(count, me, True, left_from, right_from, left, right, left_in, right_in)
    fetched = fetch(
        (middle_from, cotangent_from, attended_from, out_weight_from),
        (middle, cotangent, attended, out_weight),
        others_in,
    )
    greet([(flip(me, bit), group) for bit in bits_of(count)])
    start, finish = gather_rows(count, me, group, BACK_PARTS, None, gathered, *scratch[SCATTER:])
    d_gain[...] = jnp.zeros_like(d_gain)

    def done(part, value):
        sums[...] = value

        def step(row, place):
            span_rows = pl.ds(row, 32)
            back, gain_part = norm_back(middle[span_rows, :], gain[...], sums[pl.ds(place, 32), :])
            back = back + cotangent[span_rows, :].astype(F32)
            d_middle[span_rows, :] = back
            gathered[pl.ds(pl.multiple_of(own + row, 32), 32), :] = back.astype(BF16)
            d_gain[...] += gain_part

        row_blocks(part * piece, piece, step)
        start(part)

    begin, _, pass_on, end, close = product_scatter(
        count, me, group, BACK_PARTS, True, left, right, done, *scratch[:SCATTER], ready=ready
    )
    begin()
    fetched()
    out_sum[...] = jnp.zeros_like(out_sum)

    def turn(index, carry):
        span_rows = pl.ds(pl.multiple_of(index * 256, 256), 256)
        turned[:, span_rows] = attended[span_rows, :].astype(F32).T.astype(BF16)
        return carry

    lax.fori_loop(0, attended.shape[0] // 256, turn, 0)
    pass_on(0)
    end(0)

    def arrived(row, size):
        block = gathered[pl.ds(row, size), :]
        d_attended[pl.ds(row, size), :] = nt(block, out_weight[...]).astype(BF16)
        if size % 128 == 0:
            out_sum[...] += jnp.dot(turned[:, pl.ds(row, size)], block, preferred_element_type=F32)

    finish(arrived)
    close()
    if 2 * piece % 128:
        out_sum[...] = jnp.dot(turned[...], gathered[...], preferred_element_type=F32)
    d_out[...] = out_sum[...].astype(BF16)


def back_through_middle(count, collective, left, right, middle, cotangent, gain, attended, out_weight):
    rows, width = middle.shape
    tokens, wide = attended.shape
    shape = jax.ShapeDtypeStruct
    return pl.pallas_call(
        functools.partial(back_kernel, count),
        out_shape=[
            shape((rows, width), F32),
            shape((1, width), F32),
            shape((tokens, wide), BF16),
            shape((wide, width), BF16),
        ],
        in_specs=[ANY] * 4 + [VMEM] + [ANY] * 2,
        out_specs=[VMEM] * 4,
        scratch_shapes=[
            pltpu.VMEM((rows // BACK_PARTS, width), F32),
            pltpu.VMEM((tokens, width), BF16),
            pltpu.VMEM((wide, tokens), BF16),
            pltpu.VMEM((wide, width), F32),
        ]
        + operand_scratch(count, left, right, True)
        + [
            pltpu.VMEM((rows, width), F32),
            pltpu.VMEM((rows, width), BF16),
            pltpu.VMEM((tokens, wide), BF16),
            pltpu.VMEM((wide, width), BF16),
            DMA((4,)),
        ]
        + scatter_scratch(count, rows, width, BACK_PARTS)
        + gather_scratch(count, BACK_PARTS)[:2],
        compiler_params=comm_params(collective),
        cost_estimate=cost(85),
    )(left, right, middle, cotangent, gain, attended, out_weight)


def input_kernel(
    count,
    left_from,
    right_from,
    hidden_from,
    d_middle_from,
    gain,
    parts,
    d_hidden,
    d_gain,
    d_gate_up,
    columns,
    left,
    right,
    left_in,
    right_in,
    hidden,
    d_middle,
    others_in,
    sums,
    send,
    recv,
    *scratch,
):
    me = lax.axis_index("ctx")
    group = lax.axis_index("fsdp")
    half = hidden.shape[0] // 2
    ready = load_operands(count, me, True, left_from, right_from, left, right, left_in, right_in)
    fetched = fetch((hidden_from, d_middle_from), (hidden, d_middle), others_in)
    greet(everyone(count, me, group))
    start, finish = trade(count, me, group, incoming, parts, columns, send, recv)
    early = [0, 1, 2, 4]
    start(early)
    d_gain[...] = jnp.zeros_like(d_gain)

    def done(part, value):
        sums[...] = value

        def step(row, place):
            span_rows = pl.ds(row, 32)
            values = hidden[span_rows, :].astype(F32)
            back, gain_part = norm_back(values, gain[...], sums[pl.ds(place, 32), :])
            d_hidden[span_rows, :] = d_middle[span_rows, :] + back
            d_gain[...] += gain_part

        row_blocks(part * half, half, step)

    begin, _, pass_on, end, close = product_scatter(
        count, me, group, 2, True, left, right, done, *scratch, ready=ready
    )
    begin()
    fetched()
    pass_on(0)
    start([slot for slot in range(count) if slot not in early])
    end(0)
    finish(place_columns(count, mlp_spans, columns, d_gate_up))
    close()


def back_to_input(count, collective, left, right, hidden, d_middle, gain, parts):
    rows, width = hidden.shape
    shape = jax.ShapeDtypeStruct
    return pl.pallas_call(
        functools.partial(input_kernel, count),
        out_shape=[
            shape((rows, width), F32),
            shape((1, width), F32),
            shape((parts.shape[1], 2 * FF), F32),
        ],
        in_specs=[ANY] * 4 + [VMEM, ANY],
        out_specs=[VMEM] * 3,
        scratch_shapes=[pltpu.VMEM(parts.shape, BF16)]
        + operand_scratch(count, left, right, True)
        + [
            pltpu.VMEM((rows, width), BF16),
            pltpu.VMEM((rows, width), F32),
            DMA((2,)),
            pltpu.VMEM((rows // 2, width), F32),
            DMA((count,)),
            DMA((count,)),
        ]
        + scatter_scratch(count, rows, width),
        compiler_params=comm_params(collective),
        cost_estimate=cost(60),
    )(left, right, hidden, d_middle, gain, parts)


def mlp_kernel(
    count,
    groups,
    activated_from,
    weight_from,
    middle_from,
    upstream,
    both,
    second,
    output,
    d_both,
    parts,
    up_slots,
    both_slots,
    second_slots,
    part_slots,
    up_in,
    both_in,
    second_in,
    parts_out,
    activated,
    weight,
    activated_in,
    weight_in,
    middle,
    others_in,
    *scratch,
):
    me = lax.axis_index("ctx")
    group = lax.axis_index("fsdp")
    half = middle.shape[0] // 2
    tokens, own = activated.shape
    block = up_slots.shape[1]
    columns = second_slots.shape[2]
    ready = load_operands(
        count, me, False, activated_from, weight_from, activated, weight, activated_in, weight_in
    )
    fetched = fetch((middle_from,), (middle,), others_in)
    greet([(flip(me, bit), group) for bit in bits_of(count)])

    def rows_in(index):
        slot = lax.rem(index, 4)
        rows = pl.ds(pl.multiple_of(index * block, block), block)
        return (
            pltpu.make_async_copy(upstream.at[rows], up_slots.at[slot], up_in.at[slot]),
            pltpu.make_async_copy(both.at[rows], both_slots.at[slot], both_in.at[slot]),
        )

    def second_copy(index):
        slot = lax.rem(index, 2)
        span_columns = pl.ds(pl.multiple_of(index * columns, columns), columns)
        return pltpu.make_async_copy(second.at[:, span_columns], second_slots.at[slot], second_in.at[slot])

    def part_copies(index):
        slot = lax.rem(index, 2)
        rows = columns // groups
        return [
            pltpu.make_async_copy(
                part_slots.at[slot, pl.ds(owner * rows, rows)],
                parts.at[owner, index],
                parts_out.at[slot, owner],
            )
            for owner in range(groups)
        ]

    for item in rows_in(0) + rows_in(1):
        item.start()
    second_copy(0).start()

    def done(part, value):
        span_rows = pl.ds(part * half, half)
        output[span_rows, :] = (middle[span_rows, :] + value).astype(BF16)

    begin, _, pass_on, end, close = product_scatter(
        count, me, group, 2, False, activated, weight, done, *scratch, ready=ready
    )
    begin()
    fetched()
    steps = tokens // block

    def activation(index, carry):
        @pl.when(2 * index + 2 < steps)
        def _():
            for item in rows_in(2 * index + 2) + rows_in(2 * index + 3):
                item.start()

        for item in rows_in(2 * index) + rows_in(2 * index + 1):
            item.wait()
        slots = [lax.rem(2 * index + turn, 4) for turn in (0, 1)]
        grads = [nt(up_slots[slot], weight[...]).astype(BF16).astype(F32) for slot in slots]
        for turn, (slot, grad) in enumerate(zip(slots, grads)):
            rows = pl.ds(pl.multiple_of((2 * index + turn) * block, block), block)
            gate = both_slots[slot, :, :own]
            up = both_slots[slot, :, own:]
            sigmoid = 1.0 / (1.0 + jnp.exp(-gate))
            d_both[rows, :own] = (grad * up * sigmoid * (1.0 + gate * (1.0 - sigmoid))).astype(BF16)
            d_both[rows, own:] = (grad * gate * sigmoid).astype(BF16)
        return carry

    lax.fori_loop(0, steps // 2, activation, 0)

    def weight_grad(index, carry):
        @pl.when(index + 1 < count)
        def _():
            second_copy(index + 1).start()

        second_copy(index).wait()

        @pl.when(index >= 2)
        def _():
            for item in part_copies(index - 2):
                item.wait()

        slot = lax.rem(index, 2)
        value = lax.dot_general(
            second_slots[slot], d_both[...], (((0,), (0,)), ((), ())), preferred_element_type=F32
        )
        part_slots[slot] = value.astype(BF16)
        for item in part_copies(index):
            item.start()
        return carry

    lax.fori_loop(0, count // 2, weight_grad, 0)
    pass_on(0)
    lax.fori_loop(count // 2, count, weight_grad, 0)
    for index in (count - 2, count - 1):
        for item in part_copies(index):
            item.wait()
    end(0)
    close()


def back_through_mlp(count, groups, collective, activated, weight, middle, upstream, both, second):
    rows, width = middle.shape
    tokens, own = activated.shape
    block = 256
    columns = width // count
    shape = jax.ShapeDtypeStruct
    return pl.pallas_call(
        functools.partial(mlp_kernel, count, groups),
        out_shape=[
            shape((rows, width), BF16),
            shape((tokens, 2 * own), BF16),
            shape((groups, count, columns // groups, 2 * own), BF16),
        ],
        in_specs=[ANY] * 6,
        out_specs=[VMEM, VMEM, ANY],
        scratch_shapes=[
            pltpu.VMEM((4, block, width), BF16),
            pltpu.VMEM((4, block, 2 * own), F32),
            pltpu.VMEM((2, tokens, columns), BF16),
            pltpu.VMEM((2, columns, 2 * own), BF16),
            DMA((4,)),
            DMA((4,)),
            DMA((2,)),
            DMA((2, groups)),
        ]
        + operand_scratch(count, activated, weight, False)
        + [pltpu.VMEM((rows, width), F32), DMA((1,))]
        + scatter_scratch(count, rows, width),
        compiler_params=comm_params(collective),
        cost_estimate=cost(48),
    )(activated, weight, middle, upstream, both, second)


def swap_halves(value):
    return jnp.concatenate([value[:, HEAD // 2 :], value[:, : HEAD // 2]], axis=1)


def nt(left, right):
    return lax.dot_general(left, right, (((1,), (1,)), ((), ())), preferred_element_type=F32)


def causal(keys, queries):
    key = lax.broadcasted_iota(jnp.int32, (keys, queries), 0)
    query = lax.rem(lax.broadcasted_iota(jnp.int32, (keys, queries), 1), CONT)
    return key <= query


def attention_kernel(
    heads, runs, joined, cosine, sine, q_gain, k_gain, attended, raw, queries, keys, values, mixed, lse, turned, placed
):
    tokens = joined.shape[0]
    blocks = tokens // CONT
    wide = heads * CONT

    def sort(run, carry):
        origin = pl.multiple_of(run * RUN, RUN)
        place = pl.multiple_of(runs[run] * RUN, RUN)
        raw[pl.ds(place, RUN), :] = joined[pl.ds(origin, RUN), :]
        return carry

    lax.fori_loop(0, tokens // RUN, sort, 0)

    def prepare(block, carry):
        span_rows = pl.ds(pl.multiple_of(block * CONT, CONT), CONT)
        cos_rows = cosine[span_rows, :]
        sin_rows = sine[span_rows, :]

        def turn(value, gain):
            value = value * lax.rsqrt(jnp.mean(value * value, axis=-1, keepdims=True) + EPS) * gain
            return (value * cos_rows + swap_halves(value) * sin_rows).astype(BF16)

        for head in range(heads):
            piece = raw[span_rows, head * HEAD : (head + 1) * HEAD]
            queries[block, head * CONT : (head + 1) * CONT, :] = turn(piece, q_gain[...])
        keys[span_rows, :] = turn(raw[span_rows, wide : wide + HEAD], k_gain[...])
        piece = raw[span_rows, wide + HEAD : wide + 2 * HEAD]
        values[span_rows, :] = piece.astype(BF16)
        turned[:, span_rows] = piece.T.astype(BF16)
        return carry

    lax.fori_loop(0, blocks, prepare, 0)

    def attend(block, own, before):
        query = queries[block]
        own_rows = pl.ds(own, CONT)
        weight = jnp.exp2(nt(keys[own_rows, :], query) * SCALE2)
        weight = jnp.where(causal(CONT, wide), weight, 0.0)
        sums = jnp.sum(weight, axis=0, keepdims=True)
        out = jnp.dot(turned[:, own_rows], weight.astype(BF16), preferred_element_type=F32)
        if before:
            weight = jnp.exp2(nt(keys[:before, :], query) * SCALE2)
            sums = sums + jnp.sum(weight, axis=0, keepdims=True)
            out = out + jnp.dot(turned[:, :before], weight.astype(BF16), preferred_element_type=F32)
        out = out / sums
        mixed[block] = out
        lse[block] = jnp.broadcast_to(jnp.log2(sums), (8, wide))
        for head in range(heads):
            placed[own_rows, head * HEAD : (head + 1) * HEAD] = out[
                :, head * CONT : (head + 1) * CONT
            ].T.astype(BF16)

    for block in range(PROMPT // CONT):
        attend(block, block * CONT, block * CONT)

    def continuation(block, carry):
        attend(block, pl.multiple_of(block * CONT, CONT), PROMPT)
        return carry

    lax.fori_loop(PROMPT // CONT, blocks, continuation, 0)

    def unsort(run, carry):
        origin = pl.multiple_of(run * RUN, RUN)
        place = pl.multiple_of(runs[run] * RUN, RUN)
        attended[pl.ds(origin, RUN), :] = placed[pl.ds(place, RUN), :]
        return carry

    lax.fori_loop(0, tokens // RUN, unsort, 0)


def attention(heads, runs, joined, cosine, sine, q_gain, k_gain):
    tokens = joined.shape[0]
    blocks = tokens // CONT
    wide = heads * CONT
    shape = jax.ShapeDtypeStruct
    return pl.pallas_call(
        functools.partial(attention_kernel, heads),
        out_shape=[
            shape((tokens, wide), BF16),
            shape(joined.shape, F32),
            shape((blocks, wide, HEAD), BF16),
            shape((tokens, HEAD), BF16),
            shape((tokens, HEAD), BF16),
            shape((blocks, HEAD, wide), F32),
            shape((blocks, 8, wide), F32),
        ],
        in_specs=[SMEM, VMEM, VMEM, VMEM, VMEM, VMEM],
        out_specs=[VMEM] * 7,
        scratch_shapes=[pltpu.VMEM((HEAD, tokens), BF16), pltpu.VMEM((tokens, wide), BF16)],
        compiler_params=pltpu.CompilerParams(vmem_limit_bytes=VMEM_LIMIT),
        cost_estimate=cost(15),
    )(runs, joined, cosine, sine, q_gain, k_gain)


def attention_back_kernel(
    heads,
    runs,
    d_attended,
    queries,
    keys,
    values,
    mixed,
    lse,
    d_queries,
    d_keys,
    d_values,
    arrived,
    keys_turned,
    ready=None,
):
    tokens = keys.shape[0]
    blocks = tokens // CONT
    wide = heads * CONT

    def sort(run, carry):
        origin = pl.multiple_of(run * RUN, RUN)
        place = pl.multiple_of(runs[run] * RUN, RUN)
        arrived[pl.ds(place, RUN), :] = d_attended[pl.ds(origin, RUN), :]
        return carry

    lax.fori_loop(0, tokens // RUN, sort, 0)
    d_keys[...] = jnp.zeros_like(d_keys)
    d_values[...] = jnp.zeros_like(d_values)

    def turn(block, carry):
        span_rows = pl.ds(pl.multiple_of(block * CONT, CONT), CONT)
        keys_turned[:, span_rows] = keys[span_rows, :].astype(F32).T.astype(BF16)
        return carry

    lax.fori_loop(0, blocks, turn, 0)

    if ready:
        ready()

    def back(block, own, before):
        query = queries[block]
        own_rows = pl.ds(own, CONT)
        grad = jnp.concatenate(
            [arrived[own_rows, head * HEAD : (head + 1) * HEAD] for head in range(heads)], axis=0
        )
        grad_turned = grad.astype(F32).T
        delta = jnp.sum(grad_turned * mixed[block], axis=0, keepdims=True)
        total_row = lse[block][:1, :]

        def part(rows, count, masked):
            prob = jnp.exp2(nt(keys[rows, :], query) * SCALE2 - total_row)
            if masked:
                prob = jnp.where(causal(count, wide), prob, 0.0)
            score = (prob * (nt(values[rows, :], grad) - delta)).astype(BF16)
            d_values[rows, :] += jnp.dot(prob.astype(BF16), grad, preferred_element_type=F32)
            d_keys[rows, :] += jnp.dot(score, query, preferred_element_type=F32)
            return jnp.dot(keys_turned[:, rows], score, preferred_element_type=F32)

        result = part(own_rows, CONT, True)
        if before:
            result = result + part(slice(0, before), before, False)
        result = result * SCALE
        for head in range(heads):
            d_queries[own_rows, head * HEAD : (head + 1) * HEAD] = result[
                :, head * CONT : (head + 1) * CONT
            ].T.astype(BF16)

    for block in range(PROMPT // CONT):
        back(block, block * CONT, block * CONT)

    def continuation(block, carry):
        back(block, pl.multiple_of(block * CONT, CONT), PROMPT)
        return carry

    lax.fori_loop(PROMPT // CONT, blocks, continuation, 0)


def attention_back(heads, runs, d_attended, queries, keys, values, mixed, lse):
    tokens = keys.shape[0]
    wide = heads * CONT
    shape = jax.ShapeDtypeStruct
    return pl.pallas_call(
        functools.partial(attention_back_kernel, heads),
        out_shape=[shape((tokens, wide), BF16), shape((tokens, HEAD), F32), shape((tokens, HEAD), F32)],
        in_specs=[SMEM] + [VMEM] * 6,
        out_specs=[VMEM] * 3,
        scratch_shapes=[pltpu.VMEM((tokens, wide), BF16), pltpu.VMEM((HEAD, tokens), BF16)],
        compiler_params=pltpu.CompilerParams(vmem_limit_bytes=VMEM_LIMIT),
        cost_estimate=cost(25),
    )(runs, d_attended, queries, keys, values, mixed, lse)


def joined_back_kernel(
    heads, runs, raw, d_queries, d_keys, d_values, cosine, sine, q_gain, k_gain, share, d_joined, d_q_gain, d_k_gain, placed
):
    tokens = raw.shape[0]
    blocks = tokens // CONT
    wide = heads * CONT
    d_q_gain[...] = jnp.zeros_like(d_q_gain)
    d_k_gain[...] = jnp.zeros_like(d_k_gain)

    def step(block, carry):
        span_rows = pl.ds(pl.multiple_of(block * CONT, CONT), CONT)
        cos_rows = cosine[span_rows, :]
        sin_rows = sine[span_rows, :]

        def pull(value, grad, gain):
            grad = grad * cos_rows - swap_halves(grad) * sin_rows
            scale = lax.rsqrt(jnp.mean(value * value, axis=-1, keepdims=True) + EPS)
            scaled = value * scale
            gain_grad = jnp.sum(grad * scaled, axis=0, keepdims=True)
            grad = grad * gain
            return scale * (grad - scaled * jnp.mean(grad * scaled, axis=-1, keepdims=True)), gain_grad

        for head in range(heads):
            columns = slice(head * HEAD, (head + 1) * HEAD)
            grad, gain_grad = pull(
                raw[span_rows, columns], d_queries[span_rows, columns].astype(F32), q_gain[...]
            )
            placed[span_rows, columns] = grad.astype(BF16)
            d_q_gain[...] += gain_grad
        key_part, value_part = (1.0, 1.0) if share is None else (share[:1, :], share[1:, :])
        grad, gain_grad = pull(
            raw[span_rows, wide : wide + HEAD],
            (d_keys[span_rows, :] * SCALE).astype(BF16).astype(F32),
            k_gain[...],
        )
        placed[span_rows, wide : wide + HEAD] = (grad * key_part).astype(BF16)
        d_k_gain[...] += gain_grad * key_part
        placed[span_rows, wide + HEAD : wide + 2 * HEAD] = (d_values[span_rows, :] * value_part).astype(BF16)
        return carry

    lax.fori_loop(0, blocks, step, 0)

    def unsort(run, carry):
        origin = pl.multiple_of(run * RUN, RUN)
        place = pl.multiple_of(runs[run] * RUN, RUN)
        d_joined[pl.ds(origin, RUN), :] = placed[pl.ds(place, RUN), :]
        return carry

    lax.fori_loop(0, tokens // RUN, unsort, 0)


def attention_and_joined_back_kernel(
    heads,
    count,
    groups,
    runs,
    d_attended,
    queries,
    keys,
    values,
    mixed_from,
    lse,
    raw,
    cosine,
    sine,
    q_gain,
    k_gain,
    normed,
    d_out_from,
    d_joined_to,
    d_q_gain,
    d_k_gain,
    parts_to,
    d_queries,
    d_keys,
    d_values,
    arrived,
    keys_turned,
    raw_here,
    cosine_here,
    sine_here,
    placed,
    normed_slots,
    mixed,
    d_out,
    d_joined,
    parts,
    loaded,
    normed_in,
    joined_out,
    parts_out,
):
    columns = normed_slots.shape[2]

    def normed_copy(index):
        slot = lax.rem(index, 2)
        span_columns = pl.ds(pl.multiple_of(index * columns, columns), columns)
        return pltpu.make_async_copy(normed.at[:, span_columns], normed_slots.at[slot], normed_in.at[slot])

    loads = [
        pltpu.make_async_copy(source, target, loaded.at[index])
        for index, (source, target) in enumerate(
            [
                (raw, raw_here),
                (cosine, cosine_here),
                (sine, sine_here),
                (mixed_from, mixed),
                (d_out_from, d_out),
            ]
        )
    ]
    ready = loads[3].wait
    for item in [loads[3]] + loads[:3] + loads[4:]:
        item.start()
    normed_copy(0).start()
    attention_back_kernel(
        heads,
        runs,
        d_attended,
        queries,
        keys,
        values,
        mixed,
        lse,
        d_queries,
        d_keys,
        d_values,
        arrived,
        keys_turned,
        ready,
    )
    for item in loads[:3] + loads[4:]:
        item.wait()
    joined_back_kernel(
        heads,
        runs,
        raw_here,
        d_queries,
        d_keys,
        d_values,
        cosine_here,
        sine_here,
        q_gain,
        k_gain,
        None,
        d_joined,
        d_q_gain,
        d_k_gain,
        placed,
    )
    rows = columns // groups
    width = d_joined.shape[1]
    joined_copy = pltpu.make_async_copy(d_joined, d_joined_to, joined_out.at[0])
    joined_copy.start()

    def part_copies(index):
        return [
            pltpu.make_async_copy(
                parts.at[owner, index], parts_to.at[owner, index], parts_out.at[owner, index]
            )
            for owner in range(groups)
        ]

    extras = range(d_out.shape[1] // width)
    for extra in extras:
        for owner in range(groups):
            parts[owner, count + extra] = d_out[
                owner * rows : (owner + 1) * rows, extra * width : (extra + 1) * width
            ]
        for item in part_copies(count + extra):
            item.start()

    def weight_grad(index, carry):
        @pl.when(index + 1 < count)
        def _():
            normed_copy(index + 1).start()

        normed_copy(index).wait()
        value = lax.dot_general(
            normed_slots[lax.rem(index, 2)], d_joined[...], (((0,), (0,)), ((), ())), preferred_element_type=F32
        ).astype(BF16)
        for owner in range(groups):
            parts[owner, index] = value[owner * rows : (owner + 1) * rows]
        for item in part_copies(index):
            item.start()
        return carry

    lax.fori_loop(0, count, weight_grad, 0)
    for index in range(count + len(extras)):
        for item in part_copies(index):
            item.wait()
    joined_copy.wait()


def attention_and_joined_back(
    heads,
    count,
    groups,
    runs,
    d_attended,
    queries,
    keys,
    values,
    mixed,
    lse,
    raw,
    cosine,
    sine,
    q_gain,
    k_gain,
    normed,
    d_out,
):
    tokens = keys.shape[0]
    columns = normed.shape[1] // count
    blocks = count + d_out.shape[1] // raw.shape[1]
    wide = heads * CONT
    shape = jax.ShapeDtypeStruct
    return pl.pallas_call(
        functools.partial(attention_and_joined_back_kernel, heads, count, groups),
        out_shape=[
            shape(raw.shape, BF16),
            shape((1, HEAD), F32),
            shape((1, HEAD), F32),
            shape((groups, blocks, columns // groups, raw.shape[1]), BF16),
        ],
        in_specs=[SMEM] + [VMEM] * 4 + [ANY, VMEM] + [ANY] * 3 + [VMEM] * 2 + [ANY] * 2,
        out_specs=[ANY, VMEM, VMEM, ANY],
        scratch_shapes=[
            pltpu.VMEM((tokens, wide), BF16),
            pltpu.VMEM((tokens, HEAD), F32),
            pltpu.VMEM((tokens, HEAD), F32),
            pltpu.VMEM((tokens, wide), BF16),
            pltpu.VMEM((HEAD, tokens), BF16),
            pltpu.VMEM(raw.shape, F32),
            pltpu.VMEM(cosine.shape, F32),
            pltpu.VMEM(sine.shape, F32),
            pltpu.VMEM(raw.shape, BF16),
            pltpu.VMEM((2, tokens, columns), BF16),
            pltpu.VMEM(mixed.shape, F32),
            pltpu.VMEM(d_out.shape, BF16),
            pltpu.VMEM(raw.shape, BF16),
            pltpu.VMEM((groups, blocks, columns // groups, raw.shape[1]), BF16),
            DMA((5,)),
            DMA((2,)),
            DMA((1,)),
            DMA((groups, blocks)),
        ],
        compiler_params=pltpu.CompilerParams(vmem_limit_bytes=VMEM_LIMIT),
        cost_estimate=cost(30),
    )(runs, d_attended, queries, keys, values, mixed, lse, raw, cosine, sine, q_gain, k_gain, normed, d_out)


def joined_back(heads, runs, raw, d_queries, d_keys, d_values, cosine, sine, q_gain, k_gain, share):
    shape = jax.ShapeDtypeStruct
    return pl.pallas_call(
        functools.partial(joined_back_kernel, heads),
        out_shape=[shape(raw.shape, BF16), shape((1, HEAD), F32), shape((1, HEAD), F32)],
        in_specs=[SMEM] + [VMEM] * 9,
        out_specs=[VMEM] * 3,
        scratch_shapes=[pltpu.VMEM(raw.shape, BF16)],
        compiler_params=pltpu.CompilerParams(vmem_limit_bytes=VMEM_LIMIT),
        cost_estimate=cost(8),
    )(runs, raw, d_queries, d_keys, d_values, cosine, sine, q_gain, k_gain, share)


def rotary(tokens):
    index = np.arange(tokens)
    place = np.where(index < PROMPT, index, PROMPT + (index - PROMPT) % CONT).astype(np.float32)
    exponent = np.arange(HEAD // 2, dtype=np.float32) * np.float32(2.0 / HEAD)
    inverse = np.power(np.float32(ROPE_BASE), -exponent).astype(np.float32)
    angles = place[:, None] * inverse[None, :]
    cosine, sine = np.cos(angles), np.sin(angles)
    tables = np.concatenate([cosine, cosine], axis=1), np.concatenate([-sine, sine], axis=1)
    return tuple(jnp.asarray(table, F32) for table in tables)


def body(
    count,
    groups,
    hidden_in,
    segment_ids,
    positions,
    attn_gain,
    qkv_weight,
    query_norm_gain,
    k_gain,
    out_weight,
    mlp_gain,
    gate_up,
    down_weight,
    cotangent,
):
    hidden = hidden_in[0].astype(F32)
    rows, width = hidden.shape
    tokens = rows * count
    heads = QUERY_HEADS // count
    repeat = sharing(count)

    first = segment_ids[0, ::RUN]
    place = positions[0, ::RUN]
    order = jnp.where(first == 0, place, place + (first - 1) * CONT) // RUN
    runs = jnp.zeros((1, 8, 128), jnp.int32).at[0, 0, : rows // RUN].set(order)

    def gather_groups(values, axis):
        return lax.all_gather(values, "fsdp", axis=axis, tiled=True)

    def scatter_groups(values):
        return lax.psum_scatter(values, "fsdp", scatter_dimension=0, tiled=True)

    qkv_parts = spread_qkv(count, 1, qkv_weight, out_weight)
    gate_up, qkv_parts = lax.optimization_barrier((gate_up, qkv_parts))
    w_qkv = gather_groups(qkv_parts, 1)
    if merges(count, width):
        w_out = w_qkv[count:].transpose(1, 0, 2).reshape(-1, width)
        w_qkv = w_qkv[:count]
    else:
        w_out = gather_groups(out_weight, 0)
    w_qkv = w_qkv.reshape(width, -1)
    mlp_parts = spread_mlp(count, 5, gate_up)
    normed_local = norm_rows(hidden, attn_gain).astype(BF16)
    normed_local, mlp_parts = lax.optimization_barrier((normed_local, mlp_parts))
    normed, all_runs = opening(count, 2, normed_local, runs)
    w_qkv, normed, upstream = lax.optimization_barrier((w_qkv, normed, cotangent[0]))
    w_gu = gather_groups(mlp_parts, 1).reshape(width, -1)
    w_down = gather_groups(down_weight, 0)
    run_order = all_runs[:, 0, : rows // RUN].reshape(-1)
    cosine, sine = rotary(tokens)
    q_gain_row = query_norm_gain[None, :]
    k_gain_row = k_gain[None, :]

    blocks, masks = [upstream[None, : rows // 2], upstream[None, rows // 2 :]], [[0], [0]]
    chip_steps = len(bits_of(count)) - 1
    for step in range(chip_steps - 1):
        arrived, filled = gather_step(count, masks, blocks, step)
        if step == 0:
            joined = jnp.dot(normed, w_qkv, preferred_element_type=F32)
            joined, arrived = lax.optimization_barrier((joined, arrived))
        blocks = [jnp.concatenate(pair) for pair in zip(blocks, arrived)]
        masks = [held + more for held, more in zip(masks, filled)]
    arrived, filled = gather_step(count, masks, blocks, chip_steps - 1)
    attended, raw, queries, keys, values, mixed, lse = attention(
        heads, run_order, joined, cosine, sine, q_gain_row, k_gain_row
    )
    attended, arrived = lax.optimization_barrier((attended, arrived))
    middle, second, upstream = middle_and_second(
        count, 3, attended, w_out, hidden_in[0], mlp_gain[None, :], masks, blocks, filled, arrived
    )
    both = jnp.dot(second, w_gu, preferred_element_type=F32)
    own = both.shape[1] // 2
    gate, up = both[:, :own], both[:, own:]
    activated = (gate * jax.nn.sigmoid(gate) * up).astype(BF16)

    d_down = jnp.dot(activated.T, upstream, preferred_element_type=F32).astype(BF16)
    d_down, upstream = lax.optimization_barrier((d_down, upstream))
    d_down = scatter_groups(d_down)
    output, d_both, gu_parts = back_through_mlp(
        count, groups, 9, activated, w_down, middle, upstream, both, second
    )
    gu_parts, d_both = lax.optimization_barrier((gu_parts, d_both))
    gu_parts = scatter_groups(gu_parts.reshape((groups * count,) + gu_parts.shape[2:]))

    def weight_grad(left, right):
        grad = lax.dot_general(left, right, (((0,), (0,)), ((), ())), preferred_element_type=F32)
        grad = grad.astype(BF16).reshape(count, groups, -1, right.shape[1])
        return grad.transpose(1, 0, 2, 3).reshape(groups * count, -1, right.shape[1])

    d_middle, mlp_gain_grad, d_attended, d_out = back_through_middle(
        count, 6, d_both, w_gu, middle, cotangent[0], mlp_gain[None, :], attended, w_out
    )
    d_attended, d_down = lax.optimization_barrier((d_attended, d_down))
    tables = (cosine, sine, q_gain_row, k_gain_row)
    if repeat == 1:
        d_joined, q_gain_grad, k_gain_grad, parts = attention_and_joined_back(
            heads,
            count,
            groups,
            run_order,
            d_attended,
            queries,
            keys,
            values,
            mixed,
            lse,
            raw,
            *tables,
            normed,
            d_out,
        )
        parts, gu_parts, d_joined = lax.optimization_barrier((parts, gu_parts, d_joined))
        qkv_grad_parts = scatter_groups(parts.reshape((-1,) + parts.shape[2:]))
    else:
        d_queries, d_keys, d_values = attention_back(
            heads, run_order, d_attended, queries, keys, values, mixed, lse
        )
        d_keys = d_keys + across(count, 1, d_keys)
        d_values = d_values + across(count, 1, d_values)
        mine = lax.rem(lax.axis_index("ctx"), 2) == jnp.arange(2)
        share = jnp.broadcast_to(mine[:, None].astype(F32), (2, HEAD))
        d_joined, q_gain_grad, k_gain_grad = joined_back(
            heads, run_order, raw, d_queries, d_keys, d_values, *tables, share
        )
        d_out = scatter_groups(d_out)
        qkv_grad_parts = scatter_groups(weight_grad(normed, d_joined))
    d_hidden, attn_gain_grad, d_gate_up = back_to_input(
        count, 8, d_joined, w_qkv, hidden_in[0], d_middle, attn_gain[None, :], gu_parts
    )
    d_hidden, qkv_grad_parts = lax.optimization_barrier((d_hidden, qkv_grad_parts))

    gains = (attn_gain_grad, mlp_gain_grad, q_gain_grad, k_gain_grad)
    if repeat > 1:
        extra = jnp.zeros((1,) + qkv_grad_parts.shape[1:], BF16)
        qkv_grad_parts = jnp.concatenate([qkv_grad_parts, extra])
    *gains, d_qkv, out_rows = last(count, groups, 11, gains, qkv_grad_parts, qkv_weight.shape[1])
    if repeat == 1:
        d_out = out_rows
    return (
        output[None],
        d_hidden[None],
        gains[0].reshape(-1),
        d_qkv,
        gains[2].reshape(-1),
        gains[3].reshape(-1),
        d_out.astype(F32),
        gains[1].reshape(-1),
        d_gate_up,
        d_down.astype(F32),
    )


def solution(mesh):
    return jax.shard_map(
        functools.partial(body, mesh.shape["ctx"], mesh.shape["fsdp"]),
        mesh=mesh,
        in_specs=(
            P("fsdp", "ctx", None),
            P("fsdp", "ctx"),
            P("fsdp", "ctx"),
            P(),
            P(("ctx", "fsdp"), None),
            P(),
            P(),
            P(("ctx", "fsdp"), None),
            P(),
            P(("ctx", "fsdp"), None),
            P(("ctx", "fsdp"), None),
            P("fsdp", "ctx", None),
        ),
        out_specs=(
            P("fsdp", "ctx", None),
            P("fsdp", "ctx", None),
            P(),
            P(("ctx", "fsdp"), None),
            P(),
            P(),
            P(("ctx", "fsdp"), None),
            P(),
            P(("ctx", "fsdp"), None),
            P(("ctx", "fsdp"), None),
        ),
        check_vma=False,
    )
```

```python
import functools
import math

import jax
import jax.numpy as jnp
import numpy as np
from jax import lax
from jax.experimental import pallas as pl
from jax.experimental.pallas import tpu as pltpu
from jax.sharding import PartitionSpec as P

QUERY_HEADS = 16
KEY_VALUE_HEADS = 8
HEAD = 128
FF = 6144
PROMPT = 1024
CONT = 128
RUN = 32
EPS = 1e-06
ROPE_BASE = 1000000.0
SCALE = HEAD ** (-0.5)
SCALE2 = SCALE * math.log2(math.e)
MESH = pl.DeviceIdType.MESH
ANY = pl.BlockSpec(memory_space=pl.ANY)
VMEM = pl.BlockSpec(memory_space=pltpu.VMEM)
SMEM = pl.BlockSpec(memory_space=pltpu.SMEM)
BF16 = jnp.bfloat16
F32 = jnp.float32
DMA = pltpu.SemaphoreType.DMA
VMEM_LIMIT = 60 * 2**20


def cost(us):
    return pl.CostEstimate(flops=0, bytes_accessed=int(us * 1e6), transcendentals=0)


def flip(me, mask):
    result = me
    bit = 1
    while bit <= mask:
        if mask & bit:
            result = result + bit - 2 * bit * lax.rem(lax.div(me, bit), 2)
        bit *= 2
    return result


def bits_of(count):
    bits = []
    bit = 1
    while bit < count:
        bits.append(bit)
        bit *= 2
    return bits


def greet(peers):
    barrier = pltpu.get_barrier_semaphore()
    for peer in peers:
        pl.semaphore_signal(barrier, inc=1, device_id=peer, device_id_type=MESH)
    pl.semaphore_wait(barrier, len(peers))


def gather_orders(count):
    chip_bits = bits_of(count)[1:]
    return [chip_bits + [1], chip_bits[::-1] + [1]]


def last_bit(order, slot):
    return [bit for bit in order if slot & bit][-1]


def gather_rows(count, me, group, parts, source, target, send, recv, own=None):
    rows = target.shape[0] // count
    piece = rows // parts
    orders = gather_orders(count)
    copies = []

    def place(part, slot):
        return pl.multiple_of(flip(me, slot) * rows + part * piece, piece)

    def copy(part, slot, bit):
        there = target.at[pl.ds(place(part, slot), piece)]
        own_place = slot == 0 and source is not None
        origin = source.at[pl.ds(part * piece, piece)] if own_place else there
        number = part * count + (slot ^ bit)
        return pltpu.make_async_remote_copy(
            origin,
            there,
            send.at[number],
            recv.at[number],
            device_id=(flip(me, bit), group),
            device_id_type=MESH,
        )

    def keep(part):
        there = target.at[pl.ds(place(part, 0), piece)]
        return pltpu.make_async_copy(source.at[pl.ds(part * piece, piece)], there, own.at[part])

    def start(part):
        for bit in orders[part % 2]:
            item = copy(part, 0, bit)
            item.start()
            copies.append(item)
        if source is not None:
            keep(part).start()

    def wait(part, slot):
        there = target.at[pl.ds(place(part, slot), piece)]
        number = part * count + slot
        pltpu.make_async_remote_copy(
            there,
            there,
            send.at[number],
            recv.at[number],
            device_id=(flip(me, last_bit(orders[part % 2], slot)), group),
            device_id_type=MESH,
        ).wait_recv()

    def finish(arrived=None):
        waits = []
        for part in range(parts):
            order = orders[part % 2]
            for slot in range(1, count):
                last = order.index(last_bit(order, slot))
                waits.append((part // 2 + last, last, bin(slot).count("1"), part, slot))
        if arrived:
            for part in range(0, parts, 2):
                arrived(place(part, 0), 2 * piece)
        there = set()
        for _, last, _, part, slot in sorted(waits):
            wait(part, slot)
            for bit in orders[part % 2][last + 1 :]:
                item = copy(part, slot, bit)
                item.start()
                copies.append(item)
            there.add((part, slot))
            if arrived and (part ^ 1, slot) in there:
                arrived(place(part // 2 * 2, slot), 2 * piece)
        for part in range(parts):
            if source is not None:
                keep(part).wait()
        for item in copies:
            item.wait_send()

    return start, finish


def trade(count, me, group, pieces, source, target, send, recv):
    copies = []
    local = []

    def start(slots):
        for slot in slots:
            peer = flip(me, slot)
            for number, (origin, place) in enumerate(pieces(peer, me)):
                total = len(pieces(peer, me))
                index = slot * total + number
                if slot == 0:
                    item = pltpu.make_async_copy(source.at[origin], target.at[place], send.at[index])
                    local.append(item)
                else:
                    item = pltpu.make_async_remote_copy(
                        source.at[origin],
                        target.at[place],
                        send.at[index],
                        recv.at[index],
                        device_id=(peer, group),
                        device_id_type=MESH,
                    )
                    copies.append(item)
                item.start()

    def finish(arrived=None):
        for item in local:
            item.wait()
        if arrived:
            arrived(me)
        for slot in range(1, count):
            peer = flip(me, slot)
            listed = pieces(me, peer)
            for number, (origin, place) in enumerate(listed):
                index = slot * len(listed) + number
                pltpu.make_async_remote_copy(
                    source.at[origin],
                    target.at[place],
                    send.at[index],
                    recv.at[index],
                    device_id=(peer, group),
                    device_id_type=MESH,
                ).wait_recv()
            if arrived:
                arrived(peer)
        for item in copies:
            item.wait_send()

    return start, finish


def all_slots(count):
    return list(range(1, count)) + [0]


def span(start, width):
    return pl.ds(pl.multiple_of(start, HEAD), width)


def sharing(count):
    if count not in (KEY_VALUE_HEADS, QUERY_HEADS):
        raise ValueError(count)
    return count // KEY_VALUE_HEADS


def qkv_spans(count, device, gradients=False):
    own = QUERY_HEADS // count * HEAD
    repeat = sharing(count)
    queries = QUERY_HEADS * HEAD
    shared = lax.div(device, repeat) * HEAD
    if repeat == 2 and gradients:
        which = lax.rem(device, 2)
        return [
            (device * own, 0, own),
            (queries + which * (KEY_VALUE_HEADS * HEAD) + shared, own + which * HEAD, HEAD),
        ]
    return [
        (device * own, 0, own),
        (queries + shared, own, HEAD),
        (queries + KEY_VALUE_HEADS * HEAD + shared, own + HEAD, HEAD),
    ]


def mlp_spans(count, device, gradients=False):
    own = FF // count
    return [(device * own, 0, own), (FF + device * own, own, own)]


def outgoing(spans, count):
    def pieces(device, owner):
        return [
            ((slice(None), span(whole, width)), (owner, slice(None), pl.ds(part, width)))
            for whole, part, width in spans(count, device)
        ]

    return pieces


def incoming(device, owner):
    return [((device,), (owner,))]


def place_columns(count, spans, arrived, target):
    def place(peer):
        for whole, part, width in spans(count, peer, True):
            target[:, span(whole, width)] = arrived[peer, :, span(part, width)].astype(F32)

    return place


def everyone(count, me, group):
    return [(flip(me, slot), group) for slot in range(1, count)]


def spread_qkv_kernel(count, qkv, out, parts, send, recv, local):
    me = lax.axis_index("ctx")
    group = lax.axis_index("fsdp")
    width = parts.shape[2]
    greet(everyone(count, me, group))
    start, finish = trade(count, me, group, outgoing(qkv_spans, count), qkv, parts, send, recv)
    start(all_slots(count))
    items = [
        pltpu.make_async_copy(
            out.at[:, pl.ds(index * width, width)], parts.at[count + index], local.at[index]
        )
        for index in range(parts.shape[0] - count)
    ]
    for item in items:
        item.start()
    finish()
    for item in items:
        item.wait()


def spread_qkv(count, collective, qkv, out):
    rows = qkv.shape[0]
    width = qkv_width(count)
    extra = out.shape[1] // width if merges(count, out.shape[1]) else 0
    return pl.pallas_call(
        functools.partial(spread_qkv_kernel, count),
        out_shape=jax.ShapeDtypeStruct((count + extra, rows, width), BF16),
        in_specs=[ANY, VMEM],
        out_specs=ANY,
        scratch_shapes=[DMA((3 * count,)), DMA((3 * count,)), DMA((max(1, extra),))],
        compiler_params=pltpu.CompilerParams(collective_id=collective, has_side_effects=True),
        cost_estimate=cost(12),
    )(qkv, out)


def qkv_width(count):
    return QUERY_HEADS // count * HEAD + 2 * HEAD


def merges(count, width):
    return width % qkv_width(count) == 0


def spread_mlp_kernel(count, weight, parts, send, recv):
    me = lax.axis_index("ctx")
    group = lax.axis_index("fsdp")
    greet(everyone(count, me, group))
    start, finish = trade(count, me, group, outgoing(mlp_spans, count), weight, parts, send, recv)
    start(all_slots(count))
    finish()


def spread_mlp(count, collective, weight):
    return pl.pallas_call(
        functools.partial(spread_mlp_kernel, count),
        out_shape=jax.ShapeDtypeStruct((count, weight.shape[0], 2 * FF // count), BF16),
        in_specs=[ANY],
        out_specs=ANY,
        scratch_shapes=[DMA((2 * count,)), DMA((2 * count,))],
        compiler_params=pltpu.CompilerParams(collective_id=collective, has_side_effects=True),
        cost_estimate=cost(22),
    )(weight)


def opening_kernel(count, normed, runs, rows, all_runs, send, recv, own, run_send, run_recv):
    me = lax.axis_index("ctx")
    group = lax.axis_index("fsdp")
    greet(everyone(count, me, group))
    start, finish_runs = trade(
        count, me, group, lambda device, owner: [((0,), (owner,))], runs, all_runs, run_send, run_recv
    )
    start(all_slots(count))
    start, finish = gather_rows(count, me, group, 2, normed, rows, send, recv, own)
    start(0)
    start(1)
    finish()
    finish_runs()


def opening(count, collective, normed, runs):
    tokens, width = normed.shape
    return pl.pallas_call(
        functools.partial(opening_kernel, count),
        out_shape=[
            jax.ShapeDtypeStruct((count * tokens, width), BF16),
            jax.ShapeDtypeStruct((count, 8, 128), jnp.int32),
        ],
        in_specs=[VMEM, ANY],
        out_specs=[ANY, ANY],
        scratch_shapes=[DMA((2 * count,)), DMA((2 * count,)), DMA((2,)), DMA((count,)), DMA((count,))],
        compiler_params=pltpu.CompilerParams(collective_id=collective, has_side_effects=True),
        cost_estimate=cost(45),
    )(normed, runs)


def across(count, bit, values):
    return lax.ppermute(values, "ctx", [(index, index ^ bit) for index in range(count)])


def join_rows(count, me, group, slots, blocks, target, send, recv, local):
    other = flip(me, 1)
    half = blocks[0].shape[1]
    items = []
    for block, (part, masks) in zip(blocks, slots):
        items += [(block, index, part, mask) for index, mask in enumerate(masks)]

    def place(number, owner):
        _, _, part, mask = items[number]
        return pl.ds(pl.multiple_of(flip(owner, mask) * 2 * half + part * half, half), half)

    def copy(number, owner):
        block, index = items[number][:2]
        return pltpu.make_async_remote_copy(
            block.at[index],
            target.at[place(number, owner)],
            send.at[number],
            recv.at[number],
            device_id=(other, group),
            device_id_type=MESH,
        )

    def keep(number):
        block, index = items[number][:2]
        return pltpu.make_async_copy(block.at[index], target.at[place(number, me)], local.at[number])

    def start():
        for number in range(len(items)):
            copy(number, me).start()
            keep(number).start()

    def finish():
        for number in range(len(items)):
            keep(number).wait()
            copy(number, other).wait_recv()
            copy(number, me).wait_send()

    return start, finish


def gather_step(count, masks, blocks, step):
    arrived, filled = [], []
    for part, order in enumerate(gather_orders(count)):
        arrived.append(across(count, order[step], blocks[part]))
        filled.append([mask ^ order[step] for mask in masks[part]])
    return arrived, filled


def last_kernel(
    count,
    groups,
    attn_part,
    mlp_part,
    q_part,
    k_part,
    parts,
    attn_gain,
    mlp_gain,
    q_gain,
    k_gain,
    d_qkv,
    d_out,
    columns,
    out_parts,
    values,
    near,
    far,
    send,
    recv,
    far_send,
    far_recv,
    part_send,
    part_recv,
    out_in,
):
    me = lax.axis_index("ctx")
    group = lax.axis_index("fsdp")
    others = [lax.rem(group + step, groups) for step in range(1, groups)]
    fetched = fetch([parts.at[pl.ds(count, out_parts.shape[0])]], [out_parts], out_in)
    rows = attn_gain.shape[0]
    for row in range(rows):
        values[row : row + 1] = attn_part[:, row * 128 : (row + 1) * 128]
        values[rows + row : rows + row + 1] = mlp_part[:, row * 128 : (row + 1) * 128]
    values[2 * rows : 2 * rows + 1] = q_part[...]
    values[2 * rows + 1 : 2 * rows + 2] = k_part[...]
    values[2 * rows + 2 :] = jnp.zeros((6, 128), F32)
    near[me] = values[...]
    greet(everyone(count, me, group) + [(me, other) for other in others])
    start, finish = trade(count, me, group, incoming, parts, columns, part_send, part_recv)
    start(all_slots(count))
    copies = []
    for slot in range(1, count):
        item = pltpu.make_async_remote_copy(
            values,
            near.at[me],
            send.at[slot],
            recv.at[slot],
            device_id=(flip(me, slot), group),
            device_id_type=MESH,
        )
        item.start()
        copies.append(item)
    for item in copies:
        item.wait()
    summed = near[0]
    for index in range(1, count):
        summed = summed + near[index]
    far[group] = summed
    copies = []
    for step, other in enumerate(others):
        item = pltpu.make_async_remote_copy(
            far.at[group],
            far.at[group],
            far_send.at[step],
            far_recv.at[step],
            device_id=(me, other),
            device_id_type=MESH,
        )
        item.start()
        copies.append(item)
    for item in copies:
        item.wait()
    summed = far[0]
    for index in range(1, groups):
        summed = summed + far[index]
    attn_gain[...] = summed[:rows]
    mlp_gain[...] = summed[rows : 2 * rows]
    q_gain[...] = summed[2 * rows : 2 * rows + 1]
    k_gain[...] = summed[2 * rows + 1 : 2 * rows + 2]
    fetched()
    width = out_parts.shape[2]
    for index in range(out_parts.shape[0]):
        d_out[:, index * width : (index + 1) * width] = out_parts[index].astype(F32)
    finish(place_columns(count, qkv_spans, columns, d_qkv))


def last(count, groups, collective, gains, parts, columns):
    width = gains[0].shape[1]
    rows = width // 128
    shape = (2 * rows + 8, 128)
    long, short = (rows, 128), (1, 128)
    out_shape = (parts.shape[0] - count,) + parts.shape[1:]
    return pl.pallas_call(
        functools.partial(last_kernel, count, groups),
        out_shape=[jax.ShapeDtypeStruct(size, F32) for size in (long, long, short, short)]
        + [
            jax.ShapeDtypeStruct((parts.shape[1], columns), F32),
            jax.ShapeDtypeStruct((parts.shape[1], out_shape[0] * out_shape[2]), F32),
        ],
        in_specs=[VMEM] * 4 + [ANY],
        out_specs=[VMEM] * 6,
        scratch_shapes=[
            pltpu.VMEM((count,) + parts.shape[1:], BF16),
            pltpu.VMEM(out_shape, BF16),
            pltpu.VMEM(shape, F32),
            pltpu.VMEM((count,) + shape, F32),
            pltpu.VMEM((groups,) + shape, F32),
            DMA((count,)),
            DMA((count,)),
            DMA((groups,)),
            DMA((groups,)),
            DMA((count,)),
            DMA((count,)),
            DMA((1,)),
        ],
        compiler_params=pltpu.CompilerParams(collective_id=collective, has_side_effects=True),
        cost_estimate=cost(14),
    )(*gains, parts)


def product_slots(count):
    slots = []
    for pair in range(count // 2)[::-1]:
        slots += [2 * pair - 1, 2 * pair] if slots and pair else [2 * pair + 1, 2 * pair - 1, 2 * pair] if pair else [0]
    return slots


def load_operands(count, me, flipped, left_from, right_from, left, right, left_in, right_in):
    rows = left.shape[0] // count
    width = right.shape[0] if flipped else right.shape[1]
    tile = min(512, width)

    def left_copy(slot):
        span_rows = pl.ds(pl.multiple_of(flip(me, slot) * rows, rows), rows)
        return pltpu.make_async_copy(left_from.at[span_rows], left.at[span_rows], left_in.at[slot])

    def right_copy(index):
        span_tile = pl.ds(pl.multiple_of(index * tile, tile), tile)
        place = (span_tile,) if flipped else (slice(None), span_tile)
        return pltpu.make_async_copy(right_from.at[place], right.at[place], right_in.at[index])

    slots = product_slots(count)
    right_copy(0).start()
    left_copy(slots[0]).start()
    for index in range(1, width // tile):
        right_copy(index).start()
    for slot in slots[1:]:
        left_copy(slot).start()
    return lambda slot: left_copy(slot).wait(), lambda index: right_copy(index).wait()


def operand_scratch(count, left, right, flipped):
    width = right.shape[0] if flipped else right.shape[1]
    return [
        pltpu.VMEM(left.shape, BF16),
        pltpu.VMEM(right.shape, BF16),
        DMA((count,)),
        DMA((width // min(512, width),)),
    ]


def fetch(sources, targets, arrived):
    items = [
        pltpu.make_async_copy(source, target, arrived.at[index])
        for index, (source, target) in enumerate(zip(sources, targets))
    ]
    for item in items:
        item.start()

    def wait():
        for item in items:
            item.wait()

    return wait


def product_scatter(
    count,
    me,
    group,
    parts,
    flipped,
    left,
    right,
    done,
    kept,
    near_out,
    near_in,
    far_out,
    far_in,
    ns,
    nr,
    fs,
    fr,
    ready=None,
):
    rows, width = kept.shape
    piece = rows // parts
    bits = bits_of(count)
    orders = [bits[1:][::-1], bits[1:]]
    tile = min(512, width)
    pairs = list(range(count // 2))[::-1]

    def product(slot, store):
        start = pl.multiple_of(flip(me, slot) * rows, rows)
        if ready:
            ready[0](slot)
        block = left[pl.ds(start, rows), :]

        def step(index, carry):
            columns = pl.ds(pl.multiple_of(index * tile, tile), tile)
            if ready and slot == count - 1:
                ready[1](index)
            if flipped:
                value = nt(block, right[columns, :])
            else:
                value = jnp.dot(block, right[:, columns], preferred_element_type=F32)
            store(columns, value)
            return carry

        lax.fori_loop(0, width // tile, step, 0)

    def first(part, slot):
        return [bit for bit in orders[part % 2] if slot & bit][0]

    def near(pair):
        return pltpu.make_async_remote_copy(
            near_out.at[pair],
            near_in.at[pair],
            ns.at[pair],
            nr.at[pair],
            device_id=(flip(me, 1), group),
            device_id_type=MESH,
        )

    def number(part, pair):
        return part * (count // 2 - 1) + pair - 1

    def far(part, pair):
        index = number(part, pair)
        return pltpu.make_async_remote_copy(
            far_out.at[index],
            far_in.at[index],
            fs.at[index],
            fr.at[index],
            device_id=(flip(me, first(part, 2 * pair)), group),
            device_id_type=MESH,
        )

    def needs(part, pair):
        found = []
        for bit in orders[part % 2]:
            if 2 * pair & bit:
                break
            found.append((2 * pair ^ bit) // 2)
        return found

    def settle(part, pair):
        if pair == 0:
            value = kept[pl.ds(part * piece, piece), :]
        else:
            value = far_out[number(part, pair)].astype(F32)
        for other in needs(part, pair):
            far(part, other).wait_recv()
            value = value + far_in[number(part, other)].astype(F32)
        if pair == 0:
            done(part, value)
        else:
            far_out[number(part, pair)] = value.astype(BF16)
            far(part, pair).start()

    def send_near(pair):
        def store(columns, value):
            near_out[pair, :, columns] = value.astype(BF16)

        product(2 * pair + 1, store)
        near(pair).start()

    def batch_parts(batch):
        return (2 * batch, 2 * batch + 1)

    def send_pair(batch, pair):
        for part in batch_parts(batch):
            if pair and not needs(part, pair):
                far(part, pair).start()

    def sum_near(pair):
        near(pair).wait_recv()

        def store(columns, value):
            value = value + near_in[pair, :, columns].astype(F32)
            if pair == 0:
                kept[:, columns] = value
            else:
                for part in range(parts):
                    far_out[number(part, pair), :, columns] = value[
                        part * piece : (part + 1) * piece
                    ].astype(BF16)

        product(2 * pair, store)
        send_pair(0, pair)

    def begin():
        send_near(pairs[0])
        for pair in pairs:
            if pair:
                send_near(pair - 1)
            sum_near(pair)

    def send(batch):
        for pair in pairs:
            send_pair(batch, pair)

    def pass_on(batch):
        for pair in pairs:
            for part in batch_parts(batch):
                if pair and needs(part, pair):
                    settle(part, pair)

    def end(batch):
        for part in batch_parts(batch):
            settle(part, 0)

    def close():
        for pair in pairs:
            near(pair).wait_send()
            for part in range(parts):
                if pair:
                    far(part, pair).wait_send()

    return begin, send, pass_on, end, close


def scatter_scratch(count, rows, width, parts=2):
    pairs = count // 2
    links = parts * (pairs - 1)
    return [
        pltpu.VMEM((rows, width), F32),
        pltpu.VMEM((pairs, rows, width), BF16),
        pltpu.VMEM((pairs, rows, width), BF16),
        pltpu.VMEM((links, rows // parts, width), BF16),
        pltpu.VMEM((links, rows // parts, width), BF16),
        DMA((pairs,)),
        DMA((pairs,)),
        DMA((links,)),
        DMA((links,)),
    ]


SCATTER = 9
PARTS = 4
BACK_PARTS = 2


def comm_params(collective):
    return pltpu.CompilerParams(
        collective_id=collective, has_side_effects=True, vmem_limit_bytes=VMEM_LIMIT
    )


def row_blocks(first, count, step):
    def body(index, carry):
        step(pl.multiple_of(first + index * 32, 32), pl.multiple_of(index * 32, 32))
        return carry

    lax.fori_loop(0, count // 32, body, 0)


def norm_back(values, gain, grad):
    scale = lax.rsqrt(jnp.mean(values * values, axis=-1, keepdims=True) + EPS)
    scaled = values * scale
    pushed = grad * gain
    back = scale * (pushed - scaled * jnp.mean(pushed * scaled, axis=-1, keepdims=True))
    return back, jnp.sum(grad * scaled, axis=0, keepdims=True)


def norm_rows(values, gain):
    return values * lax.rsqrt(jnp.mean(values * values, axis=-1, keepdims=True) + EPS) * gain


def middle_kernel(count, slots, left, right, hidden, gain, *refs):
    held, refs = refs[: len(slots)], refs[len(slots) :]
    (middle, gathered, joined, own_rows, sums), refs = refs[:5], refs[5:]
    blocks, refs = refs[: len(slots)], refs[len(slots) :]
    (held_in, send, recv, local), scratch = refs[:4], refs[4:]
    me = lax.axis_index("ctx")
    group = lax.axis_index("fsdp")
    piece = middle.shape[0] // PARTS
    fetched = fetch(held, blocks, held_in)
    greet([(flip(me, bit), group) for bit in bits_of(count)])
    start, finish = gather_rows(count, me, group, PARTS, own_rows, gathered, *scratch[SCATTER:])
    start_join, finish_join = join_rows(count, me, group, slots, blocks, joined, send, recv, local)

    def done(part, value):
        sums[...] = value

        def step(row, place):
            total_rows = hidden[pl.ds(row, 32), :].astype(F32) + sums[pl.ds(place, 32), :]
            middle[pl.ds(row, 32), :] = total_rows
            own_rows[pl.ds(row, 32), :] = norm_rows(total_rows, gain[...]).astype(BF16)

        row_blocks(part * piece, piece, step)
        start(part)

    begin, send_batch, pass_on, end, close = product_scatter(
        count, me, group, PARTS, False, left, right, done, *scratch[:SCATTER]
    )
    begin()
    fetched()
    start_join()
    pass_on(0)
    send_batch(1)
    end(0)
    pass_on(1)
    end(1)
    finish()
    finish_join()
    close()


def gather_scratch(count, parts):
    return [DMA((parts * count,)), DMA((parts * count,)), DMA((parts,))]


def middle_and_second(count, collective, left, right, hidden, gain, masks, blocks, filled, arrived):
    rows, width = hidden.shape
    slots, held = [], []
    for part in (0, 1):
        slots += [(part, masks[part]), (part, filled[part])]
        held += [blocks[part], arrived[part]]
    return pl.pallas_call(
        functools.partial(middle_kernel, count, slots),
        out_shape=[
            jax.ShapeDtypeStruct((rows, width), F32),
            jax.ShapeDtypeStruct((count * rows, width), BF16),
            jax.ShapeDtypeStruct((count * rows, width), BF16),
        ],
        in_specs=[VMEM] * 4 + [ANY] * len(held),
        out_specs=[VMEM, ANY, ANY],
        scratch_shapes=[pltpu.VMEM((rows, width), BF16), pltpu.VMEM((rows // PARTS, width), F32)]
        + [pltpu.VMEM(block.shape, BF16) for block in held]
        + [DMA((len(held),)), DMA((count,)), DMA((count,)), DMA((count,))]
        + scatter_scratch(count, rows, width, PARTS)
        + gather_scratch(count, PARTS),
        compiler_params=comm_params(collective),
        cost_estimate=cost(80),
    )(left, right, hidden, gain, *held)


def back_kernel(
    count,
    left_from,
    right_from,
    middle_from,
    cotangent_from,
    gain,
    attended_from,
    out_weight_from,
    d_middle,
    d_gain,
    d_attended,
    d_out,
    sums,
    gathered,
    turned,
    out_sum,
    left,
    right,
    left_in,
    right_in,
    middle,
    cotangent,
    attended,
    out_weight,
    others_in,
    *scratch,
):
    me = lax.axis_index("ctx")
    group = lax.axis_index("fsdp")
    piece = middle.shape[0] // BACK_PARTS
    own = me * middle.shape[0]
    ready = load_operands(count, me, True, left_from, right_from, left, right, left_in, right_in)
    fetched = fetch(
        (middle_from, cotangent_from, attended_from, out_weight_from),
        (middle, cotangent, attended, out_weight),
        others_in,
    )
    greet([(flip(me, bit), group) for bit in bits_of(count)])
    start, finish = gather_rows(count, me, group, BACK_PARTS, None, gathered, *scratch[SCATTER:])
    d_gain[...] = jnp.zeros_like(d_gain)

    def done(part, value):
        sums[...] = value

        def step(row, place):
            span_rows = pl.ds(row, 32)
            back, gain_part = norm_back(middle[span_rows, :], gain[...], sums[pl.ds(place, 32), :])
            back = back + cotangent[span_rows, :].astype(F32)
            d_middle[span_rows, :] = back
            gathered[pl.ds(pl.multiple_of(own + row, 32), 32), :] = back.astype(BF16)
            d_gain[...] += gain_part

        row_blocks(part * piece, piece, step)
        start(part)

    begin, _, pass_on, end, close = product_scatter(
        count, me, group, BACK_PARTS, True, left, right, done, *scratch[:SCATTER], ready=ready
    )
    begin()
    fetched()
    out_sum[...] = jnp.zeros_like(out_sum)

    def turn(index, carry):
        span_rows = pl.ds(pl.multiple_of(index * 256, 256), 256)
        turned[:, span_rows] = attended[span_rows, :].astype(F32).T.astype(BF16)
        return carry

    lax.fori_loop(0, attended.shape[0] // 256, turn, 0)
    pass_on(0)
    end(0)

    def arrived(row, size):
        block = gathered[pl.ds(row, size), :]
        d_attended[pl.ds(row, size), :] = nt(block, out_weight[...]).astype(BF16)
        if size % 128 == 0:
            out_sum[...] += jnp.dot(turned[:, pl.ds(row, size)], block, preferred_element_type=F32)

    finish(arrived)
    close()
    if 2 * piece % 128:
        out_sum[...] = jnp.dot(turned[...], gathered[...], preferred_element_type=F32)
    d_out[...] = out_sum[...].astype(BF16)


def back_through_middle(count, collective, left, right, middle, cotangent, gain, attended, out_weight):
    rows, width = middle.shape
    tokens, wide = attended.shape
    shape = jax.ShapeDtypeStruct
    return pl.pallas_call(
        functools.partial(back_kernel, count),
        out_shape=[
            shape((rows, width), F32),
            shape((1, width), F32),
            shape((tokens, wide), BF16),
            shape((wide, width), BF16),
        ],
        in_specs=[ANY] * 4 + [VMEM] + [ANY] * 2,
        out_specs=[VMEM] * 4,
        scratch_shapes=[
            pltpu.VMEM((rows // BACK_PARTS, width), F32),
            pltpu.VMEM((tokens, width), BF16),
            pltpu.VMEM((wide, tokens), BF16),
            pltpu.VMEM((wide, width), F32),
        ]
        + operand_scratch(count, left, right, True)
        + [
            pltpu.VMEM((rows, width), F32),
            pltpu.VMEM((rows, width), BF16),
            pltpu.VMEM((tokens, wide), BF16),
            pltpu.VMEM((wide, width), BF16),
            DMA((4,)),
        ]
        + scatter_scratch(count, rows, width, BACK_PARTS)
        + gather_scratch(count, BACK_PARTS)[:2],
        compiler_params=comm_params(collective),
        cost_estimate=cost(85),
    )(left, right, middle, cotangent, gain, attended, out_weight)


def input_kernel(
    count,
    left_from,
    right_from,
    hidden_from,
    d_middle_from,
    gain,
    parts,
    d_hidden,
    d_gain,
    d_gate_up,
    columns,
    left,
    right,
    left_in,
    right_in,
    hidden,
    d_middle,
    others_in,
    sums,
    send,
    recv,
    *scratch,
):
    me = lax.axis_index("ctx")
    group = lax.axis_index("fsdp")
    half = hidden.shape[0] // 2
    ready = load_operands(count, me, True, left_from, right_from, left, right, left_in, right_in)
    fetched = fetch((hidden_from, d_middle_from), (hidden, d_middle), others_in)
    greet(everyone(count, me, group))
    start, finish = trade(count, me, group, incoming, parts, columns, send, recv)
    early = [0, 1, 2, 4]
    start(early)
    d_gain[...] = jnp.zeros_like(d_gain)

    def done(part, value):
        sums[...] = value

        def step(row, place):
            span_rows = pl.ds(row, 32)
            values = hidden[span_rows, :].astype(F32)
            back, gain_part = norm_back(values, gain[...], sums[pl.ds(place, 32), :])
            d_hidden[span_rows, :] = d_middle[span_rows, :] + back
            d_gain[...] += gain_part

        row_blocks(part * half, half, step)

    begin, _, pass_on, end, close = product_scatter(
        count, me, group, 2, True, left, right, done, *scratch, ready=ready
    )
    begin()
    fetched()
    pass_on(0)
    start([slot for slot in range(count) if slot not in early])
    end(0)
    finish(place_columns(count, mlp_spans, columns, d_gate_up))
    close()


def back_to_input(count, collective, left, right, hidden, d_middle, gain, parts):
    rows, width = hidden.shape
    shape = jax.ShapeDtypeStruct
    return pl.pallas_call(
        functools.partial(input_kernel, count),
        out_shape=[
            shape((rows, width), F32),
            shape((1, width), F32),
            shape((parts.shape[1], 2 * FF), F32),
        ],
        in_specs=[ANY] * 4 + [VMEM, ANY],
        out_specs=[VMEM] * 3,
        scratch_shapes=[pltpu.VMEM(parts.shape, BF16)]
        + operand_scratch(count, left, right, True)
        + [
            pltpu.VMEM((rows, width), BF16),
            pltpu.VMEM((rows, width), F32),
            DMA((2,)),
            pltpu.VMEM((rows // 2, width), F32),
            DMA((count,)),
            DMA((count,)),
        ]
        + scatter_scratch(count, rows, width),
        compiler_params=comm_params(collective),
        cost_estimate=cost(60),
    )(left, right, hidden, d_middle, gain, parts)


def mlp_kernel(
    count,
    groups,
    activated_from,
    weight_from,
    middle_from,
    upstream,
    both,
    second,
    output,
    d_both,
    parts,
    up_slots,
    both_slots,
    second_slots,
    part_slots,
    up_in,
    both_in,
    second_in,
    parts_out,
    activated,
    weight,
    activated_in,
    weight_in,
    middle,
    others_in,
    *scratch,
):
    me = lax.axis_index("ctx")
    group = lax.axis_index("fsdp")
    half = middle.shape[0] // 2
    tokens, own = activated.shape
    block = up_slots.shape[1]
    columns = second_slots.shape[2]
    ready = load_operands(
        count, me, False, activated_from, weight_from, activated, weight, activated_in, weight_in
    )
    fetched = fetch((middle_from,), (middle,), others_in)
    greet([(flip(me, bit), group) for bit in bits_of(count)])

    def rows_in(index):
        slot = lax.rem(index, 4)
        rows = pl.ds(pl.multiple_of(index * block, block), block)
        return (
            pltpu.make_async_copy(upstream.at[rows], up_slots.at[slot], up_in.at[slot]),
            pltpu.make_async_copy(both.at[rows], both_slots.at[slot], both_in.at[slot]),
        )

    def second_copy(index):
        slot = lax.rem(index, 2)
        span_columns = pl.ds(pl.multiple_of(index * columns, columns), columns)
        return pltpu.make_async_copy(second.at[:, span_columns], second_slots.at[slot], second_in.at[slot])

    def part_copies(index):
        slot = lax.rem(index, 2)
        rows = columns // groups
        return [
            pltpu.make_async_copy(
                part_slots.at[slot, pl.ds(owner * rows, rows)],
                parts.at[owner, index],
                parts_out.at[slot, owner],
            )
            for owner in range(groups)
        ]

    for item in rows_in(0) + rows_in(1):
        item.start()
    second_copy(0).start()

    def done(part, value):
        span_rows = pl.ds(part * half, half)
        output[span_rows, :] = (middle[span_rows, :] + value).astype(BF16)

    begin, _, pass_on, end, close = product_scatter(
        count, me, group, 2, False, activated, weight, done, *scratch, ready=ready
    )
    begin()
    fetched()
    steps = tokens // block

    def activation(index, carry):
        @pl.when(2 * index + 2 < steps)
        def _():
            for item in rows_in(2 * index + 2) + rows_in(2 * index + 3):
                item.start()

        for item in rows_in(2 * index) + rows_in(2 * index + 1):
            item.wait()
        slots = [lax.rem(2 * index + turn, 4) for turn in (0, 1)]
        grads = [nt(up_slots[slot], weight[...]).astype(BF16).astype(F32) for slot in slots]
        for turn, (slot, grad) in enumerate(zip(slots, grads)):
            rows = pl.ds(pl.multiple_of((2 * index + turn) * block, block), block)
            gate = both_slots[slot, :, :own]
            up = both_slots[slot, :, own:]
            sigmoid = 1.0 / (1.0 + jnp.exp(-gate))
            d_both[rows, :own] = (grad * up * sigmoid * (1.0 + gate * (1.0 - sigmoid))).astype(BF16)
            d_both[rows, own:] = (grad * gate * sigmoid).astype(BF16)
        return carry

    lax.fori_loop(0, steps // 2, activation, 0)

    def weight_grad(index, carry):
        @pl.when(index + 1 < count)
        def _():
            second_copy(index + 1).start()

        second_copy(index).wait()

        @pl.when(index >= 2)
        def _():
            for item in part_copies(index - 2):
                item.wait()

        slot = lax.rem(index, 2)
        value = lax.dot_general(
            second_slots[slot], d_both[...], (((0,), (0,)), ((), ())), preferred_element_type=F32
        )
        part_slots[slot] = value.astype(BF16)
        for item in part_copies(index):
            item.start()
        return carry

    lax.fori_loop(0, count // 2, weight_grad, 0)
    pass_on(0)
    lax.fori_loop(count // 2, count, weight_grad, 0)
    for index in (count - 2, count - 1):
        for item in part_copies(index):
            item.wait()
    end(0)
    close()


def back_through_mlp(count, groups, collective, activated, weight, middle, upstream, both, second):
    rows, width = middle.shape
    tokens, own = activated.shape
    block = 256
    columns = width // count
    shape = jax.ShapeDtypeStruct
    return pl.pallas_call(
        functools.partial(mlp_kernel, count, groups),
        out_shape=[
            shape((rows, width), BF16),
            shape((tokens, 2 * own), BF16),
            shape((groups, count, columns // groups, 2 * own), BF16),
        ],
        in_specs=[ANY] * 6,
        out_specs=[VMEM, VMEM, ANY],
        scratch_shapes=[
            pltpu.VMEM((4, block, width), BF16),
            pltpu.VMEM((4, block, 2 * own), F32),
            pltpu.VMEM((2, tokens, columns), BF16),
            pltpu.VMEM((2, columns, 2 * own), BF16),
            DMA((4,)),
            DMA((4,)),
            DMA((2,)),
            DMA((2, groups)),
        ]
        + operand_scratch(count, activated, weight, False)
        + [pltpu.VMEM((rows, width), F32), DMA((1,))]
        + scatter_scratch(count, rows, width),
        compiler_params=comm_params(collective),
        cost_estimate=cost(48),
    )(activated, weight, middle, upstream, both, second)


def swap_halves(value):
    return jnp.concatenate([value[:, HEAD // 2 :], value[:, : HEAD // 2]], axis=1)


def nt(left, right):
    return lax.dot_general(left, right, (((1,), (1,)), ((), ())), preferred_element_type=F32)


def causal(keys, queries):
    key = lax.broadcasted_iota(jnp.int32, (keys, queries), 0)
    query = lax.rem(lax.broadcasted_iota(jnp.int32, (keys, queries), 1), CONT)
    return key <= query


def attention_kernel(
    heads, runs, joined, cosine, sine, q_gain, k_gain, attended, raw, queries, keys, values, mixed, lse, turned, placed
):
    tokens = joined.shape[0]
    blocks = tokens // CONT
    wide = heads * CONT

    def sort(run, carry):
        origin = pl.multiple_of(run * RUN, RUN)
        place = pl.multiple_of(runs[run] * RUN, RUN)
        raw[pl.ds(place, RUN), :] = joined[pl.ds(origin, RUN), :]
        return carry

    lax.fori_loop(0, tokens // RUN, sort, 0)

    def prepare(block, carry):
        span_rows = pl.ds(pl.multiple_of(block * CONT, CONT), CONT)
        cos_rows = cosine[span_rows, :]
        sin_rows = sine[span_rows, :]

        def turn(value, gain):
            value = value * lax.rsqrt(jnp.mean(value * value, axis=-1, keepdims=True) + EPS) * gain
            return (value * cos_rows + swap_halves(value) * sin_rows).astype(BF16)

        for head in range(heads):
            piece = raw[span_rows, head * HEAD : (head + 1) * HEAD]
            queries[block, head * CONT : (head + 1) * CONT, :] = turn(piece, q_gain[...])
        keys[span_rows, :] = turn(raw[span_rows, wide : wide + HEAD], k_gain[...])
        piece = raw[span_rows, wide + HEAD : wide + 2 * HEAD]
        values[span_rows, :] = piece.astype(BF16)
        turned[:, span_rows] = piece.T.astype(BF16)
        return carry

    lax.fori_loop(0, blocks, prepare, 0)

    def attend(block, own, before):
        query = queries[block]
        own_rows = pl.ds(own, CONT)
        weight = jnp.exp2(nt(keys[own_rows, :], query) * SCALE2)
        weight = jnp.where(causal(CONT, wide), weight, 0.0)
        sums = jnp.sum(weight, axis=0, keepdims=True)
        out = jnp.dot(turned[:, own_rows], weight.astype(BF16), preferred_element_type=F32)
        if before:
            weight = jnp.exp2(nt(keys[:before, :], query) * SCALE2)
            sums = sums + jnp.sum(weight, axis=0, keepdims=True)
            out = out + jnp.dot(turned[:, :before], weight.astype(BF16), preferred_element_type=F32)
        out = out / sums
        mixed[block] = out
        lse[block] = jnp.broadcast_to(jnp.log2(sums), (8, wide))
        for head in range(heads):
            placed[own_rows, head * HEAD : (head + 1) * HEAD] = out[
                :, head * CONT : (head + 1) * CONT
            ].T.astype(BF16)

    for block in range(PROMPT // CONT):
        attend(block, block * CONT, block * CONT)

    def continuation(block, carry):
        attend(block, pl.multiple_of(block * CONT, CONT), PROMPT)
        return carry

    lax.fori_loop(PROMPT // CONT, blocks, continuation, 0)

    def unsort(run, carry):
        origin = pl.multiple_of(run * RUN, RUN)
        place = pl.multiple_of(runs[run] * RUN, RUN)
        attended[pl.ds(origin, RUN), :] = placed[pl.ds(place, RUN), :]
        return carry

    lax.fori_loop(0, tokens // RUN, unsort, 0)


def attention(heads, runs, joined, cosine, sine, q_gain, k_gain):
    tokens = joined.shape[0]
    blocks = tokens // CONT
    wide = heads * CONT
    shape = jax.ShapeDtypeStruct
    return pl.pallas_call(
        functools.partial(attention_kernel, heads),
        out_shape=[
            shape((tokens, wide), BF16),
            shape(joined.shape, F32),
            shape((blocks, wide, HEAD), BF16),
            shape((tokens, HEAD), BF16),
            shape((tokens, HEAD), BF16),
            shape((blocks, HEAD, wide), F32),
            shape((blocks, 8, wide), F32),
        ],
        in_specs=[SMEM, VMEM, VMEM, VMEM, VMEM, VMEM],
        out_specs=[VMEM] * 7,
        scratch_shapes=[pltpu.VMEM((HEAD, tokens), BF16), pltpu.VMEM((tokens, wide), BF16)],
        compiler_params=pltpu.CompilerParams(vmem_limit_bytes=VMEM_LIMIT),
        cost_estimate=cost(15),
    )(runs, joined, cosine, sine, q_gain, k_gain)


def attention_back_kernel(
    heads,
    runs,
    d_attended,
    queries,
    keys,
    values,
    mixed,
    lse,
    d_queries,
    d_keys,
    d_values,
    arrived,
    keys_turned,
    ready=None,
):
    tokens = keys.shape[0]
    blocks = tokens // CONT
    wide = heads * CONT

    def sort(run, carry):
        origin = pl.multiple_of(run * RUN, RUN)
        place = pl.multiple_of(runs[run] * RUN, RUN)
        arrived[pl.ds(place, RUN), :] = d_attended[pl.ds(origin, RUN), :]
        return carry

    lax.fori_loop(0, tokens // RUN, sort, 0)
    d_keys[...] = jnp.zeros_like(d_keys)
    d_values[...] = jnp.zeros_like(d_values)

    def turn(block, carry):
        span_rows = pl.ds(pl.multiple_of(block * CONT, CONT), CONT)
        keys_turned[:, span_rows] = keys[span_rows, :].astype(F32).T.astype(BF16)
        return carry

    lax.fori_loop(0, blocks, turn, 0)

    if ready:
        ready()

    def back(block, own, before):
        query = queries[block]
        own_rows = pl.ds(own, CONT)
        grad = jnp.concatenate(
            [arrived[own_rows, head * HEAD : (head + 1) * HEAD] for head in range(heads)], axis=0
        )
        grad_turned = grad.astype(F32).T
        delta = jnp.sum(grad_turned * mixed[block], axis=0, keepdims=True)
        total_row = lse[block][:1, :]

        def part(rows, count, masked):
            prob = jnp.exp2(nt(keys[rows, :], query) * SCALE2 - total_row)
            if masked:
                prob = jnp.where(causal(count, wide), prob, 0.0)
            score = (prob * (nt(values[rows, :], grad) - delta)).astype(BF16)
            d_values[rows, :] += jnp.dot(prob.astype(BF16), grad, preferred_element_type=F32)
            d_keys[rows, :] += jnp.dot(score, query, preferred_element_type=F32)
            return jnp.dot(keys_turned[:, rows], score, preferred_element_type=F32)

        result = part(own_rows, CONT, True)
        if before:
            result = result + part(slice(0, before), before, False)
        result = result * SCALE
        for head in range(heads):
            d_queries[own_rows, head * HEAD : (head + 1) * HEAD] = result[
                :, head * CONT : (head + 1) * CONT
            ].T.astype(BF16)

    for block in range(PROMPT // CONT):
        back(block, block * CONT, block * CONT)

    def continuation(block, carry):
        back(block, pl.multiple_of(block * CONT, CONT), PROMPT)
        return carry

    lax.fori_loop(PROMPT // CONT, blocks, continuation, 0)


def attention_back(heads, runs, d_attended, queries, keys, values, mixed, lse):
    tokens = keys.shape[0]
    wide = heads * CONT
    shape = jax.ShapeDtypeStruct
    return pl.pallas_call(
        functools.partial(attention_back_kernel, heads),
        out_shape=[shape((tokens, wide), BF16), shape((tokens, HEAD), F32), shape((tokens, HEAD), F32)],
        in_specs=[SMEM] + [VMEM] * 6,
        out_specs=[VMEM] * 3,
        scratch_shapes=[pltpu.VMEM((tokens, wide), BF16), pltpu.VMEM((HEAD, tokens), BF16)],
        compiler_params=pltpu.CompilerParams(vmem_limit_bytes=VMEM_LIMIT),
        cost_estimate=cost(25),
    )(runs, d_attended, queries, keys, values, mixed, lse)


def joined_back_kernel(
    heads, runs, raw, d_queries, d_keys, d_values, cosine, sine, q_gain, k_gain, share, d_joined, d_q_gain, d_k_gain, placed
):
    tokens = raw.shape[0]
    blocks = tokens // CONT
    wide = heads * CONT
    d_q_gain[...] = jnp.zeros_like(d_q_gain)
    d_k_gain[...] = jnp.zeros_like(d_k_gain)

    def step(block, carry):
        span_rows = pl.ds(pl.multiple_of(block * CONT, CONT), CONT)
        cos_rows = cosine[span_rows, :]
        sin_rows = sine[span_rows, :]

        def pull(value, grad, gain):
            grad = grad * cos_rows - swap_halves(grad) * sin_rows
            scale = lax.rsqrt(jnp.mean(value * value, axis=-1, keepdims=True) + EPS)
            scaled = value * scale
            gain_grad = jnp.sum(grad * scaled, axis=0, keepdims=True)
            grad = grad * gain
            return scale * (grad - scaled * jnp.mean(grad * scaled, axis=-1, keepdims=True)), gain_grad

        for head in range(heads):
            columns = slice(head * HEAD, (head + 1) * HEAD)
            grad, gain_grad = pull(
                raw[span_rows, columns], d_queries[span_rows, columns].astype(F32), q_gain[...]
            )
            placed[span_rows, columns] = grad.astype(BF16)
            d_q_gain[...] += gain_grad
        key_part, value_part = (1.0, 1.0) if share is None else (share[:1, :], share[1:, :])
        grad, gain_grad = pull(
            raw[span_rows, wide : wide + HEAD],
            (d_keys[span_rows, :] * SCALE).astype(BF16).astype(F32),
            k_gain[...],
        )
        placed[span_rows, wide : wide + HEAD] = (grad * key_part).astype(BF16)
        d_k_gain[...] += gain_grad * key_part
        placed[span_rows, wide + HEAD : wide + 2 * HEAD] = (d_values[span_rows, :] * value_part).astype(BF16)
        return carry

    lax.fori_loop(0, blocks, step, 0)

    def unsort(run, carry):
        origin = pl.multiple_of(run * RUN, RUN)
        place = pl.multiple_of(runs[run] * RUN, RUN)
        d_joined[pl.ds(origin, RUN), :] = placed[pl.ds(place, RUN), :]
        return carry

    lax.fori_loop(0, tokens // RUN, unsort, 0)


def attention_and_joined_back_kernel(
    heads,
    count,
    groups,
    runs,
    d_attended,
    queries,
    keys,
    values,
    mixed_from,
    lse,
    raw,
    cosine,
    sine,
    q_gain,
    k_gain,
    normed,
    d_out_from,
    d_joined_to,
    d_q_gain,
    d_k_gain,
    parts_to,
    d_queries,
    d_keys,
    d_values,
    arrived,
    keys_turned,
    raw_here,
    cosine_here,
    sine_here,
    placed,
    normed_slots,
    mixed,
    d_out,
    d_joined,
    parts,
    loaded,
    normed_in,
    joined_out,
    parts_out,
):
    columns = normed_slots.shape[2]

    def normed_copy(index):
        slot = lax.rem(index, 2)
        span_columns = pl.ds(pl.multiple_of(index * columns, columns), columns)
        return pltpu.make_async_copy(normed.at[:, span_columns], normed_slots.at[slot], normed_in.at[slot])

    loads = [
        pltpu.make_async_copy(source, target, loaded.at[index])
        for index, (source, target) in enumerate(
            [
                (raw, raw_here),
                (cosine, cosine_here),
                (sine, sine_here),
                (mixed_from, mixed),
                (d_out_from, d_out),
            ]
        )
    ]
    ready = loads[3].wait
    for item in [loads[3]] + loads[:3] + loads[4:]:
        item.start()
    normed_copy(0).start()
    attention_back_kernel(
        heads,
        runs,
        d_attended,
        queries,
        keys,
        values,
        mixed,
        lse,
        d_queries,
        d_keys,
        d_values,
        arrived,
        keys_turned,
        ready,
    )
    for item in loads[:3] + loads[4:]:
        item.wait()
    joined_back_kernel(
        heads,
        runs,
        raw_here,
        d_queries,
        d_keys,
        d_values,
        cosine_here,
        sine_here,
        q_gain,
        k_gain,
        None,
        d_joined,
        d_q_gain,
        d_k_gain,
        placed,
    )
    rows = columns // groups
    width = d_joined.shape[1]
    joined_copy = pltpu.make_async_copy(d_joined, d_joined_to, joined_out.at[0])
    joined_copy.start()

    def part_copies(index):
        return [
            pltpu.make_async_copy(
                parts.at[owner, index], parts_to.at[owner, index], parts_out.at[owner, index]
            )
            for owner in range(groups)
        ]

    extras = range(d_out.shape[1] // width)
    for extra in extras:
        for owner in range(groups):
            parts[owner, count + extra] = d_out[
                owner * rows : (owner + 1) * rows, extra * width : (extra + 1) * width
            ]
        for item in part_copies(count + extra):
            item.start()

    def weight_grad(index, carry):
        @pl.when(index + 1 < count)
        def _():
            normed_copy(index + 1).start()

        normed_copy(index).wait()
        value = lax.dot_general(
            normed_slots[lax.rem(index, 2)], d_joined[...], (((0,), (0,)), ((), ())), preferred_element_type=F32
        ).astype(BF16)
        for owner in range(groups):
            parts[owner, index] = value[owner * rows : (owner + 1) * rows]
        for item in part_copies(index):
            item.start()
        return carry

    lax.fori_loop(0, count, weight_grad, 0)
    for index in range(count + len(extras)):
        for item in part_copies(index):
            item.wait()
    joined_copy.wait()


def attention_and_joined_back(
    heads,
    count,
    groups,
    runs,
    d_attended,
    queries,
    keys,
    values,
    mixed,
    lse,
    raw,
    cosine,
    sine,
    q_gain,
    k_gain,
    normed,
    d_out,
):
    tokens = keys.shape[0]
    columns = normed.shape[1] // count
    blocks = count + d_out.shape[1] // raw.shape[1]
    wide = heads * CONT
    shape = jax.ShapeDtypeStruct
    return pl.pallas_call(
        functools.partial(attention_and_joined_back_kernel, heads, count, groups),
        out_shape=[
            shape(raw.shape, BF16),
            shape((1, HEAD), F32),
            shape((1, HEAD), F32),
            shape((groups, blocks, columns // groups, raw.shape[1]), BF16),
        ],
        in_specs=[SMEM] + [VMEM] * 4 + [ANY, VMEM] + [ANY] * 3 + [VMEM] * 2 + [ANY] * 2,
        out_specs=[ANY, VMEM, VMEM, ANY],
        scratch_shapes=[
            pltpu.VMEM((tokens, wide), BF16),
            pltpu.VMEM((tokens, HEAD), F32),
            pltpu.VMEM((tokens, HEAD), F32),
            pltpu.VMEM((tokens, wide), BF16),
            pltpu.VMEM((HEAD, tokens), BF16),
            pltpu.VMEM(raw.shape, F32),
            pltpu.VMEM(cosine.shape, F32),
            pltpu.VMEM(sine.shape, F32),
            pltpu.VMEM(raw.shape, BF16),
            pltpu.VMEM((2, tokens, columns), BF16),
            pltpu.VMEM(mixed.shape, F32),
            pltpu.VMEM(d_out.shape, BF16),
            pltpu.VMEM(raw.shape, BF16),
            pltpu.VMEM((groups, blocks, columns // groups, raw.shape[1]), BF16),
            DMA((5,)),
            DMA((2,)),
            DMA((1,)),
            DMA((groups, blocks)),
        ],
        compiler_params=pltpu.CompilerParams(vmem_limit_bytes=VMEM_LIMIT),
        cost_estimate=cost(30),
    )(runs, d_attended, queries, keys, values, mixed, lse, raw, cosine, sine, q_gain, k_gain, normed, d_out)


def joined_back(heads, runs, raw, d_queries, d_keys, d_values, cosine, sine, q_gain, k_gain, share):
    shape = jax.ShapeDtypeStruct
    return pl.pallas_call(
        functools.partial(joined_back_kernel, heads),
        out_shape=[shape(raw.shape, BF16), shape((1, HEAD), F32), shape((1, HEAD), F32)],
        in_specs=[SMEM] + [VMEM] * 9,
        out_specs=[VMEM] * 3,
        scratch_shapes=[pltpu.VMEM(raw.shape, BF16)],
        compiler_params=pltpu.CompilerParams(vmem_limit_bytes=VMEM_LIMIT),
        cost_estimate=cost(8),
    )(runs, raw, d_queries, d_keys, d_values, cosine, sine, q_gain, k_gain, share)


def rotary(tokens):
    index = np.arange(tokens)
    place = np.where(index < PROMPT, index, PROMPT + (index - PROMPT) % CONT).astype(np.float32)
    exponent = np.arange(HEAD // 2, dtype=np.float32) * np.float32(2.0 / HEAD)
    inverse = np.power(np.float32(ROPE_BASE), -exponent).astype(np.float32)
    angles = place[:, None] * inverse[None, :]
    cosine, sine = np.cos(angles), np.sin(angles)
    tables = np.concatenate([cosine, cosine], axis=1), np.concatenate([-sine, sine], axis=1)
    return tuple(jnp.asarray(table, F32) for table in tables)


def body(
    count,
    groups,
    hidden_in,
    segment_ids,
    positions,
    attn_gain,
    qkv_weight,
    query_norm_gain,
    k_gain,
    out_weight,
    mlp_gain,
    gate_up,
    down_weight,
    cotangent,
):
    hidden = hidden_in[0].astype(F32)
    rows, width = hidden.shape
    tokens = rows * count
    heads = QUERY_HEADS // count
    repeat = sharing(count)

    first = segment_ids[0, ::RUN]
    place = positions[0, ::RUN]
    order = jnp.where(first == 0, place, place + (first - 1) * CONT) // RUN
    runs = jnp.zeros((1, 8, 128), jnp.int32).at[0, 0, : rows // RUN].set(order)

    def gather_groups(values, axis):
        return lax.all_gather(values, "fsdp", axis=axis, tiled=True)

    def scatter_groups(values):
        return lax.psum_scatter(values, "fsdp", scatter_dimension=0, tiled=True)

    qkv_parts = spread_qkv(count, 1, qkv_weight, out_weight)
    gate_up, qkv_parts = lax.optimization_barrier((gate_up, qkv_parts))
    w_qkv = gather_groups(qkv_parts, 1)
    if merges(count, width):
        w_out = w_qkv[count:].transpose(1, 0, 2).reshape(-1, width)
        w_qkv = w_qkv[:count]
    else:
        w_out = gather_groups(out_weight, 0)
    w_qkv = w_qkv.reshape(width, -1)
    mlp_parts = spread_mlp(count, 5, gate_up)
    normed_local = norm_rows(hidden, attn_gain).astype(BF16)
    normed_local, mlp_parts = lax.optimization_barrier((normed_local, mlp_parts))
    normed, all_runs = opening(count, 2, normed_local, runs)
    w_qkv, normed, upstream = lax.optimization_barrier((w_qkv, normed, cotangent[0]))
    w_gu = gather_groups(mlp_parts, 1).reshape(width, -1)
    w_down = gather_groups(down_weight, 0)
    run_order = all_runs[:, 0, : rows // RUN].reshape(-1)
    cosine, sine = rotary(tokens)
    q_gain_row = query_norm_gain[None, :]
    k_gain_row = k_gain[None, :]

    blocks, masks = [upstream[None, : rows // 2], upstream[None, rows // 2 :]], [[0], [0]]
    chip_steps = len(bits_of(count)) - 1
    for step in range(chip_steps - 1):
        arrived, filled = gather_step(count, masks, blocks, step)
        if step == 0:
            joined = jnp.dot(normed, w_qkv, preferred_element_type=F32)
            joined, arrived = lax.optimization_barrier((joined, arrived))
        blocks = [jnp.concatenate(pair) for pair in zip(blocks, arrived)]
        masks = [held + more for held, more in zip(masks, filled)]
    arrived, filled = gather_step(count, masks, blocks, chip_steps - 1)
    attended, raw, queries, keys, values, mixed, lse = attention(
        heads, run_order, joined, cosine, sine, q_gain_row, k_gain_row
    )
    attended, arrived = lax.optimization_barrier((attended, arrived))
    middle, second, upstream = middle_and_second(
        count, 3, attended, w_out, hidden_in[0], mlp_gain[None, :], masks, blocks, filled, arrived
    )
    both = jnp.dot(second, w_gu, preferred_element_type=F32)
    own = both.shape[1] // 2
    gate, up = both[:, :own], both[:, own:]
    activated = (gate * jax.nn.sigmoid(gate) * up).astype(BF16)

    d_down = jnp.dot(activated.T, upstream, preferred_element_type=F32).astype(BF16)
    d_down, upstream = lax.optimization_barrier((d_down, upstream))
    d_down = scatter_groups(d_down)
    output, d_both, gu_parts = back_through_mlp(
        count, groups, 9, activated, w_down, middle, upstream, both, second
    )
    gu_parts, d_both = lax.optimization_barrier((gu_parts, d_both))
    gu_parts = scatter_groups(gu_parts.reshape((groups * count,) + gu_parts.shape[2:]))

    def weight_grad(left, right):
        grad = lax.dot_general(left, right, (((0,), (0,)), ((), ())), preferred_element_type=F32)
        grad = grad.astype(BF16).reshape(count, groups, -1, right.shape[1])
        return grad.transpose(1, 0, 2, 3).reshape(groups * count, -1, right.shape[1])

    d_middle, mlp_gain_grad, d_attended, d_out = back_through_middle(
        count, 6, d_both, w_gu, middle, cotangent[0], mlp_gain[None, :], attended, w_out
    )
    d_attended, d_down = lax.optimization_barrier((d_attended, d_down))
    tables = (cosine, sine, q_gain_row, k_gain_row)
    if repeat == 1:
        d_joined, q_gain_grad, k_gain_grad, parts = attention_and_joined_back(
            heads,
            count,
            groups,
            run_order,
            d_attended,
            queries,
            keys,
            values,
            mixed,
            lse,
            raw,
            *tables,
            normed,
            d_out,
        )
        parts, gu_parts, d_joined = lax.optimization_barrier((parts, gu_parts, d_joined))
        qkv_grad_parts = scatter_groups(parts.reshape((-1,) + parts.shape[2:]))
    else:
        d_queries, d_keys, d_values = attention_back(
            heads, run_order, d_attended, queries, keys, values, mixed, lse
        )
        d_keys = d_keys + across(count, 1, d_keys)
        d_values = d_values + across(count, 1, d_values)
        mine = lax.rem(lax.axis_index("ctx"), 2) == jnp.arange(2)
        share = jnp.broadcast_to(mine[:, None].astype(F32), (2, HEAD))
        d_joined, q_gain_grad, k_gain_grad = joined_back(
            heads, run_order, raw, d_queries, d_keys, d_values, *tables, share
        )
        d_out = scatter_groups(d_out)
        qkv_grad_parts = scatter_groups(weight_grad(normed, d_joined))
    d_hidden, attn_gain_grad, d_gate_up = back_to_input(
        count, 8, d_joined, w_qkv, hidden_in[0], d_middle, attn_gain[None, :], gu_parts
    )
    d_hidden, qkv_grad_parts = lax.optimization_barrier((d_hidden, qkv_grad_parts))

    gains = (attn_gain_grad, mlp_gain_grad, q_gain_grad, k_gain_grad)
    if repeat > 1:
        extra = jnp.zeros((1,) + qkv_grad_parts.shape[1:], BF16)
        qkv_grad_parts = jnp.concatenate([qkv_grad_parts, extra])
    *gains, d_qkv, out_rows = last(count, groups, 11, gains, qkv_grad_parts, qkv_weight.shape[1])
    if repeat == 1:
        d_out = out_rows
    return (
        output[None],
        d_hidden[None],
        gains[0].reshape(-1),
        d_qkv,
        gains[2].reshape(-1),
        gains[3].reshape(-1),
        d_out.astype(F32),
        gains[1].reshape(-1),
        d_gate_up,
        d_down.astype(F32),
    )


def solution(mesh):
    return jax.shard_map(
        functools.partial(body, mesh.shape["ctx"], mesh.shape["fsdp"]),
        mesh=mesh,
        in_specs=(
            P("fsdp", "ctx", None),
            P("fsdp", "ctx"),
            P("fsdp", "ctx"),
            P(),
            P(("ctx", "fsdp"), None),
            P(),
            P(),
            P(("ctx", "fsdp"), None),
            P(),
            P(("ctx", "fsdp"), None),
            P(("ctx", "fsdp"), None),
            P("fsdp", "ctx", None),
        ),
        out_specs=(
            P("fsdp", "ctx", None),
            P("fsdp", "ctx", None),
            P(),
            P(("ctx", "fsdp"), None),
            P(),
            P(),
            P(("ctx", "fsdp"), None),
            P(),
            P(("ctx", "fsdp"), None),
            P(("ctx", "fsdp"), None),
        ),
        check_vma=False,
    )
```
